256 devices in a mesh: rep: 16 (over x, z_lo), filt: 16 (over z_hi, y, core).
Axes of the slice: x: 4, y: 4, z: 8 (z_hi: 2, z_lo: 4; z = z_hi * 4 + z_lo), core: 2. Of those that a mesh axis runs over, the one named last changes fastest.
Arguments:
- images: bfloat16 [2016, 16, 224], P('filt', 'rep'), may hold values from -6 to 6
- labels: int32 [16], P('rep'), may hold values from 0 to 999
- partner: int32 [16], replicated, may hold values from 0 to 15, as said below
- student_w3: bfloat16 [16, 2016, 9, 1008], P('rep', 'filt'), may hold values from -0.0625 to 0.0625
- student_w1: bfloat16 [16, 2016, 2016], P('rep', 'filt'), may hold values from -0.125 to 0.125
- student_head: bfloat16 [16, 2016, 1000], P('rep', 'filt')
- stale_w3: bfloat16 [16, 2016, 9, 1008], P('rep', 'filt'), may hold values from -0.0625 to 0.0625
- stale_w1: bfloat16 [16, 2016, 2016], P('rep', 'filt'), may hold values from -0.125 to 0.125
- stale_head: bfloat16 [16, 2016, 1000], P('rep', 'filt')
Outputs:
- grad_w3: float32 [16, 2016, 9, 1008], P('rep', 'filt')
- grad_w1: float32 [16, 2016, 2016], P('rep', 'filt')
- grad_head: float32 [16, 2016, 1000], P('rep', 'filt')
The draws below stay inside these ranges and needn't reach their ends.
Inputs may be any that keep to these rules, and one draw needn't show every extreme that they name: Replicas are paired both ways: partner[partner[r]] = r, no replica is its own partner, and partner[r] = r XOR partner[0] for every r.
All inputs are finite; a program needn't handle non-finite values.
Results may differ from the reference program's by a relative error of at most 0.0083.
Values may be sent and summed in bfloat16 or wider, within the bound.
A program may use at most 128 MiB of HBM per device.

```python
import math
import jax
import jax.numpy as jnp
from jax import lax

C = 2016
GW = 1008
K = 1000
IMG_DEV = 1
ROWS = 4
MAP_W = 56
IMGS = 16
N_REP = 16


def draw_partner(key, part):
    key = jax.random.fold_in(key, 41)
    flipper = jax.random.randint(key, (), 1, N_REP, dtype=jnp.int32)
    return jnp.bitwise_xor(jnp.arange(N_REP, dtype=jnp.int32), flipper)


def draw_student_head(key, part):
    key = jax.random.fold_in(key, 11)
    base_key = jax.random.fold_in(key, 0)
    values = jnp.clip(jax.random.normal(base_key, (N_REP, C, K), jnp.float32), -6.0, 6.0) * (8.0 / math.sqrt(C))
    return values.astype(jnp.bfloat16)


def draw_stale_head(key, part):
    key = jax.random.fold_in(key, 12)
    base_key = jax.random.fold_in(key, 0)
    values = jnp.clip(jax.random.normal(base_key, (N_REP, C, K), jnp.float32), -6.0, 6.0) * (8.0 / math.sqrt(C))
    return values.astype(jnp.bfloat16)


def place_ends(entries, rng, smallest, high):
    index_at = [jax.random.randint(jax.random.fold_in(rng, axis), (), 0, length) for axis, length in enumerate(entries.shape)]
    main_axis = entries.shape.index(max(entries.shape))
    neighbour = index_at[:main_axis] + [(index_at[main_axis] + 1) % entries.shape[main_axis]] + index_at[main_axis + 1:]
    return entries.at[tuple(index_at)].set(smallest).at[tuple(neighbour)].set(high)


def block_levels(rng, extent, shards, smallest, top_value):
    loudness, own = 1.0, jax.random.fold_in(rng, 6)
    for dim, shards_of in shards:
        steps = jnp.exp(jax.random.uniform(jax.random.fold_in(own, dim), (shards_of,), jnp.float32, smallest / len(shards), top_value / len(shards)))
        loudness = loudness * jnp.repeat(steps, extent[dim] // shards_of).reshape([-1 if axis == dim else 1 for axis in range(len(extent))])
    return loudness


def centred(key, dims, scale, bound, cuts=(), kind=jnp.bfloat16):
    factor_of = block_levels(key, dims, cuts, -0.22, 0.18) if cuts else 1.0
    result = jax.random.normal(key, dims, jnp.float32) * scale * factor_of
    return jnp.minimum(jnp.maximum(result, -bound), bound).astype(kind)


def setup_inputs(seed: int = 0) -> dict:
    keys = jax.random.split(jax.random.key(seed), 10)
    images = centred(keys[0], (C, IMGS, ROWS * MAP_W), 1.0, 6.0, ((0, 16), (1, 16)))
    labels = place_ends(jax.random.randint(keys[1], (IMGS,), 0, K), jax.random.fold_in(keys[1], 1), 0, K - 1).astype(jnp.int32)
    partner = draw_partner(jax.random.fold_in(keys[9], 71), 0)
    student_w3 = centred(keys[3], (N_REP, C, 9, GW), (9 * GW) ** -0.5, 0.0625, ((0, 16), (1, 16)))
    student_w1 = centred(keys[4], (N_REP, C, C), C ** -0.5, 0.125, ((0, 16), (1, 16)))
    student_head = draw_student_head(jax.random.fold_in(keys[9], 71), 0)
    stale_w3 = centred(keys[6], (N_REP, C, 9, GW), (9 * GW) ** -0.5, 0.0625, ((0, 16), (1, 16)))
    stale_w1 = centred(keys[7], (N_REP, C, C), C ** -0.5, 0.125, ((0, 16), (1, 16)))
    stale_head = draw_stale_head(jax.random.fold_in(keys[9], 71), 0)
    return {"images": images, "labels": labels, "partner": partner, "student_w3": student_w3, "student_w1": student_w1, "student_head": student_head, "stale_w3": stale_w3, "stale_w1": stale_w1, "stale_head": stale_head}


def dsilu(values):
    sig = jax.nn.sigmoid(values)
    return sig * (1.0 + values * (1.0 - sig))


def tap_stack(panel):
    chans, count = panel.shape[0], panel.shape[1]
    grid = panel.reshape(chans, count, ROWS, MAP_W)
    padded = jnp.pad(grid, ((0, 0), (0, 0), (1, 1), (1, 1)))
    taps = [padded[:, :, row_off:row_off + ROWS, col_off:col_off + MAP_W].reshape(chans, count * ROWS * MAP_W)
            for row_off in range(3) for col_off in range(3)]
    return jnp.stack(taps).reshape(9 * chans, count * ROWS * MAP_W)


def model_front(group_taps, conv_w3, conv_w1, classifier, inputs):
    groups = C // GW
    pieces = []
    for group in range(groups):
        weights = conv_w3[group::groups].reshape(GW, 9 * GW)
        pieces.append(jnp.dot(weights, group_taps[group], preferred_element_type=jnp.float32))
    pre = jnp.stack(pieces, axis=1).reshape(C, -1)
    hidden = jax.nn.silu(pre).astype(jnp.bfloat16)
    z_total = inputs.reshape(C, -1).astype(jnp.float32) + jnp.dot(conv_w1, hidden, preferred_element_type=jnp.float32)
    pooled = jax.nn.silu(z_total).reshape(C, IMG_DEV, ROWS * MAP_W).mean(axis=2)
    logits = jnp.dot(pooled.T, classifier.astype(jnp.float32), precision=lax.Precision.HIGHEST)
    return pre, hidden, z_total, pooled, logits


def reference(images, labels, partner, student_w3, student_w1, student_head, stale_w3, stale_w1, stale_head):
    groups = C // GW

    def one_replica(replica):
        inputs = lax.dynamic_slice_in_dim(images, replica * IMG_DEV, IMG_DEV, 1)
        label_row = lax.dynamic_slice_in_dim(labels, replica * IMG_DEV, IMG_DEV, 0)
        other = partner[replica]
        group_taps = [tap_stack(inputs[group::groups]) for group in range(groups)]
        pre, hidden, z_total, pooled, logits = model_front(group_taps, student_w3[replica], student_w1[replica], student_head[replica], inputs)
        teacher = model_front(group_taps, stale_w3[other], stale_w1[other], stale_head[other], inputs)[4]
        onehot = (label_row[:, None] == jnp.arange(K, dtype=jnp.int32)[None, :]).astype(jnp.float32)
        dlogit = 2.0 * jax.nn.softmax(logits, axis=-1) - onehot - jax.nn.softmax(teacher, axis=-1)
        classifier = student_head[replica].astype(jnp.float32)
        grad_head = jnp.dot(pooled, dlogit, precision=lax.Precision.HIGHEST)
        dpooled = jnp.dot(dlogit, classifier.T, precision=lax.Precision.HIGHEST)
        dz_full = (dpooled.T[:, :, None] / (ROWS * MAP_W)) * dsilu(z_total.reshape(C, IMG_DEV, ROWS * MAP_W))
        dz_half = dz_full.reshape(C, -1).astype(jnp.bfloat16)
        grad_w1 = lax.dot_general(dz_half, hidden, (((1,), (1,)), ((), ())), preferred_element_type=jnp.float32)
        dhidden = lax.dot_general(student_w1[replica], dz_half, (((0,), (0,)), ((), ())), preferred_element_type=jnp.float32)
        dpre = (dhidden * dsilu(pre)).astype(jnp.bfloat16)
        pieces = []
        for group in range(groups):
            part_grad = lax.dot_general(dpre[group::groups], group_taps[group], (((1,), (1,)), ((), ())), preferred_element_type=jnp.float32)
            pieces.append(part_grad.reshape(GW, 9, GW))
        return jnp.stack(pieces, axis=1).reshape(C, 9, GW), grad_w1, grad_head

    return lax.map(one_replica, jnp.arange(N_REP, dtype=jnp.int32))
```

```python
import functools

import jax
import jax.numpy as jnp
from jax import lax
from jax.experimental import pallas as pl
from jax.experimental.pallas import tpu as pltpu
from jax.sharding import PartitionSpec as P

C = 2016
GW = 1008
K = 1000
ROWS = 4
MAP_W = 56
POS = ROWS * MAP_W
N_REP = 16
N_FILT = 16
LOC = C // N_FILT
HALF = LOC // 2
RELAY = 32
CHUNKS = POS // RELAY
LANES = 128
F32 = jnp.float32
BF16 = jnp.bfloat16
MESH = pl.DeviceIdType.MESH


def mm(a, b, dims=((1,), (0,))):
    return lax.dot_general(a, b, (dims, ((), ())), preferred_element_type=F32)


def silu(v):
    return v / (1.0 + jnp.exp(-v))


def dsilu(v):
    sig = 1.0 / (1.0 + jnp.exp(-v))
    return sig * (1.0 + v * (1.0 - sig))


def split3(v):
    hi = v.astype(BF16)
    rest = v - hi.astype(F32)
    mid = rest.astype(BF16)
    low = (rest - mid.astype(F32)).astype(BF16)
    pad = jnp.zeros((13,) + v.shape[1:], BF16)
    return jnp.concatenate([hi, mid, low, pad], axis=0)


class Gather:
    def __init__(self, panel, send, recv, here):
        self.panel, self.send, self.recv, self.here = panel, send, recv, here
        self.started = []

    def copy(self, kind, slot, target):
        where = self.panel.at[:, pl.ds(pl.multiple_of(slot * LANES, LANES), LANES)]
        return pltpu.make_async_remote_copy(
            src_ref=where,
            dst_ref=where,
            send_sem=self.send.at[kind],
            recv_sem=self.recv.at[kind],
            device_id={"rep": self.here.rep, "filt": target},
            device_id_type=MESH,
        )

    def go(self, kind, slot, target):
        made = self.copy(kind, slot, target)
        made.start()
        self.started.append(made)

    def got(self, kind, slot):
        self.copy(kind, slot, self.here.sib).wait_recv()

    def own(self):
        h = self.here
        self.go(0, h.me, h.opp)
        self.go(1, h.me, h.right)
        self.go(2, h.me, h.left)
        self.go(7, h.me, h.sib)

    def across(self):
        h = self.here
        self.got(0, h.opp)
        self.go(3, h.opp, h.right)
        self.go(4, h.opp, h.left)
        self.go(8, h.opp, h.sib)

    def near(self):
        h = self.here
        self.got(1, h.left)
        self.go(5, h.left, h.right)
        self.go(9, h.left, h.sib)
        self.got(2, h.right)
        self.go(10, h.right, h.sib)

    def near_opp(self):
        h = self.here
        self.got(4, h.right_opp)
        self.go(6, h.right_opp, h.left)
        self.go(11, h.right_opp, h.sib)
        self.got(3, h.left_opp)
        self.go(12, h.left_opp, h.sib)

    def far(self):
        h = self.here
        self.got(5, h.far)
        self.go(13, h.far, h.sib)

    def far_opp(self):
        h = self.here
        self.got(6, h.far_opp)
        self.go(14, h.far_opp, h.sib)

    def plane(self):
        h = self.here
        self.got(7, h.sib)
        self.got(9, h.other(h.left))
        self.got(10, h.other(h.right))
        self.got(13, h.other(h.far))

    def plane_opp(self):
        h = self.here
        self.got(8, h.other(h.opp))
        self.got(11, h.other(h.right_opp))
        self.got(12, h.other(h.left_opp))
        self.got(14, h.other(h.far_opp))

    def drain(self):
        for made in self.started:
            made.wait_send()


class Here:
    def __init__(self):
        self.rep = lax.axis_index("rep")
        self.me = lax.axis_index("filt")
        self.z = self.me // 8
        self.y = (self.me % 8) // 2
        self.k = self.me % 2
        self.up = (self.y + 1) % 4
        self.down = (self.y + 3) % 4
        self.beyond = (self.y + 2) % 4
        self.sib = self.at(self.z, self.y, 1 - self.k)
        self.opp = self.at(1 - self.z, self.y, self.k)
        self.right = self.at(self.z, self.up, self.k)
        self.left = self.at(self.z, self.down, self.k)
        self.far = self.at(self.z, self.beyond, self.k)
        self.right_opp = self.at(1 - self.z, self.up, self.k)
        self.left_opp = self.at(1 - self.z, self.down, self.k)
        self.far_opp = self.at(1 - self.z, self.beyond, self.k)

    def at(self, z, y, k):
        return z * 8 + y * 2 + k

    def other(self, slot):
        return slot + 1 - 2 * (slot % 2)


def main_kernel(
    label, partner_h, x_h, w3s_h, w1s_h, hds_h, w3t_h, w1t_h, hdt_h,
    xeo, hc, dz_out, dpre_out, dl_out, pooled_out,
    partner, x, w3s, w3t, wxs, wxt, w1raw, w1p, hds, hdt, xg, xgt, hg, hgt, accs, acct,
    a1, sb, ls, lt, ua, row, sendb, block, ra, rb, rc,
    wsem, gsend, grecv, asend, arecv, lsend, lrecv, rsend, rrecv,
):
    h = Here()
    rep, me = h.rep, h.me

    barrier = pltpu.get_barrier_semaphore()
    for i in range(1, N_REP):
        pl.semaphore_signal(
            barrier, inc=1, device_id={"rep": (rep + i) % N_REP, "filt": me}, device_id_type=MESH
        )
    for i in range(1, N_FILT):
        pl.semaphore_signal(
            barrier, inc=1, device_id={"rep": rep, "filt": (me + i) % N_FILT}, device_id_type=MESH
        )

    loads = [
        pltpu.make_async_copy(src, dst, wsem.at[i])
        for i, (src, dst) in enumerate(
            (
                (x_h, x),
                (partner_h, partner),
                (w3s_h, w3s),
                (w3t_h, w3t),
                (w1s_h, w1raw.at[0]),
                (w1t_h, w1raw.at[1]),
                (hds_h, hds),
                (hdt_h, hdt),
            )
        )
    ]
    for load in loads:
        load.start()

    lane_from = lax.broadcasted_iota(jnp.int32, (LOC, LANES), 0)
    lane_to = lax.broadcasted_iota(jnp.int32, (LOC, LANES), 1)
    inside = lane_to % 64
    perm = jnp.where((inside < HALF) & (lane_from == 2 * inside + lane_to // 64), 1.0, 0.0)
    perm = perm.astype(BF16)
    own = pl.ds(pl.multiple_of(me * LANES, LANES), LANES)
    loads[0].wait()
    xg[:, own] = mm(x[...], perm).astype(BF16)

    pl.semaphore_wait(barrier, N_REP - 1 + N_FILT - 1)

    gx = Gather(xg, gsend.at[0], grecv.at[0], h)
    gxt = Gather(xgt, gsend.at[1], grecv.at[1], h)
    gh = Gather(hg, gsend.at[2], grecv.at[2], h)
    ght = Gather(hgt, gsend.at[3], grecv.at[3], h)

    for i in range(1, N_REP):
        q = (rep + i) % N_REP

        @pl.when(q < CHUNKS)
        def _():
            pltpu.make_async_remote_copy(
                src_ref=xg.at[pl.ds(pl.multiple_of(q * RELAY, RELAY), RELAY), own],
                dst_ref=a1.at[rep],
                send_sem=asend.at[0],
                recv_sem=arecv.at[0],
                device_id={"rep": q, "filt": me},
                device_id_type=MESH,
            ).start()

    gx.own()
    loads[1].wait()

    def ordered(w3, wx, first, last):
        keep = lax.broadcasted_iota(jnp.int32, (64, LOC), 0) < HALF
        even = lax.broadcasted_iota(jnp.int32, (64, LOC), 1) % 2 == 0

        def body(t, carry):
            where = pl.ds(pl.multiple_of(t * LANES, LANES), LOC)
            w = jnp.concatenate([w3[t].astype(F32), jnp.zeros((8, LOC), F32)], axis=0)
            for f in range(N_FILT):
                piece = w[f * HALF : f * HALF + 64]
                wx[f * LANES : f * LANES + 64, where] = jnp.where(
                    keep & even, piece, 0.0
                ).astype(BF16)
                wx[f * LANES + 64 : (f + 1) * LANES, where] = jnp.where(
                    keep & ~even, piece, 0.0
                ).astype(BF16)
            return carry

        lax.fori_loop(first, last, body, 0)

    chunk = pl.ds(pl.multiple_of(rep * RELAY, RELAY), RELAY)
    loads[2].wait()
    ordered(w3s, wxs, 0, 3)

    @pl.when(rep < CHUNKS)
    def _():
        pltpu.make_async_copy(a1.at[pl.ds(0, 15)], a1.at[pl.ds(0, 15)], arecv.at[0]).wait()
        a1[rep] = xg[chunk, own]
        xgt[chunk, own] = a1[partner[rep]]
        for i in range(1, N_REP):
            p = (rep + i) % N_REP
            sb[i] = a1[partner[p]]
            pltpu.make_async_remote_copy(
                src_ref=sb.at[i],
                dst_ref=xgt.at[chunk, own],
                send_sem=asend.at[1],
                recv_sem=arecv.at[1],
                device_id={"rep": p, "filt": me},
                device_id_type=MESH,
            ).start()

    gx.near()
    ordered(w3s, wxs, 3, 6)
    gx.far()
    gx.across()

    @pl.when(rep < CHUNKS)
    def _():
        pltpu.make_async_copy(
            xgt.at[pl.ds(0, RELAY * (CHUNKS - 1)), own],
            xgt.at[pl.ds(0, RELAY * (CHUNKS - 1)), own],
            arecv.at[1],
        ).wait()

    @pl.when(rep >= CHUNKS)
    def _():
        pltpu.make_async_copy(xgt.at[:, own], xgt.at[:, own], arecv.at[1]).wait()

    gxt.own()
    ordered(w3s, wxs, 6, 9)
    gx.near_opp()
    gx.far_opp()

    def conv_half(panel, wx, acc, z, first):
        rows = pl.ds(pl.multiple_of(z * (8 * LANES), 8 * LANES), 8 * LANES)
        for i in range(3):
            where = slice(i * 3 * LANES, (i + 1) * 3 * LANES)
            part = mm(panel[:, rows], wx[rows, where])
            acc[:, where] = part if first else acc[:, where] + part

    lanes = lax.broadcasted_iota(jnp.int32, (POS, LANES), 1)
    column = lax.broadcasted_iota(jnp.int32, (POS, LANES), 0) % MAP_W

    def conv_end(acc):
        total = None
        top = jnp.zeros((MAP_W, LANES), F32)

        def tap(t, low, high):
            return acc[low:high, t * LANES : (t + 1) * LANES]

        for b in range(3):
            part = tap(3 + b, 0, POS)
            part = part + jnp.concatenate([top, tap(b, 0, POS - MAP_W)], axis=0)
            part = part + jnp.concatenate([tap(6 + b, MAP_W, POS), top], axis=0)
            if b == 0:
                part = jnp.where(column >= 1, pltpu.roll(part, 1, 0), 0.0)
            if b == 2:
                part = jnp.where(column <= MAP_W - 2, pltpu.roll(part, POS - 1, 0), 0.0)
            total = part if total is None else total + part
        return total

    def hidden_of(pre):
        return jnp.where(lanes < LOC, silu(pre), 0.0).astype(BF16)

    gxt.near()
    gx.plane()
    conv_half(xg, wxs, accs, h.z, True)
    gxt.far()
    gxt.across()
    gx.plane_opp()
    conv_half(xg, wxs, accs, 1 - h.z, False)
    pre = conv_end(accs)
    hg[:, own] = hidden_of(pre)
    gh.own()
    gxt.near_opp()
    loads[3].wait()
    ordered(w3t, wxt, 0, 4)
    gxt.far_opp()
    ordered(w3t, wxt, 4, 9)
    gh.near()
    gxt.plane()
    conv_half(xgt, wxt, acct, h.z, True)
    gh.far()
    gxt.plane_opp()
    conv_half(xgt, wxt, acct, 1 - h.z, False)
    hgt[:, own] = hidden_of(conv_end(acct))
    ght.own()
    gh.across()

    for which in range(2):
        loads[4 + which].wait()
        for f in range(N_FILT):
            w1p[which, f * LANES : f * LANES + LOC, :] = w1raw[which, f * LOC : (f + 1) * LOC, :]
            w1p[which, f * LANES + LOC : (f + 1) * LANES, :] = jnp.zeros((LANES - LOC, LOC), BF16)

    gh.near_opp()
    ght.near()
    gh.far_opp()
    ght.far()
    ght.across()
    gh.plane()
    gh.plane_opp()

    def logits_of(z, head):
        pooled = jnp.sum(silu(z), axis=0, keepdims=True) * (1.0 / POS)
        parts = mm(split3(pooled), head[...], ((1,), (1,)))
        row[...] = jnp.zeros((1, 1024), F32)
        row[:, :K] = parts[0:1] + parts[1:2] + parts[2:3]
        full = row[...]
        return pooled, jnp.concatenate(
            [full[:, i * LANES : (i + 1) * LANES] for i in range(8)], axis=0
        )

    def give_logits(buf, part, idx):
        buf[me] = part
        for i in range(1, N_FILT):
            pltpu.make_async_remote_copy(
                src_ref=buf.at[me],
                dst_ref=buf.at[me],
                send_sem=lsend.at[idx],
                recv_sem=lrecv.at[idx],
                device_id={"rep": rep, "filt": (me + i) % N_FILT},
                device_id_type=MESH,
            ).start()

    def wait_bytes(buf, count, sem):
        pltpu.make_async_copy(buf.at[pl.ds(0, count)], buf.at[pl.ds(0, count)], sem).wait()

    def sum_logits(buf, idx):
        wait_bytes(buf, N_FILT - 1, lrecv.at[idx])
        return jnp.sum(buf[...], axis=0)

    loads[6].wait()
    loads[7].wait()
    z_mixed = x[...].astype(F32) + mm(hg[...], w1p[0])
    pooled, part = logits_of(z_mixed, hds)
    give_logits(ls, part, 0)
    ght.near_opp()
    ght.far_opp()
    xt = mm(xgt[:, own], perm, ((1,), (1,)))
    ght.plane()
    ght.plane_opp()
    part = logits_of(xt + mm(hgt[...], w1p[1]), hdt)[1]
    give_logits(lt, part, 1)
    for f in range(N_FILT):
        hc[:, f * LOC : (f + 1) * LOC] = hg[:, f * LANES : f * LANES + LOC]
    logits = sum_logits(ls, 0)

    cls = lax.broadcasted_iota(jnp.int32, (8, LANES), 0) * LANES + lax.broadcasted_iota(
        jnp.int32, (8, LANES), 1
    )
    real = cls < K

    def softmax(v):
        top = jnp.max(jnp.where(real, v, -jnp.inf))
        e = jnp.where(real, jnp.exp(v - top), 0.0)
        return e / jnp.sum(e)

    own_part = 2.0 * softmax(logits) - jnp.where(cls == label[0], 1.0, 0.0)
    slope = dsilu(z_mixed) * (1.0 / POS)
    ua[rep] = sum_logits(lt, 1)
    for i in range(1, N_REP):
        pltpu.make_async_remote_copy(
            src_ref=ua.at[rep],
            dst_ref=ua.at[rep],
            send_sem=asend.at[2],
            recv_sem=arecv.at[2],
            device_id={"rep": (rep + i) % N_REP, "filt": me},
            device_id_type=MESH,
        ).start()
    pooled_out[...] = pooled
    for f in range(N_FILT):
        for g in range(2):
            xeo[g * POS : (g + 1) * POS, f * HALF : (f + 1) * HALF] = xg[
                :, f * LANES + 64 * g : f * LANES + 64 * g + HALF
            ]
    wait_bytes(ua, N_REP - 1, arecv.at[2])
    dl = own_part - softmax(ua[partner[rep]])
    dl_out[...] = dl
    dl_row = jnp.concatenate([dl[i : i + 1, :] for i in range(8)], axis=1)[:, :K]
    parts = mm(split3(dl_row), hds[...])
    dz = ((parts[0:1] + parts[1:2] + parts[2:3]) * slope).astype(BF16)
    dz_out[...] = dz

    def remote(src, dst, kind, target):
        return pltpu.make_async_remote_copy(
            src_ref=src,
            dst_ref=dst,
            send_sem=rsend.at[kind],
            recv_sem=rrecv.at[kind],
            device_id={"rep": rep, "filt": target},
            device_id_type=MESH,
        )

    targets = (
        h.at(0, h.beyond, h.k),
        h.at(1, h.beyond, h.k),
        h.at(0, h.up, h.k),
        h.at(1, h.down, h.k),
        h.at(1, h.up, h.k),
        h.at(0, h.down, h.k),
        h.opp,
        me,
    )
    mine_at = pl.ds(pl.multiple_of(h.k * LANES, LANES), LANES)
    other_at = pl.ds(pl.multiple_of((1 - h.k) * LANES, LANES), LANES)
    for z in range(2):
        rows = slice(z * 8 * LANES, (z + 1) * 8 * LANES)
        part = mm(dz, w1p[0, rows, :], ((1,), (1,)))
        for y in range(4):
            block[z * 4 + y] = part[:, y * 2 * LANES : (y + 1) * 2 * LANES]
    sib_copies = []
    for i, slot in enumerate(targets):
        sendb[i] = block[slot // 2, :, other_at].astype(BF16)
        made = remote(sendb.at[i], ra.at[i], i, h.sib)
        made.start()
        sib_copies.append(made)

    def chip_sum(i):
        sib_copies[i].wait_recv()
        return block[targets[i] // 2, :, mine_at] + ra[i].astype(F32)

    ring = []

    def ring_send(i, value, target):
        sendb[8 + i] = value.astype(BF16)
        made = remote(sendb.at[8 + i], rb.at[i], 8 + i, target)
        made.start()
        ring.append(made)

    ring_send(0, chip_sum(0), h.right)
    ring_send(1, chip_sum(1), h.left)
    ring_send(2, chip_sum(4), h.right)
    ring_send(3, chip_sum(5), h.left)
    up0 = chip_sum(2)
    down1 = chip_sum(3)
    ring[0].wait_recv()
    ring_send(4, up0 + rb[0].astype(F32), h.right)
    ring[1].wait_recv()
    ring_send(5, down1 + rb[1].astype(F32), h.left)
    to_opp = chip_sum(6)
    mine = chip_sum(7)
    ring[2].wait_recv()
    ring[3].wait_recv()
    ring[4].wait_recv()
    ring[5].wait_recv()
    low = h.z == 0
    sum0 = rb[4].astype(F32) + rb[3].astype(F32)
    sum1 = rb[5].astype(F32) + rb[2].astype(F32)
    sendb[14] = (to_opp + jnp.where(low, sum1, sum0)).astype(BF16)
    last = remote(sendb.at[14], rc, 14, h.opp)
    last.start()
    mine = mine + jnp.where(low, sum0, sum1)
    slope = dsilu(pre)
    last.wait_recv()
    dhidden = mine + rc[...].astype(F32)
    dpre_out[...] = (dhidden * slope)[:, :LOC].astype(BF16)

    for gather in (gx, gxt, gh, ght):
        gather.drain()
    for made in sib_copies + ring + [last]:
        made.wait_send()
    wait_bytes(ls, N_FILT - 1, lsend.at[0])
    wait_bytes(lt, N_FILT - 1, lsend.at[1])
    wait_bytes(ua, N_REP - 1, asend.at[2])

    @pl.when(rep < CHUNKS)
    def _():
        wait_bytes(sb, CHUNKS - 1, asend.at[0])
        wait_bytes(sb, N_REP - 1, asend.at[1])

    @pl.when(rep >= CHUNKS)
    def _():
        wait_bytes(sb, CHUNKS, asend.at[0])


def grads_kernel(xeo, hc, dz, dpre, dl, pooled, gw3, gw1, gh, turned, r3, r1, r0, sem):
    copies = []

    def out(src, dst, i):
        made = pltpu.make_async_copy(src, dst, sem.at[i])
        made.start()
        copies.append(made)

    dp = dpre[...].astype(F32)
    even = lax.broadcasted_iota(jnp.int32, (POS, LOC), 1) % 2 == 0
    column = lax.broadcasted_iota(jnp.int32, (POS, LOC), 0) % MAP_W
    zero = jnp.zeros((MAP_W, LOC), F32)
    for b in range(3):
        moved = dp
        if b == 0:
            moved = pltpu.roll(jnp.where(column >= 1, dp, 0.0), POS - 1, 0)
        if b == 2:
            moved = pltpu.roll(jnp.where(column <= MAP_W - 2, dp, 0.0), 1, 0)
        for a in range(3):
            d = moved
            if a == 0:
                d = jnp.concatenate([moved[MAP_W:], zero], axis=0)
            if a == 2:
                d = jnp.concatenate([zero, moved[: POS - MAP_W]], axis=0)
            where = slice(a * LANES, a * LANES + LOC)
            turned[b, :POS, where] = jnp.where(even, d, 0.0).astype(BF16)
            turned[b, POS:, where] = jnp.where(even, 0.0, d).astype(BF16)
    for b in range(3):
        rows = mm(turned[b], xeo[...], ((0,), (0,)))
        for a in range(3):
            t = 3 * a + b
            r3[t] = rows[a * LANES : a * LANES + LOC]
            out(r3.at[t], gw3.at[:, t, 0, :], t)
    r1[...] = mm(dz[...], hc[...], ((0,), (0,)))
    out(r1, gw1.at[:, 0, :], 9)
    flip = dl[...].T
    for i in range(8):
        size = min(LANES, K - i * LANES)
        r0[i * LANES : i * LANES + size, :] = flip[:size, i : i + 1] * pooled[...]
    out(r0, gh, 10)
    for made in copies:
        made.wait()


def per_device(
    images, labels, partner, student_w3, student_w1, student_head, stale_w3, stale_w1, stale_head
):
    vmem = pl.BlockSpec(memory_space=pltpu.VMEM)
    hbm = pl.BlockSpec(memory_space=pltpu.HBM)
    sds = jax.ShapeDtypeStruct
    dma = pltpu.SemaphoreType.DMA
    weights = []
    for w3, w1, head in (
        (student_w3, student_w1, student_head),
        (stale_w3, stale_w1, stale_head),
    ):
        weights += [w3[0].transpose(1, 2, 0), w1[0].T, head[0].T]
    saved = pl.pallas_call(
        main_kernel,
        out_shape=(
            pltpu.VMEM((2 * POS, GW), BF16),
            pltpu.VMEM((POS, C), BF16),
            pltpu.VMEM((POS, LOC), BF16),
            pltpu.VMEM((POS, LOC), BF16),
            pltpu.VMEM((8, LANES), F32),
            pltpu.VMEM((1, LOC), F32),
        ),
        in_specs=[pl.BlockSpec(memory_space=pltpu.SMEM)] + [hbm] * 8,
        out_specs=[vmem] * 6,
        scratch_shapes=[
            pltpu.SMEM((N_REP,), jnp.int32),
            pltpu.VMEM((POS, LOC), BF16),
            pltpu.VMEM((9, GW, LOC), BF16),
            pltpu.VMEM((9, GW, LOC), BF16),
            pltpu.VMEM((N_FILT * LANES, 9 * LANES), BF16),
            pltpu.VMEM((N_FILT * LANES, 9 * LANES), BF16),
            pltpu.VMEM((2, C, LOC), BF16),
            pltpu.VMEM((2, N_FILT * LANES, LOC), BF16),
            pltpu.VMEM((K, LOC), BF16),
            pltpu.VMEM((K, LOC), BF16),
            pltpu.VMEM((POS, N_FILT * LANES), BF16),
            pltpu.VMEM((POS, N_FILT * LANES), BF16),
            pltpu.VMEM((POS, N_FILT * LANES), BF16),
            pltpu.VMEM((POS, N_FILT * LANES), BF16),
            pltpu.VMEM((POS, 9 * LANES), F32),
            pltpu.VMEM((POS, 9 * LANES), F32),
            pltpu.VMEM((N_REP, RELAY, LANES), BF16),
            pltpu.VMEM((N_REP, RELAY, LANES), BF16),
            pltpu.VMEM((N_FILT, 8, LANES), F32),
            pltpu.VMEM((N_FILT, 8, LANES), F32),
            pltpu.VMEM((N_REP, 8, LANES), F32),
            pltpu.VMEM((1, 1024), F32),
            pltpu.VMEM((15, POS, LANES), BF16),
            pltpu.VMEM((8, POS, 2 * LANES), F32),
            pltpu.VMEM((8, POS, LANES), BF16),
            pltpu.VMEM((6, POS, LANES), BF16),
            pltpu.VMEM((POS, LANES), BF16),
            dma((8,)),
            dma((4, 15)),
            dma((4, 15)),
            dma((3,)),
            dma((3,)),
            dma((2,)),
            dma((2,)),
            dma((15,)),
            dma((15,)),
        ],
        compiler_params=pltpu.CompilerParams(
            collective_id=0, has_side_effects=True, vmem_limit_bytes=48 * 1024 * 1024
        ),
        name="step",
    )(
        labels,
        *(
            pltpu.with_memory_space_constraint(a, pltpu.HBM)
            for a in (partner, images.transpose(1, 2, 0)[0], *weights)
        ),
    )
    gw3, gw1, gh = pl.pallas_call(
        grads_kernel,
        out_shape=(
            sds((LOC, 9, 1, GW), F32),
            sds((LOC, 1, C), F32),
            sds((K, LOC), F32),
        ),
        in_specs=[vmem] * 6,
        out_specs=[hbm] * 3,
        scratch_shapes=[
            pltpu.VMEM((3, 2 * POS, 3 * LANES), BF16),
            pltpu.VMEM((9, LOC, GW), F32),
            pltpu.VMEM((LOC, C), F32),
            pltpu.VMEM((K, LOC), F32),
            dma((11,)),
        ],
        compiler_params=pltpu.CompilerParams(vmem_limit_bytes=40 * 1024 * 1024),
        name="grads",
    )(*saved)
    return (gw3.transpose(2, 0, 1, 3), gw1.transpose(1, 0, 2), gh.T[None])


def solution(mesh):
    in_specs = (
        P("filt", "rep", None),
        P("rep"),
        P(),
        P("rep", "filt", None, None),
        P("rep", "filt", None),
        P("rep", "filt", None),
        P("rep", "filt", None, None),
        P("rep", "filt", None),
        P("rep", "filt", None),
    )
    out_specs = (P("rep", "filt", None, None), P("rep", "filt", None), P("rep", "filt", None))
    return jax.shard_map(
        per_device, mesh=mesh, in_specs=in_specs, out_specs=out_specs, check_vma=False
    )
```

```python
import functools

import jax
import jax.numpy as jnp
from jax import lax
from jax.experimental import pallas as pl
from jax.experimental.pallas import tpu as pltpu
from jax.sharding import PartitionSpec as P

C = 2016
GW = 1008
K = 1000
ROWS = 4
MAP_W = 56
POS = ROWS * MAP_W
N_REP = 16
N_FILT = 16
LOC = C // N_FILT
HALF = LOC // 2
RELAY = 32
CHUNKS = POS // RELAY
LANES = 128
F32 = jnp.float32
BF16 = jnp.bfloat16
MESH = pl.DeviceIdType.MESH


def mm(a, b, dims=((1,), (0,))):
    return lax.dot_general(a, b, (dims, ((), ())), preferred_element_type=F32)


def silu(v):
    return v / (1.0 + jnp.exp(-v))


def dsilu(v):
    sig = 1.0 / (1.0 + jnp.exp(-v))
    return sig * (1.0 + v * (1.0 - sig))


def split3(v):
    hi = v.astype(BF16)
    rest = v - hi.astype(F32)
    mid = rest.astype(BF16)
    low = (rest - mid.astype(F32)).astype(BF16)
    pad = jnp.zeros((13,) + v.shape[1:], BF16)
    return jnp.concatenate([hi, mid, low, pad], axis=0)


class Gather:
    def __init__(self, panel, send, recv, here, parts=1):
        self.panel, self.send, self.recv, self.here = panel, send, recv, here
        self.parts = parts
        self.started = []

    def copy(self, kind, slot, target, part=None):
        where = self.panel.at[slot]
        if part is not None and self.parts > 1:
            size = POS // self.parts
            where = self.panel.at[slot, pl.ds(part * size, size)]
            kind = kind if part == 0 else 15 + (0, 3, 4, 6).index(kind)
        return pltpu.make_async_remote_copy(
            src_ref=where,
            dst_ref=where,
            send_sem=self.send.at[kind],
            recv_sem=self.recv.at[kind],
            device_id={"rep": self.here.rep, "filt": target},
            device_id_type=MESH,
        )

    def go(self, kind, slot, target, part=None):
        made = self.copy(kind, slot, target, part)
        made.start()
        self.started.append(made)

    def got(self, kind, slot, part=None):
        self.copy(kind, slot, self.here.sib, part).wait_recv()

    def own(self):
        for part in range(self.parts):
            self.go(0, self.here.me, self.here.opp, part)
        self.spread()

    def spread(self):
        h = self.here
        self.go(1, h.me, h.right)
        self.go(2, h.me, h.left)
        self.go(5, h.me, h.far)
        self.go(7, h.me, h.sib)

    def across(self):
        for part in range(self.parts):
            self.got(0, self.here.opp, part)
            self.spread_opp(part)
        self.go(8, self.here.opp, self.here.sib)

    def spread_opp(self, part):
        h = self.here
        self.go(3, h.opp, h.right, part)
        self.go(4, h.opp, h.left, part)
        self.go(6, h.opp, h.far, part)

    def near(self):
        h = self.here
        for kind, slot, onward in ((1, h.left, 9), (2, h.right, 10), (5, h.far, 13)):
            self.got(kind, slot)
            self.go(onward, slot, h.sib)

    def near_opp(self):
        h = self.here
        for kind, slot, onward in ((3, h.left_opp, 11), (4, h.right_opp, 12), (6, h.far_opp, 14)):
            for part in range(self.parts):
                self.got(kind, slot, part)
            self.go(onward, slot, h.sib)

    def plane(self):
        h = self.here
        self.got(7, h.sib)
        self.got(9, h.other(h.left))
        self.got(10, h.other(h.right))
        self.got(13, h.other(h.far))

    def plane_opp(self):
        h = self.here
        self.got(8, h.other(h.opp))
        self.got(11, h.other(h.left_opp))
        self.got(12, h.other(h.right_opp))
        self.got(14, h.other(h.far_opp))

    def drain(self):
        for made in self.started:
            made.wait_send()


class Here:
    def __init__(self):
        self.rep = lax.axis_index("rep")
        self.me = lax.axis_index("filt")
        self.z = self.me // 8
        self.y = (self.me % 8) // 2
        self.k = self.me % 2
        self.up = (self.y + 1) % 4
        self.down = (self.y + 3) % 4
        self.beyond = (self.y + 2) % 4
        self.sib = self.at(self.z, self.y, 1 - self.k)
        self.opp = self.at(1 - self.z, self.y, self.k)
        self.right = self.at(self.z, self.up, self.k)
        self.left = self.at(self.z, self.down, self.k)
        self.far = self.at(self.z, self.beyond, self.k)
        self.right_opp = self.at(1 - self.z, self.up, self.k)
        self.left_opp = self.at(1 - self.z, self.down, self.k)
        self.far_opp = self.at(1 - self.z, self.beyond, self.k)

    def at(self, z, y, k):
        return z * 8 + y * 2 + k

    def other(self, slot):
        return slot + 1 - 2 * (slot % 2)


def main_kernel(
    label, partner_h, x_h, w3s_h, w1s_h, hds_h, w3t_h, w1t_h, hdt_h,
    xeo, dpre_out, gw1_out, gh_out,
    partner, x, hc, w3s, w3t, wxs, wxt, w1raw, w1p, hds, hdt, xg, xgt, hg, hgt, accs, acct,
    a1, sb, ls, lt, ua, row, sendb, block, ra, rb, rc,
    wsem, gsend, grecv, asend, arecv, lsend, lrecv, rsend, rrecv,
):
    h = Here()
    rep, me = h.rep, h.me

    barrier = pltpu.get_barrier_semaphore()
    for i in range(1, N_REP):
        pl.semaphore_signal(
            barrier, inc=1, device_id={"rep": (rep + i) % N_REP, "filt": me}, device_id_type=MESH
        )
    for i in range(1, N_FILT):
        pl.semaphore_signal(
            barrier, inc=1, device_id={"rep": rep, "filt": (me + i) % N_FILT}, device_id_type=MESH
        )

    loads = [
        pltpu.make_async_copy(src, dst, wsem.at[i])
        for i, (src, dst) in enumerate(
            (
                (x_h, x),
                (partner_h, partner),
                (w3s_h, w3s),
                (w3t_h, w3t),
                (w1s_h, w1raw.at[0]),
                (w1t_h, w1raw.at[1]),
                (hds_h, hds),
                (hdt_h, hdt),
            )
        )
    ]
    for load in loads:
        load.start()

    lane_from = lax.broadcasted_iota(jnp.int32, (LOC, LANES), 0)
    lane_to = lax.broadcasted_iota(jnp.int32, (LOC, LANES), 1)
    inside = lane_to % 64
    perm = jnp.where((inside < HALF) & (lane_from == 2 * inside + lane_to // 64), 1.0, 0.0)
    perm = perm.astype(BF16)
    loads[0].wait()
    xg[me] = mm(x[...], perm).astype(BF16)

    pl.semaphore_wait(barrier, N_REP - 1 + N_FILT - 1)

    gx = Gather(xg, gsend.at[0], grecv.at[0], h)
    gxt = Gather(xgt, gsend.at[1], grecv.at[1], h)
    gh = Gather(hg, gsend.at[2], grecv.at[2], h)
    ght = Gather(hgt, gsend.at[3], grecv.at[3], h, 2)

    for i in range(1, N_REP):
        q = (rep + i) % N_REP

        @pl.when((q % 2 == 0) & (q < 2 * CHUNKS))
        def _():
            pltpu.make_async_remote_copy(
                src_ref=xg.at[me, pl.ds(pl.multiple_of(q // 2 * RELAY, RELAY), RELAY)],
                dst_ref=a1.at[rep],
                send_sem=asend.at[0],
                recv_sem=arecv.at[0],
                device_id={"rep": q, "filt": me},
                device_id_type=MESH,
            ).start()

    gx.own()
    loads[1].wait()

    def ordered(w3, wx, first, last):
        keep = lax.broadcasted_iota(jnp.int32, (64, LOC), 0) < HALF
        even = lax.broadcasted_iota(jnp.int32, (64, LOC), 1) % 2 == 0

        def body(t, carry):
            where = pl.ds(pl.multiple_of(t * LANES, LANES), LOC)
            w = jnp.concatenate([w3[t].astype(F32), jnp.zeros((8, LOC), F32)], axis=0)
            for f in range(N_FILT):
                piece = w[f * HALF : f * HALF + 64]
                wx[f * LANES : f * LANES + 64, where] = jnp.where(
                    keep & even, piece, 0.0
                ).astype(BF16)
                wx[f * LANES + 64 : (f + 1) * LANES, where] = jnp.where(
                    keep & ~even, piece, 0.0
                ).astype(BF16)
            return carry

        lax.fori_loop(first, last, body, 0)

    relay = (rep % 2 == 0) & (rep < 2 * CHUNKS)
    chunk = pl.ds(pl.multiple_of(rep % (2 * CHUNKS) // 2 * RELAY, RELAY), RELAY)
    loads[2].wait()
    ordered(w3s, wxs, 0, 3)

    @pl.when(relay)
    def _():
        pltpu.make_async_copy(a1.at[pl.ds(0, 15)], a1.at[pl.ds(0, 15)], arecv.at[0]).wait()
        a1[rep] = xg[me, chunk]
        xgt[me, chunk] = a1[partner[rep]]
        for i in range(N_REP):
            p = (rep + i) % N_REP
            sb[i] = a1[partner[p]]
            for plane, target in enumerate((h.opp, me)):
                if i > 0 or plane == 0:
                    pltpu.make_async_remote_copy(
                        src_ref=sb.at[i],
                        dst_ref=xgt.at[me, chunk],
                        send_sem=asend.at[1 + 2 * plane],
                        recv_sem=arecv.at[1 + 2 * plane],
                        device_id={"rep": p, "filt": target},
                        device_id_type=MESH,
                    ).start()

    gx.near()
    ordered(w3s, wxs, 3, 7)
    gx.across()

    @pl.when(relay)
    def _():
        pltpu.make_async_copy(
            xgt.at[me, pl.ds(0, RELAY * (CHUNKS - 1))],
            xgt.at[me, pl.ds(0, RELAY * (CHUNKS - 1))],
            arecv.at[3],
        ).wait()

    @pl.when(jnp.logical_not(relay))
    def _():
        pltpu.make_async_copy(xgt.at[me], xgt.at[me], arecv.at[3]).wait()

    gxt.spread()
    pltpu.make_async_copy(xgt.at[h.opp], xgt.at[h.opp], arecv.at[1]).wait()
    gxt.spread_opp(0)
    gxt.go(8, h.opp, h.sib)
    ordered(w3s, wxs, 7, 9)

    def conv_half(panel, wx, acc, z, first):
        rows = pl.ds(pl.multiple_of(z * (8 * LANES), 8 * LANES), 8 * LANES)
        left = jnp.concatenate([panel[z * 8 + i] for i in range(8)], axis=1)
        for i in range(3):
            where = slice(i * 3 * LANES, (i + 1) * 3 * LANES)
            part = mm(left, wx[rows, where])
            acc[:, where] = part if first else acc[:, where] + part

    lanes = lax.broadcasted_iota(jnp.int32, (POS, LANES), 1)
    column = lax.broadcasted_iota(jnp.int32, (POS, LANES), 0) % MAP_W

    def conv_end(acc):
        total = None
        top = jnp.zeros((MAP_W, LANES), F32)

        def tap(t, low, high):
            return acc[low:high, t * LANES : (t + 1) * LANES]

        for b in range(3):
            part = tap(3 + b, 0, POS)
            part = part + jnp.concatenate([top, tap(b, 0, POS - MAP_W)], axis=0)
            part = part + jnp.concatenate([tap(6 + b, MAP_W, POS), top], axis=0)
            if b == 0:
                part = jnp.where(column >= 1, pltpu.roll(part, 1, 0), 0.0)
            if b == 2:
                part = jnp.where(column <= MAP_W - 2, pltpu.roll(part, POS - 1, 0), 0.0)
            total = part if total is None else total + part
        return total

    def hidden_of(pre):
        return jnp.where(lanes < LOC, silu(pre), 0.0).astype(BF16)

    gx.plane()
    conv_half(xg, wxs, accs, h.z, True)
    loads[3].wait()
    ordered(w3t, wxt, 0, 3)
    gxt.near()
    gx.near_opp()
    ordered(w3t, wxt, 3, 6)
    gx.plane_opp()
    conv_half(xg, wxs, accs, 1 - h.z, False)
    gxt.near_opp()
    pre = conv_end(accs)
    hg[me] = hidden_of(pre)
    gh.own()
    ordered(w3t, wxt, 6, 9)
    gxt.plane()
    conv_half(xgt, wxt, acct, h.z, True)
    gxt.plane_opp()
    conv_half(xgt, wxt, acct, 1 - h.z, False)
    hgt[me] = hidden_of(conv_end(acct))
    ght.own()
    gh.near()
    gh.across()

    for which in range(2):
        loads[4 + which].wait()
        for f in range(N_FILT):
            w1p[which, f * LANES : f * LANES + LOC, :] = w1raw[which, f * LOC : (f + 1) * LOC, :]
            w1p[which, f * LANES + LOC : (f + 1) * LANES, :] = jnp.zeros((LANES - LOC, LOC), BF16)

    gh.near_opp()
    ght.near()
    ght.across()
    gh.plane()
    gh.plane_opp()
    ght.near_opp()

    def whole(panel):
        return jnp.concatenate([panel[i] for i in range(N_FILT)], axis=1)

    def logits_of(z, head):
        pooled = jnp.sum(silu(z), axis=0, keepdims=True) * (1.0 / POS)
        parts = mm(split3(pooled), head[...], ((1,), (1,)))
        row[...] = jnp.zeros((1, 1024), F32)
        row[:, :K] = parts[0:1] + parts[1:2] + parts[2:3]
        full = row[...]
        return pooled, jnp.concatenate(
            [full[:, i * LANES : (i + 1) * LANES] for i in range(8)], axis=0
        )

    def give_logits(buf, part, idx):
        buf[me] = part
        for i in range(1, N_FILT):
            pltpu.make_async_remote_copy(
                src_ref=buf.at[me],
                dst_ref=buf.at[me],
                send_sem=lsend.at[idx],
                recv_sem=lrecv.at[idx],
                device_id={"rep": rep, "filt": (me + i) % N_FILT},
                device_id_type=MESH,
            ).start()

    def wait_bytes(buf, count, sem):
        pltpu.make_async_copy(buf.at[pl.ds(0, count)], buf.at[pl.ds(0, count)], sem).wait()

    def sum_logits(buf, idx):
        wait_bytes(buf, N_FILT - 1, lrecv.at[idx])
        return jnp.sum(buf[...], axis=0)

    loads[6].wait()
    loads[7].wait()
    z_mixed = x[...].astype(F32) + mm(whole(hg), w1p[0])
    pooled, part = logits_of(z_mixed, hds)
    give_logits(ls, part, 0)
    xt = mm(xgt[me], perm, ((1,), (1,)))
    ght.plane()
    ght.plane_opp()
    part = logits_of(xt + mm(whole(hgt), w1p[1]), hdt)[1]
    give_logits(lt, part, 1)
    for f in range(N_FILT):
        hc[:, f * LOC : (f + 1) * LOC] = hg[f, :, :LOC]
    logits = sum_logits(ls, 0)

    cls = lax.broadcasted_iota(jnp.int32, (8, LANES), 0) * LANES + lax.broadcasted_iota(
        jnp.int32, (8, LANES), 1
    )
    real = cls < K

    def softmax(v):
        top = jnp.max(jnp.where(real, v, -jnp.inf))
        e = jnp.where(real, jnp.exp(v - top), 0.0)
        return e / jnp.sum(e)

    own_part = 2.0 * softmax(logits) - jnp.where(cls == label[0], 1.0, 0.0)
    slope = dsilu(z_mixed) * (1.0 / POS)
    ua[rep] = sum_logits(lt, 1)
    for i in range(1, N_REP):
        pltpu.make_async_remote_copy(
            src_ref=ua.at[rep],
            dst_ref=ua.at[rep],
            send_sem=asend.at[2],
            recv_sem=arecv.at[2],
            device_id={"rep": (rep + i) % N_REP, "filt": me},
            device_id_type=MESH,
        ).start()
    for f in range(N_FILT):
        for g in range(2):
            xeo[g * POS : (g + 1) * POS, f * HALF : (f + 1) * HALF] = xg[
                f, :, 64 * g : 64 * g + HALF
            ]
    wait_bytes(ua, N_REP - 1, arecv.at[2])
    dl = own_part - softmax(ua[partner[rep]])
    dl_row = jnp.concatenate([dl[i : i + 1, :] for i in range(8)], axis=1)[:, :K]
    parts = mm(split3(dl_row), hds[...])
    dz = ((parts[0:1] + parts[1:2] + parts[2:3]) * slope).astype(BF16)

    def remote(src, dst, kind, target):
        return pltpu.make_async_remote_copy(
            src_ref=src,
            dst_ref=dst,
            send_sem=rsend.at[kind],
            recv_sem=rrecv.at[kind],
            device_id={"rep": rep, "filt": target},
            device_id_type=MESH,
        )

    zz = 1 - h.z
    ya = (h.y + 1 + 2 * zz) % 4
    yb = (h.y + 1 + 2 * h.z) % 4
    side_a = h.at(h.z, ya, h.k)
    side_b = h.at(h.z, yb, h.k)
    mine_at = pl.ds(pl.multiple_of(h.k * LANES, LANES), LANES)
    other_at = pl.ds(pl.multiple_of((1 - h.k) * LANES, LANES), LANES)
    places = ((h.beyond, yb, ya, h.y), (h.beyond, ya, yb, h.y))
    sib_copies = []
    for i, z in enumerate((zz, h.z)):
        rows = pl.ds(pl.multiple_of(z * 8 * LANES, 8 * LANES), 8 * LANES)
        part = mm(dz, w1p[0, rows, :], ((1,), (1,)))
        for y in range(4):
            block[i * 4 + y] = part[:, y * 2 * LANES : (y + 1) * 2 * LANES]
        for j, y in enumerate(places[i]):
            sendb[i * 4 + j] = block[i * 4 + y, :, other_at].astype(BF16)
            made = remote(sendb.at[i * 4 + j], ra.at[i * 4 + j], i * 4 + j, h.sib)
            made.start()
            sib_copies.append(made)

    def chip_sum(i, j):
        sib_copies[i * 4 + j].wait_recv()
        return block[i * 4 + places[i][j], :, mine_at] + ra[i * 4 + j].astype(F32)

    ring = []

    def ring_send(value, target):
        i = len(ring)
        sendb[8 + i] = value.astype(BF16)
        made = remote(sendb.at[8 + i], rb.at[i], 8 + i, target)
        made.start()
        ring.append(made)

    def arrived(i):
        ring[i].wait_recv()
        return rb[i].astype(F32)

    ring_send(chip_sum(0, 0), side_a)
    ring_send(chip_sum(0, 1), side_b)
    ring_send(chip_sum(1, 0), side_b)
    ring_send(chip_sum(1, 1), side_a)
    onward = chip_sum(0, 2)
    ring_send(onward + arrived(0), side_a)
    onward = chip_sum(1, 2)
    ring_send(onward + arrived(2), side_b)
    to_opp = chip_sum(0, 3) + arrived(1)
    sendb[14] = (to_opp + arrived(4)).astype(BF16)
    last = remote(sendb.at[14], rc, 14, h.opp)
    last.start()
    mine = chip_sum(1, 3) + arrived(3)
    mine = mine + arrived(5)
    gw1_out[...] = mm(dz, hc[...], ((0,), (0,)))
    flip = dl.T
    for i in range(8):
        size = min(LANES, K - i * LANES)
        gh_out[i * LANES : i * LANES + size, :] = flip[:size, i : i + 1] * pooled
    slope = dsilu(pre)
    last.wait_recv()
    dhidden = mine + rc[...].astype(F32)
    dpre_out[...] = (dhidden * slope)[:, :LOC].astype(BF16)

    for gather in (gx, gxt, gh, ght):
        gather.drain()
    for made in sib_copies + ring + [last]:
        made.wait_send()
    wait_bytes(ls, N_FILT - 1, lsend.at[0])
    wait_bytes(lt, N_FILT - 1, lsend.at[1])
    wait_bytes(ua, N_REP - 1, asend.at[2])

    @pl.when(relay)
    def _():
        wait_bytes(sb, CHUNKS - 1, asend.at[0])
        wait_bytes(sb, N_REP, asend.at[1])
        wait_bytes(sb, N_REP - 1, asend.at[3])

    @pl.when(jnp.logical_not(relay))
    def _():
        wait_bytes(sb, CHUNKS, asend.at[0])


def grads_kernel(xeo, dpre, r1, r0, gw3, gw1, gh, turned, r3, sem):
    copies = []

    def out(src, dst, i):
        made = pltpu.make_async_copy(src, dst, sem.at[i])
        made.start()
        copies.append(made)

    out(r1, gw1.at[:, 0, :], 9)
    out(r0, gh, 10)
    dp = dpre[...].astype(F32)
    even = lax.broadcasted_iota(jnp.int32, (POS, LOC), 1) % 2 == 0
    column = lax.broadcasted_iota(jnp.int32, (POS, LOC), 0) % MAP_W
    zero = jnp.zeros((MAP_W, LOC), F32)
    for b in range(3):
        moved = dp
        if b == 0:
            moved = pltpu.roll(jnp.where(column >= 1, dp, 0.0), POS - 1, 0)
        if b == 2:
            moved = pltpu.roll(jnp.where(column <= MAP_W - 2, dp, 0.0), 1, 0)
        for a in range(3):
            d = moved
            if a == 0:
                d = jnp.concatenate([moved[MAP_W:], zero], axis=0)
            if a == 2:
                d = jnp.concatenate([zero, moved[: POS - MAP_W]], axis=0)
            where = slice(a * LANES, a * LANES + LOC)
            turned[b, :POS, where] = jnp.where(even, d, 0.0).astype(BF16)
            turned[b, POS:, where] = jnp.where(even, 0.0, d).astype(BF16)
    for b in range(3):
        rows = mm(turned[b], xeo[...], ((0,), (0,)))
        for a in range(3):
            t = 3 * a + b
            r3[t] = rows[a * LANES : a * LANES + LOC]
            out(r3.at[t], gw3.at[:, t, 0, :], t)
    for made in copies:
        made.wait()


def per_device(
    images, labels, partner, student_w3, student_w1, student_head, stale_w3, stale_w1, stale_head
):
    vmem = pl.BlockSpec(memory_space=pltpu.VMEM)
    hbm = pl.BlockSpec(memory_space=pltpu.HBM)
    sds = jax.ShapeDtypeStruct
    dma = pltpu.SemaphoreType.DMA
    weights = []
    for w3, w1, head in (
        (student_w3, student_w1, student_head),
        (stale_w3, stale_w1, stale_head),
    ):
        weights += [w3[0].transpose(1, 2, 0), w1[0].T, head[0].T]
    saved = pl.pallas_call(
        main_kernel,
        out_shape=(
            pltpu.VMEM((2 * POS, GW), BF16),
            pltpu.VMEM((POS, LOC), BF16),
            pltpu.VMEM((LOC, C), F32),
            pltpu.VMEM((K, LOC), F32),
        ),
        in_specs=[pl.BlockSpec(memory_space=pltpu.SMEM)] + [hbm] * 8,
        out_specs=[vmem] * 4,
        scratch_shapes=[
            pltpu.SMEM((N_REP,), jnp.int32),
            pltpu.VMEM((POS, LOC), BF16),
            pltpu.VMEM((POS, C), BF16),
            pltpu.VMEM((9, GW, LOC), BF16),
            pltpu.VMEM((9, GW, LOC), BF16),
            pltpu.VMEM((N_FILT * LANES, 9 * LANES), BF16),
            pltpu.VMEM((N_FILT * LANES, 9 * LANES), BF16),
            pltpu.VMEM((2, C, LOC), BF16),
            pltpu.VMEM((2, N_FILT * LANES, LOC), BF16),
            pltpu.VMEM((K, LOC), BF16),
            pltpu.VMEM((K, LOC), BF16),
            pltpu.VMEM((N_FILT, POS, LANES), BF16),
            pltpu.VMEM((N_FILT, POS, LANES), BF16),
            pltpu.VMEM((N_FILT, POS, LANES), BF16),
            pltpu.VMEM((N_FILT, POS, LANES), BF16),
            pltpu.VMEM((POS, 9 * LANES), F32),
            pltpu.VMEM((POS, 9 * LANES), F32),
            pltpu.VMEM((N_REP, RELAY, LANES), BF16),
            pltpu.VMEM((N_REP, RELAY, LANES), BF16),
            pltpu.VMEM((N_FILT, 8, LANES), F32),
            pltpu.VMEM((N_FILT, 8, LANES), F32),
            pltpu.VMEM((N_REP, 8, LANES), F32),
            pltpu.VMEM((1, 1024), F32),
            pltpu.VMEM((15, POS, LANES), BF16),
            pltpu.VMEM((8, POS, 2 * LANES), F32),
            pltpu.VMEM((8, POS, LANES), BF16),
            pltpu.VMEM((6, POS, LANES), BF16),
            pltpu.VMEM((POS, LANES), BF16),
            dma((8,)),
            dma((4, 19)),
            dma((4, 19)),
            dma((4,)),
            dma((4,)),
            dma((2,)),
            dma((2,)),
            dma((15,)),
            dma((15,)),
        ],
        compiler_params=pltpu.CompilerParams(
            collective_id=0, has_side_effects=True, vmem_limit_bytes=48 * 1024 * 1024
        ),
        name="step",
    )(
        labels,
        *(
            pltpu.with_memory_space_constraint(a, pltpu.HBM)
            for a in (partner, images.transpose(1, 2, 0)[0], *weights)
        ),
    )
    gw3, gw1, gh = pl.pallas_call(
        grads_kernel,
        out_shape=(
            sds((LOC, 9, 1, GW), F32),
            sds((LOC, 1, C), F32),
            sds((K, LOC), F32),
        ),
        in_specs=[vmem] * 4,
        out_specs=[hbm] * 3,
        scratch_shapes=[
            pltpu.VMEM((3, 2 * POS, 3 * LANES), BF16),
            pltpu.VMEM((9, LOC, GW), F32),
            dma((11,)),
        ],
        compiler_params=pltpu.CompilerParams(vmem_limit_bytes=40 * 1024 * 1024),
        name="grads",
    )(*saved)
    return (gw3.transpose(2, 0, 1, 3), gw1.transpose(1, 0, 2), gh.T[None])


def solution(mesh):
    in_specs = (
        P("filt", "rep", None),
        P("rep"),
        P(),
        P("rep", "filt", None, None),
        P("rep", "filt", None),
        P("rep", "filt", None),
        P("rep", "filt", None, None),
        P("rep", "filt", None),
        P("rep", "filt", None),
    )
    out_specs = (P("rep", "filt", None, None), P("rep", "filt", None), P("rep", "filt", None))
    return jax.shard_map(
        per_device, mesh=mesh, in_specs=in_specs, out_specs=out_specs, check_vma=False
    )
```

```python
import functools

import jax
import jax.numpy as jnp
from jax import lax
from jax.experimental import pallas as pl
from jax.experimental.pallas import tpu as pltpu
from jax.sharding import PartitionSpec as P

C = 2016
GW = 1008
K = 1000
ROWS = 4
MAP_W = 56
POS = ROWS * MAP_W
N_REP = 16
N_FILT = 16
LOC = C // N_FILT
HALF = LOC // 2
RELAY = 32
CHUNKS = POS // RELAY
LANES = 128
F32 = jnp.float32
BF16 = jnp.bfloat16
MESH = pl.DeviceIdType.MESH


def mm(a, b, dims=((1,), (0,))):
    return lax.dot_general(a, b, (dims, ((), ())), preferred_element_type=F32)


def silu(v):
    return v / (1.0 + jnp.exp(-v))


def dsilu(v):
    sig = 1.0 / (1.0 + jnp.exp(-v))
    return sig * (1.0 + v * (1.0 - sig))


def split3(v):
    hi = v.astype(BF16)
    rest = v - hi.astype(F32)
    mid = rest.astype(BF16)
    low = (rest - mid.astype(F32)).astype(BF16)
    pad = jnp.zeros((13,) + v.shape[1:], BF16)
    return jnp.concatenate([hi, mid, low, pad], axis=0)


class Gather:
    def __init__(self, panel, send, recv, here, parts=1):
        self.panel, self.send, self.recv, self.here = panel, send, recv, here
        self.parts = parts
        self.started = []

    def copy(self, kind, slot, target, part=None):
        where = self.panel.at[slot]
        if part is not None and self.parts > 1:
            size = POS // self.parts
            where = self.panel.at[slot, pl.ds(part * size, size)]
            kind = kind if part == 0 else 15 + (0, 3, 4, 6).index(kind)
        return pltpu.make_async_remote_copy(
            src_ref=where,
            dst_ref=where,
            send_sem=self.send.at[kind],
            recv_sem=self.recv.at[kind],
            device_id={"rep": self.here.rep, "filt": target},
            device_id_type=MESH,
        )

    def go(self, kind, slot, target, part=None):
        made = self.copy(kind, slot, target, part)
        made.start()
        self.started.append(made)

    def got(self, kind, slot, part=None):
        self.copy(kind, slot, self.here.sib, part).wait_recv()

    def own(self):
        for part in range(self.parts):
            self.go(0, self.here.me, self.here.opp, part)
        self.spread()

    def spread(self):
        h = self.here
        self.go(1, h.me, h.right)
        self.go(2, h.me, h.left)
        self.go(5, h.me, h.far)
        self.go(7, h.me, h.sib)

    def across(self):
        for part in range(self.parts):
            self.got(0, self.here.opp, part)
            self.spread_opp(part)
        self.go(8, self.here.opp, self.here.sib)

    def spread_opp(self, part):
        h = self.here
        self.go(3, h.opp, h.right, part)
        self.go(4, h.opp, h.left, part)
        self.go(6, h.opp, h.far, part)

    def near(self):
        h = self.here
        for kind, slot, onward in ((1, h.left, 9), (2, h.right, 10), (5, h.far, 13)):
            self.got(kind, slot)
            self.go(onward, slot, h.sib)

    def near_opp(self):
        h = self.here
        for kind, slot, onward in ((3, h.left_opp, 11), (4, h.right_opp, 12), (6, h.far_opp, 14)):
            for part in range(self.parts):
                self.got(kind, slot, part)
            self.go(onward, slot, h.sib)

    def plane(self):
        h = self.here
        self.got(7, h.sib)
        self.got(9, h.other(h.left))
        self.got(10, h.other(h.right))
        self.got(13, h.other(h.far))

    def plane_opp(self):
        h = self.here
        self.got(8, h.other(h.opp))
        self.got(11, h.other(h.left_opp))
        self.got(12, h.other(h.right_opp))
        self.got(14, h.other(h.far_opp))

    def drain(self):
        for made in self.started:
            made.wait_send()


class Here:
    def __init__(self):
        self.rep = lax.axis_index("rep")
        self.me = lax.axis_index("filt")
        self.z = self.me // 8
        self.y = (self.me % 8) // 2
        self.k = self.me % 2
        self.up = (self.y + 1) % 4
        self.down = (self.y + 3) % 4
        self.beyond = (self.y + 2) % 4
        self.sib = self.at(self.z, self.y, 1 - self.k)
        self.opp = self.at(1 - self.z, self.y, self.k)
        self.right = self.at(self.z, self.up, self.k)
        self.left = self.at(self.z, self.down, self.k)
        self.far = self.at(self.z, self.beyond, self.k)
        self.right_opp = self.at(1 - self.z, self.up, self.k)
        self.left_opp = self.at(1 - self.z, self.down, self.k)
        self.far_opp = self.at(1 - self.z, self.beyond, self.k)

    def at(self, z, y, k):
        return z * 8 + y * 2 + k

    def other(self, slot):
        return slot + 1 - 2 * (slot % 2)


def main_kernel(
    label, partner_h, x_h, w3s_h, w1s_h, hds_h, w3t_h, w1t_h, hdt_h,
    xeo, dpre_out, gw1_out, gh_out,
    partner, x, xraw, hc, w3s, w3t, wxs, wxt, w1raw, w1p, hds, hdt, xg, xgt, hg, hgt, accs, acct,
    a1, sb, ls, lt, ua, row, sendb, block, ra, rb, rc,
    wsem, gsend, grecv, asend, arecv, lsend, lrecv, rsend, rrecv,
):
    h = Here()
    rep, me = h.rep, h.me

    barrier = pltpu.get_barrier_semaphore()
    for i in range(1, N_REP):
        pl.semaphore_signal(
            barrier, inc=1, device_id={"rep": (rep + i) % N_REP, "filt": me}, device_id_type=MESH
        )
    for i in range(1, N_FILT):
        pl.semaphore_signal(
            barrier, inc=1, device_id={"rep": rep, "filt": (me + i) % N_FILT}, device_id_type=MESH
        )

    loads = [
        pltpu.make_async_copy(src, dst, wsem.at[i])
        for i, (src, dst) in enumerate(
            (
                (x_h, x),
                (partner_h, partner),
                (w3s_h, w3s),
                (w3t_h, w3t),
                (w1s_h, w1raw.at[0]),
                (w1t_h, w1raw.at[1]),
                (hds_h, hds),
                (hdt_h, hdt),
            )
        )
    ]
    for load in loads:
        load.start()

    lane_from = lax.broadcasted_iota(jnp.int32, (LOC, LANES), 0)
    lane_to = lax.broadcasted_iota(jnp.int32, (LOC, LANES), 1)
    inside = lane_to % 64
    perm = jnp.where((inside < HALF) & (lane_from == 2 * inside + lane_to // 64), 1.0, 0.0)
    perm = perm.astype(BF16)
    pl.semaphore_wait(barrier, N_REP - 1 + N_FILT - 1)

    gx = Gather(xg, gsend.at[0], grecv.at[0], h)
    gxt = Gather(xgt, gsend.at[1], grecv.at[1], h)
    gh = Gather(hg, gsend.at[2], grecv.at[2], h)
    ght = Gather(hgt, gsend.at[3], grecv.at[3], h, 2)

    for i in range(1, N_REP):
        q = (rep + i) % N_REP

        @pl.when((q % 2 == 0) & (q < 2 * CHUNKS))
        def _():
            pltpu.make_async_remote_copy(
                src_ref=x_h.at[pl.ds(pl.multiple_of(q // 2 * RELAY, RELAY), RELAY)],
                dst_ref=a1.at[rep],
                send_sem=asend.at[0],
                recv_sem=arecv.at[0],
                device_id={"rep": q, "filt": me},
                device_id_type=MESH,
            ).start()

    loads[0].wait()
    xg[me] = mm(x[...], perm).astype(BF16)
    gx.own()
    loads[1].wait()

    def ordered(w3, wx, first, last):
        keep = lax.broadcasted_iota(jnp.int32, (64, LOC), 0) < HALF
        even = lax.broadcasted_iota(jnp.int32, (64, LOC), 1) % 2 == 0

        def body(t, carry):
            where = pl.ds(pl.multiple_of(t * LANES, LANES), LOC)
            w = jnp.concatenate([w3[t].astype(F32), jnp.zeros((8, LOC), F32)], axis=0)
            for f in range(N_FILT):
                piece = w[f * HALF : f * HALF + 64]
                wx[f * LANES : f * LANES + 64, where] = jnp.where(
                    keep & even, piece, 0.0
                ).astype(BF16)
                wx[f * LANES + 64 : (f + 1) * LANES, where] = jnp.where(
                    keep & ~even, piece, 0.0
                ).astype(BF16)
            return carry

        lax.fori_loop(first, last, body, 0)

    relay = (rep % 2 == 0) & (rep < 2 * CHUNKS)
    chunk = pl.ds(pl.multiple_of(rep % (2 * CHUNKS) // 2 * RELAY, RELAY), RELAY)
    loads[2].wait()
    ordered(w3s, wxs, 0, 4)

    @pl.when(relay)
    def _():
        pltpu.make_async_copy(a1.at[pl.ds(0, 15)], a1.at[pl.ds(0, 15)], arecv.at[0]).wait()
        a1[rep] = x[chunk]
        xraw[0, chunk] = a1[partner[rep]]
        for i in range(N_REP):
            p = (rep + i) % N_REP
            sb[i] = a1[partner[p]]
            for plane, target in enumerate((h.opp, me)):
                if i > 0 or plane == 0:
                    pltpu.make_async_remote_copy(
                        src_ref=sb.at[i],
                        dst_ref=xraw.at[1 - plane, chunk],
                        send_sem=asend.at[1 + 2 * plane],
                        recv_sem=arecv.at[1 + 2 * plane],
                        device_id={"rep": p, "filt": target},
                        device_id_type=MESH,
                    ).start()

    gx.near()
    ordered(w3s, wxs, 4, 8)
    gx.across()
    ordered(w3s, wxs, 8, 9)
    loads[3].wait()
    ordered(w3t, wxt, 0, 2)

    @pl.when(relay)
    def _():
        pltpu.make_async_copy(
            xraw.at[0, pl.ds(0, RELAY * (CHUNKS - 1))],
            xraw.at[0, pl.ds(0, RELAY * (CHUNKS - 1))],
            arecv.at[3],
        ).wait()

    @pl.when(jnp.logical_not(relay))
    def _():
        pltpu.make_async_copy(xraw.at[0], xraw.at[0], arecv.at[3]).wait()

    xgt[me] = mm(xraw[0], perm).astype(BF16)
    gxt.spread()
    pltpu.make_async_copy(xraw.at[1], xraw.at[1], arecv.at[1]).wait()
    xgt[h.opp] = mm(xraw[1], perm).astype(BF16)
    gxt.spread_opp(0)
    gxt.go(8, h.opp, h.sib)
    ordered(w3t, wxt, 2, 5)

    def conv_half(panel, wx, acc, z, first):
        rows = pl.ds(pl.multiple_of(z * (8 * LANES), 8 * LANES), 8 * LANES)
        left = jnp.concatenate([panel[z * 8 + i] for i in range(8)], axis=1)
        for i in range(3):
            where = slice(i * 3 * LANES, (i + 1) * 3 * LANES)
            part = mm(left, wx[rows, where])
            acc[:, where] = part if first else acc[:, where] + part

    lanes = lax.broadcasted_iota(jnp.int32, (POS, LANES), 1)
    column = lax.broadcasted_iota(jnp.int32, (POS, LANES), 0) % MAP_W

    def conv_end(acc):
        total = None
        top = jnp.zeros((MAP_W, LANES), F32)

        def tap(t, low, high):
            return acc[low:high, t * LANES : (t + 1) * LANES]

        for b in range(3):
            part = tap(3 + b, 0, POS)
            part = part + jnp.concatenate([top, tap(b, 0, POS - MAP_W)], axis=0)
            part = part + jnp.concatenate([tap(6 + b, MAP_W, POS), top], axis=0)
            if b == 0:
                part = jnp.where(column >= 1, pltpu.roll(part, 1, 0), 0.0)
            if b == 2:
                part = jnp.where(column <= MAP_W - 2, pltpu.roll(part, POS - 1, 0), 0.0)
            total = part if total is None else total + part
        return total

    def hidden_of(pre):
        return jnp.where(lanes < LOC, silu(pre), 0.0).astype(BF16)

    gx.plane()
    conv_half(xg, wxs, accs, h.z, True)
    gxt.near()
    gx.near_opp()
    ordered(w3t, wxt, 5, 9)
    gx.plane_opp()
    conv_half(xg, wxs, accs, 1 - h.z, False)
    gxt.near_opp()
    pre = conv_end(accs)
    hg[me] = hidden_of(pre)
    gh.own()
    gxt.plane()
    conv_half(xgt, wxt, acct, h.z, True)
    gxt.plane_opp()
    conv_half(xgt, wxt, acct, 1 - h.z, False)
    hgt[me] = hidden_of(conv_end(acct))
    ght.own()
    gh.near()
    gh.across()

    for which in range(2):
        loads[4 + which].wait()
        for f in range(N_FILT):
            w1p[which, f * LANES : f * LANES + LOC, :] = w1raw[which, f * LOC : (f + 1) * LOC, :]
            w1p[which, f * LANES + LOC : (f + 1) * LANES, :] = jnp.zeros((LANES - LOC, LOC), BF16)

    gh.near_opp()
    ght.near()
    ght.across()
    gh.plane()
    gh.plane_opp()
    ght.near_opp()

    def whole(panel):
        return jnp.concatenate([panel[i] for i in range(N_FILT)], axis=1)

    def logits_of(z, head):
        pooled = jnp.sum(silu(z), axis=0, keepdims=True) * (1.0 / POS)
        parts = mm(split3(pooled), head[...], ((1,), (1,)))
        row[...] = jnp.zeros((1, 1024), F32)
        row[:, :K] = parts[0:1] + parts[1:2] + parts[2:3]
        full = row[...]
        return pooled, jnp.concatenate(
            [full[:, i * LANES : (i + 1) * LANES] for i in range(8)], axis=0
        )

    def give_logits(buf, part, idx):
        buf[me] = part
        for i in (8, 7, 9, 6, 10, 5, 11, 4, 12, 3, 13, 2, 14, 1, 15):
            pltpu.make_async_remote_copy(
                src_ref=buf.at[me],
                dst_ref=buf.at[me],
                send_sem=lsend.at[idx],
                recv_sem=lrecv.at[idx],
                device_id={"rep": rep, "filt": (me + i) % N_FILT},
                device_id_type=MESH,
            ).start()

    def wait_bytes(buf, count, sem):
        pltpu.make_async_copy(buf.at[pl.ds(0, count)], buf.at[pl.ds(0, count)], sem).wait()

    def sum_logits(buf, idx):
        wait_bytes(buf, N_FILT - 1, lrecv.at[idx])
        return jnp.sum(buf[...], axis=0)

    loads[6].wait()
    loads[7].wait()
    z_mixed = x[...].astype(F32) + mm(whole(hg), w1p[0])
    pooled, part = logits_of(z_mixed, hds)
    give_logits(ls, part, 0)
    xt = xraw[0].astype(F32)
    ght.plane()
    ght.plane_opp()
    part = logits_of(xt + mm(whole(hgt), w1p[1]), hdt)[1]
    give_logits(lt, part, 1)
    for f in range(N_FILT):
        hc[:, f * LOC : (f + 1) * LOC] = hg[f, :, :LOC]
    logits = sum_logits(ls, 0)

    cls = lax.broadcasted_iota(jnp.int32, (8, LANES), 0) * LANES + lax.broadcasted_iota(
        jnp.int32, (8, LANES), 1
    )
    real = cls < K

    def softmax(v):
        top = jnp.max(jnp.where(real, v, -jnp.inf))
        e = jnp.where(real, jnp.exp(v - top), 0.0)
        return e / jnp.sum(e)

    own_part = 2.0 * softmax(logits) - jnp.where(cls == label[0], 1.0, 0.0)
    slope = dsilu(z_mixed) * (1.0 / POS)
    ua[rep] = sum_logits(lt, 1)
    for i in range(1, N_REP):
        pltpu.make_async_remote_copy(
            src_ref=ua.at[rep],
            dst_ref=ua.at[rep],
            send_sem=asend.at[2],
            recv_sem=arecv.at[2],
            device_id={"rep": (rep + i) % N_REP, "filt": me},
            device_id_type=MESH,
        ).start()
    for f in range(N_FILT):
        for g in range(2):
            xeo[g * POS : (g + 1) * POS, f * HALF : (f + 1) * HALF] = xg[
                f, :, 64 * g : 64 * g + HALF
            ]
    wait_bytes(ua, N_REP - 1, arecv.at[2])
    dl = own_part - softmax(ua[partner[rep]])
    dl_row = jnp.concatenate([dl[i : i + 1, :] for i in range(8)], axis=1)[:, :K]
    parts = mm(split3(dl_row), hds[...])
    dz = ((parts[0:1] + parts[1:2] + parts[2:3]) * slope).astype(BF16)

    def remote(src, dst, kind, target):
        return pltpu.make_async_remote_copy(
            src_ref=src,
            dst_ref=dst,
            send_sem=rsend.at[kind],
            recv_sem=rrecv.at[kind],
            device_id={"rep": rep, "filt": target},
            device_id_type=MESH,
        )

    zz = 1 - h.z
    mine_at = pl.ds(pl.multiple_of(h.k * LANES, LANES), LANES)
    other_at = pl.ds(pl.multiple_of((1 - h.k) * LANES, LANES), LANES)
    places = (h.beyond, h.up, h.down, h.y)
    sib_copies = []
    for i, z in enumerate((zz, h.z)):
        rows = pl.ds(pl.multiple_of(z * 8 * LANES, 8 * LANES), 8 * LANES)
        part = mm(dz, w1p[0, rows, :], ((1,), (1,)))
        for y in range(4):
            block[i * 4 + y] = part[:, y * 2 * LANES : (y + 1) * 2 * LANES]
        for j, y in enumerate(places):
            sendb[i * 4 + j] = block[i * 4 + y, :, other_at].astype(BF16)
            made = remote(sendb.at[i * 4 + j], ra.at[i * 4 + j], i * 4 + j, h.sib)
            made.start()
            sib_copies.append(made)

    mid = POS // 2
    halves = (slice(0, mid), slice(mid, POS))

    def chip_sum(i, j, rows):
        return block[i * 4 + places[j], rows, mine_at] + ra[i * 4 + j, rows].astype(F32)

    side = [h.at(h.z, y, h.k) for y in places[:3]]
    across = []
    for half, rows in enumerate(halves):
        for j in range(3):
            if half == 0:
                sib_copies[j].wait_recv()
            sendb[8 + j, rows] = chip_sum(0, j, rows).astype(BF16)
            made = remote(sendb.at[8 + j, rows], rb.at[j, rows], 8 + half * 3 + j, side[j])
            made.start()
            across.append(made)
    for j in range(3):
        sib_copies[4 + j].wait_recv()
        sendb[11 + j] = chip_sum(1, j, slice(0, POS)).astype(BF16)
        made = remote(sendb.at[11 + j], rb.at[3 + j], 14 + j, side[j])
        made.start()
        across.append(made)
    sib_copies[3].wait_recv()
    last = []
    for half, rows in enumerate(halves):
        total = chip_sum(0, 3, rows)
        for j in (1, 2, 0):
            across[half * 3 + j].wait_recv()
            total = total + rb[j, rows].astype(F32)
        sendb[14, rows] = total.astype(BF16)
        made = remote(sendb.at[14, rows], rc.at[rows], 17 + half, h.opp)
        made.start()
        last.append(made)
    sib_copies[7].wait_recv()
    mine = chip_sum(1, 3, slice(0, POS))
    for j in (1, 2, 0):
        across[6 + j].wait_recv()
        mine = mine + rb[3 + j].astype(F32)
    gw1_out[...] = mm(dz, hc[...], ((0,), (0,)))
    flip = dl.T
    for i in range(8):
        size = min(LANES, K - i * LANES)
        gh_out[i * LANES : i * LANES + size, :] = flip[:size, i : i + 1] * pooled
    slope = dsilu(pre)
    for made in last:
        made.wait_recv()
    dhidden = mine + rc[...].astype(F32)
    dpre_out[...] = (dhidden * slope)[:, :LOC].astype(BF16)

    for gather in (gx, gxt, gh, ght):
        gather.drain()
    for made in sib_copies + across + last:
        made.wait_send()
    wait_bytes(ls, N_FILT - 1, lsend.at[0])
    wait_bytes(lt, N_FILT - 1, lsend.at[1])
    wait_bytes(ua, N_REP - 1, asend.at[2])

    @pl.when(relay)
    def _():
        wait_bytes(sb, CHUNKS - 1, asend.at[0])
        wait_bytes(sb, N_REP, asend.at[1])
        wait_bytes(sb, N_REP - 1, asend.at[3])

    @pl.when(jnp.logical_not(relay))
    def _():
        wait_bytes(sb, CHUNKS, asend.at[0])


def grads_kernel(xeo, dpre, r1, r0, gw3, gw1, gh, turned, r3, sem):
    copies = []

    def out(src, dst, i):
        made = pltpu.make_async_copy(src, dst, sem.at[i])
        made.start()
        copies.append(made)

    out(r1, gw1.at[:, 0, :], 9)
    out(r0, gh, 10)
    dp = dpre[...].astype(F32)
    even = lax.broadcasted_iota(jnp.int32, (POS, LOC), 1) % 2 == 0
    column = lax.broadcasted_iota(jnp.int32, (POS, LOC), 0) % MAP_W
    zero = jnp.zeros((MAP_W, LOC), F32)
    for b in range(3):
        moved = dp
        if b == 0:
            moved = pltpu.roll(jnp.where(column >= 1, dp, 0.0), POS - 1, 0)
        if b == 2:
            moved = pltpu.roll(jnp.where(column <= MAP_W - 2, dp, 0.0), 1, 0)
        for a in range(3):
            d = moved
            if a == 0:
                d = jnp.concatenate([moved[MAP_W:], zero], axis=0)
            if a == 2:
                d = jnp.concatenate([zero, moved[: POS - MAP_W]], axis=0)
            where = slice(a * LANES, a * LANES + LOC)
            turned[b, :POS, where] = jnp.where(even, d, 0.0).astype(BF16)
            turned[b, POS:, where] = jnp.where(even, 0.0, d).astype(BF16)
    for b in range(3):
        rows = mm(turned[b], xeo[...], ((0,), (0,)))
        for a in range(3):
            t = 3 * a + b
            r3[t] = rows[a * LANES : a * LANES + LOC]
            out(r3.at[t], gw3.at[:, t, 0, :], t)
    for made in copies:
        made.wait()


def per_device(
    images, labels, partner, student_w3, student_w1, student_head, stale_w3, stale_w1, stale_head
):
    vmem = pl.BlockSpec(memory_space=pltpu.VMEM)
    hbm = pl.BlockSpec(memory_space=pltpu.HBM)
    sds = jax.ShapeDtypeStruct
    dma = pltpu.SemaphoreType.DMA
    weights = []
    for w3, w1, head in (
        (student_w3, student_w1, student_head),
        (stale_w3, stale_w1, stale_head),
    ):
        weights += [w3[0].transpose(1, 2, 0), w1[0].T, head[0].T]
    saved = pl.pallas_call(
        main_kernel,
        out_shape=(
            pltpu.VMEM((2 * POS, GW), BF16),
            pltpu.VMEM((POS, LOC), BF16),
            pltpu.VMEM((LOC, C), F32),
            pltpu.VMEM((K, LOC), F32),
        ),
        in_specs=[pl.BlockSpec(memory_space=pltpu.SMEM)] + [hbm] * 8,
        out_specs=[vmem] * 4,
        scratch_shapes=[
            pltpu.SMEM((N_REP,), jnp.int32),
            pltpu.VMEM((POS, LOC), BF16),
            pltpu.VMEM((2, POS, LOC), BF16),
            pltpu.VMEM((POS, C), BF16),
            pltpu.VMEM((9, GW, LOC), BF16),
            pltpu.VMEM((9, GW, LOC), BF16),
            pltpu.VMEM((N_FILT * LANES, 9 * LANES), BF16),
            pltpu.VMEM((N_FILT * LANES, 9 * LANES), BF16),
            pltpu.VMEM((2, C, LOC), BF16),
            pltpu.VMEM((2, N_FILT * LANES, LOC), BF16),
            pltpu.VMEM((K, LOC), BF16),
            pltpu.VMEM((K, LOC), BF16),
            pltpu.VMEM((N_FILT, POS, LANES), BF16),
            pltpu.VMEM((N_FILT, POS, LANES), BF16),
            pltpu.VMEM((N_FILT, POS, LANES), BF16),
            pltpu.VMEM((N_FILT, POS, LANES), BF16),
            pltpu.VMEM((POS, 9 * LANES), F32),
            pltpu.VMEM((POS, 9 * LANES), F32),
            pltpu.VMEM((N_REP, RELAY, LOC), BF16),
            pltpu.VMEM((N_REP, RELAY, LOC), BF16),
            pltpu.VMEM((N_FILT, 8, LANES), F32),
            pltpu.VMEM((N_FILT, 8, LANES), F32),
            pltpu.VMEM((N_REP, 8, LANES), F32),
            pltpu.VMEM((1, 1024), F32),
            pltpu.VMEM((15, POS, LANES), BF16),
            pltpu.VMEM((8, POS, 2 * LANES), F32),
            pltpu.VMEM((8, POS, LANES), BF16),
            pltpu.VMEM((6, POS, LANES), BF16),
            pltpu.VMEM((POS, LANES), BF16),
            dma((8,)),
            dma((4, 19)),
            dma((4, 19)),
            dma((4,)),
            dma((4,)),
            dma((2,)),
            dma((2,)),
            dma((19,)),
            dma((19,)),
        ],
        compiler_params=pltpu.CompilerParams(
            collective_id=0, has_side_effects=True, vmem_limit_bytes=48 * 1024 * 1024
        ),
        name="step",
    )(
        labels,
        *(
            pltpu.with_memory_space_constraint(a, pltpu.HBM)
            for a in (partner, images.transpose(1, 2, 0)[0], *weights)
        ),
    )
    gw3, gw1, gh = pl.pallas_call(
        grads_kernel,
        out_shape=(
            sds((LOC, 9, 1, GW), F32),
            sds((LOC, 1, C), F32),
            sds((K, LOC), F32),
        ),
        in_specs=[vmem] * 4,
        out_specs=[hbm] * 3,
        scratch_shapes=[
            pltpu.VMEM((3, 2 * POS, 3 * LANES), BF16),
            pltpu.VMEM((9, LOC, GW), F32),
            dma((11,)),
        ],
        compiler_params=pltpu.CompilerParams(vmem_limit_bytes=40 * 1024 * 1024),
        name="grads",
    )(*saved)
    return (gw3.transpose(2, 0, 1, 3), gw1.transpose(1, 0, 2), gh.T[None])


def solution(mesh):
    in_specs = (
        P("filt", "rep", None),
        P("rep"),
        P(),
        P("rep", "filt", None, None),
        P("rep", "filt", None),
        P("rep", "filt", None),
        P("rep", "filt", None, None),
        P("rep", "filt", None),
        P("rep", "filt", None),
    )
    out_specs = (P("rep", "filt", None, None), P("rep", "filt", None), P("rep", "filt", None))
    return jax.shard_map(
        per_device, mesh=mesh, in_specs=in_specs, out_specs=out_specs, check_vma=False
    )
```

```python
import functools

import jax
import jax.numpy as jnp
from jax import lax
from jax.experimental import pallas as pl
from jax.experimental.pallas import tpu as pltpu
from jax.sharding import PartitionSpec as P

C = 2016
GW = 1008
K = 1000
ROWS = 4
MAP_W = 56
POS = ROWS * MAP_W
N_REP = 16
N_FILT = 16
LOC = C // N_FILT
HALF = LOC // 2
RELAY = 32
CHUNKS = POS // RELAY
LANES = 128
F32 = jnp.float32
BF16 = jnp.bfloat16
MESH = pl.DeviceIdType.MESH


def mm(a, b, dims=((1,), (0,))):
    return lax.dot_general(a, b, (dims, ((), ())), preferred_element_type=F32)


def silu(v):
    return v / (1.0 + jnp.exp(-v))


def dsilu(v):
    sig = 1.0 / (1.0 + jnp.exp(-v))
    return sig * (1.0 + v * (1.0 - sig))


def split3(v):
    hi = v.astype(BF16)
    rest = v - hi.astype(F32)
    mid = rest.astype(BF16)
    low = (rest - mid.astype(F32)).astype(BF16)
    pad = jnp.zeros((13,) + v.shape[1:], BF16)
    return jnp.concatenate([hi, mid, low, pad], axis=0)


class Gather:
    def __init__(self, panel, send, recv, here, parts=1, ring=False):
        self.panel, self.send, self.recv, self.here = panel, send, recv, here
        self.parts = parts
        self.ring = ring
        self.started = []

    def copy(self, kind, slot, target, part=None):
        where = self.panel.at[slot]
        if part is not None and self.parts > 1:
            size = POS // self.parts
            where = self.panel.at[slot, pl.ds(part * size, size)]
            kind = kind if part == 0 else 15 + (0, 3, 4, 6).index(kind)
        return pltpu.make_async_remote_copy(
            src_ref=where,
            dst_ref=where,
            send_sem=self.send.at[kind],
            recv_sem=self.recv.at[kind],
            device_id={"rep": self.here.rep, "filt": target},
            device_id_type=MESH,
        )

    def go(self, kind, slot, target, part=None):
        made = self.copy(kind, slot, target, part)
        made.start()
        self.started.append(made)

    def got(self, kind, slot, part=None):
        self.copy(kind, slot, self.here.sib, part).wait_recv()

    def own(self):
        for part in range(self.parts):
            self.go(0, self.here.me, self.here.opp, part)
        self.spread()

    def spread(self):
        h = self.here
        self.go(1, h.me, h.right)
        self.go(2, h.me, h.left)
        self.go(7, h.me, h.sib)

    def across(self):
        for part in range(self.parts):
            self.got(0, self.here.opp, part)
            self.spread_opp(part)
        self.go(8, self.here.opp, self.here.sib)

    def spread_opp(self, part):
        h = self.here
        self.go(3, h.opp, h.right, part)
        self.go(4, h.opp, h.left, part)
        if not self.ring:
            self.go(6, h.opp, h.far, part)

    def near(self):
        h = self.here
        self.got(2, h.right)
        self.go(5, h.right, h.left)
        self.go(10, h.right, h.sib)
        self.got(1, h.left)
        self.go(9, h.left, h.sib)

    def far(self):
        self.got(5, self.here.far)
        self.go(13, self.here.far, self.here.sib)

    def near_opp(self):
        h = self.here
        for part in range(self.parts):
            self.got(3, h.left_opp, part)
        if self.ring:
            self.go(6, h.left_opp, h.right)
        self.go(11, h.left_opp, h.sib)
        for part in range(self.parts):
            self.got(4, h.right_opp, part)
        self.go(12, h.right_opp, h.sib)

    def far_opp(self):
        for part in range(self.parts):
            self.got(6, self.here.far_opp, part)
        self.go(14, self.here.far_opp, self.here.sib)

    def plane(self):
        h = self.here
        self.got(7, h.sib)
        self.got(9, h.other(h.left))
        self.got(10, h.other(h.right))
        self.got(13, h.other(h.far))

    def plane_opp(self):
        h = self.here
        self.got(8, h.other(h.opp))
        self.got(11, h.other(h.left_opp))
        self.got(12, h.other(h.right_opp))
        self.got(14, h.other(h.far_opp))

    def drain(self):
        for made in self.started:
            made.wait_send()


class Here:
    def __init__(self):
        self.rep = lax.axis_index("rep")
        self.me = lax.axis_index("filt")
        self.z = self.me // 8
        self.y = (self.me % 8) // 2
        self.k = self.me % 2
        self.up = (self.y + 1) % 4
        self.down = (self.y + 3) % 4
        self.beyond = (self.y + 2) % 4
        self.sib = self.at(self.z, self.y, 1 - self.k)
        self.opp = self.at(1 - self.z, self.y, self.k)
        self.right = self.at(self.z, self.up, self.k)
        self.left = self.at(self.z, self.down, self.k)
        self.far = self.at(self.z, self.beyond, self.k)
        self.right_opp = self.at(1 - self.z, self.up, self.k)
        self.left_opp = self.at(1 - self.z, self.down, self.k)
        self.far_opp = self.at(1 - self.z, self.beyond, self.k)

    def at(self, z, y, k):
        return z * 8 + y * 2 + k

    def other(self, slot):
        return slot + 1 - 2 * (slot % 2)


def main_kernel(
    label, partner_h, x_h, w3s_h, w1s_h, hds_h, w3t_h, w1t_h, hdt_h,
    xeo, dpre_out, gw1_out, gh_out,
    partner, x, xraw, hc, w3s, w3t, wxs, wxt, w1raw, w1p, hds, hdt, xg, xgt, hg, hgt, accs, acct,
    a1, sb, ls, lt, ua, row, sendb, block, ra, rb, rc,
    wsem, gsend, grecv, asend, arecv, lsend, lrecv, rsend, rrecv,
):
    h = Here()
    rep, me = h.rep, h.me

    barrier = pltpu.get_barrier_semaphore()
    for i in range(1, N_REP):
        pl.semaphore_signal(
            barrier, inc=1, device_id={"rep": (rep + i) % N_REP, "filt": me}, device_id_type=MESH
        )
    for i in range(1, N_FILT):
        pl.semaphore_signal(
            barrier, inc=1, device_id={"rep": rep, "filt": (me + i) % N_FILT}, device_id_type=MESH
        )

    loads = [
        pltpu.make_async_copy(src, dst, wsem.at[i])
        for i, (src, dst) in enumerate(
            (
                (x_h, x),
                (partner_h, partner),
                (w3s_h, w3s),
                (w3t_h, w3t),
                (w1s_h, w1raw.at[0]),
                (w1t_h, w1raw.at[1]),
                (hds_h, hds),
                (hdt_h, hdt),
            )
        )
    ]
    for load in loads:
        load.start()

    lane_from = lax.broadcasted_iota(jnp.int32, (LOC, LANES), 0)
    lane_to = lax.broadcasted_iota(jnp.int32, (LOC, LANES), 1)
    inside = lane_to % 64
    perm = jnp.where((inside < HALF) & (lane_from == 2 * inside + lane_to // 64), 1.0, 0.0)
    perm = perm.astype(BF16)
    pl.semaphore_wait(barrier, N_REP - 1 + N_FILT - 1)

    gx = Gather(xg, gsend.at[0], grecv.at[0], h, ring=True)
    gxt = Gather(xgt, gsend.at[1], grecv.at[1], h)
    gh = Gather(hg, gsend.at[2], grecv.at[2], h, ring=True)
    ght = Gather(hgt, gsend.at[3], grecv.at[3], h, 2)

    for i in range(1, N_REP):
        q = (rep + i) % N_REP

        @pl.when((q % 2 == 0) & (q < 2 * CHUNKS))
        def _():
            pltpu.make_async_remote_copy(
                src_ref=x_h.at[pl.ds(pl.multiple_of(q // 2 * RELAY, RELAY), RELAY)],
                dst_ref=a1.at[rep],
                send_sem=asend.at[0],
                recv_sem=arecv.at[0],
                device_id={"rep": q, "filt": me},
                device_id_type=MESH,
            ).start()

    loads[0].wait()
    xg[me] = mm(x[...], perm).astype(BF16)
    gx.own()
    loads[1].wait()

    def ordered(w3, wx, first, last):
        keep = lax.broadcasted_iota(jnp.int32, (64, LOC), 0) < HALF
        even = lax.broadcasted_iota(jnp.int32, (64, LOC), 1) % 2 == 0

        def body(t, carry):
            where = pl.ds(pl.multiple_of(t * LANES, LANES), LOC)
            w = jnp.concatenate([w3[t].astype(F32), jnp.zeros((8, LOC), F32)], axis=0)
            for f in range(N_FILT):
                piece = w[f * HALF : f * HALF + 64]
                wx[f * LANES : f * LANES + 64, where] = jnp.where(
                    keep & even, piece, 0.0
                ).astype(BF16)
                wx[f * LANES + 64 : (f + 1) * LANES, where] = jnp.where(
                    keep & ~even, piece, 0.0
                ).astype(BF16)
            return carry

        lax.fori_loop(first, last, body, 0)

    relay = (rep % 2 == 0) & (rep < 2 * CHUNKS)
    chunk = pl.ds(pl.multiple_of(rep % (2 * CHUNKS) // 2 * RELAY, RELAY), RELAY)
    loads[2].wait()
    ordered(w3s, wxs, 0, 4)

    @pl.when(relay)
    def _():
        pltpu.make_async_copy(a1.at[pl.ds(0, 15)], a1.at[pl.ds(0, 15)], arecv.at[0]).wait()
        a1[rep] = x[chunk]
        xraw[0, chunk] = a1[partner[rep]]
        for i in range(N_REP):
            p = (rep + i) % N_REP
            sb[i] = a1[partner[p]]
            for plane, target in enumerate((h.opp, me)):
                if i > 0 or plane == 0:
                    pltpu.make_async_remote_copy(
                        src_ref=sb.at[i],
                        dst_ref=xraw.at[1 - plane, chunk],
                        send_sem=asend.at[1 + 2 * plane],
                        recv_sem=arecv.at[1 + 2 * plane],
                        device_id={"rep": p, "filt": target},
                        device_id_type=MESH,
                    ).start()

    gx.near()
    ordered(w3s, wxs, 4, 8)
    gx.across()
    ordered(w3s, wxs, 8, 9)
    gx.far()
    loads[3].wait()
    ordered(w3t, wxt, 0, 2)

    @pl.when(relay)
    def _():
        pltpu.make_async_copy(
            xraw.at[0, pl.ds(0, RELAY * (CHUNKS - 1))],
            xraw.at[0, pl.ds(0, RELAY * (CHUNKS - 1))],
            arecv.at[3],
        ).wait()

    @pl.when(jnp.logical_not(relay))
    def _():
        pltpu.make_async_copy(xraw.at[0], xraw.at[0], arecv.at[3]).wait()

    xgt[me] = mm(xraw[0], perm).astype(BF16)
    gxt.spread()
    pltpu.make_async_copy(xraw.at[1], xraw.at[1], arecv.at[1]).wait()
    xgt[h.opp] = mm(xraw[1], perm).astype(BF16)
    gxt.spread_opp(0)
    gxt.go(8, h.opp, h.sib)
    ordered(w3t, wxt, 2, 5)

    def conv_half(panel, wx, acc, z, first):
        rows = pl.ds(pl.multiple_of(z * (8 * LANES), 8 * LANES), 8 * LANES)
        left = jnp.concatenate([panel[z * 8 + i] for i in range(8)], axis=1)

        def body(where):
            part = mm(left, wx[rows, where])
            acc[:, where] = part if first else acc[:, where] + part

        def step(i, carry):
            body(pl.ds(pl.multiple_of(i * 4 * LANES, 4 * LANES), 4 * LANES))
            return carry

        lax.fori_loop(0, 2, step, 0)
        body(slice(8 * LANES, 9 * LANES))

    lanes = lax.broadcasted_iota(jnp.int32, (POS, LANES), 1)
    column = lax.broadcasted_iota(jnp.int32, (POS, LANES), 0) % MAP_W

    def conv_end(acc):
        total = None
        top = jnp.zeros((MAP_W, LANES), F32)

        def tap(t, low, high):
            return acc[low:high, t * LANES : (t + 1) * LANES]

        for b in range(3):
            part = tap(3 + b, 0, POS)
            part = part + jnp.concatenate([top, tap(b, 0, POS - MAP_W)], axis=0)
            part = part + jnp.concatenate([tap(6 + b, MAP_W, POS), top], axis=0)
            if b == 0:
                part = jnp.where(column >= 1, pltpu.roll(part, 1, 0), 0.0)
            if b == 2:
                part = jnp.where(column <= MAP_W - 2, pltpu.roll(part, POS - 1, 0), 0.0)
            total = part if total is None else total + part
        return total

    def hidden_of(pre):
        return jnp.where(lanes < LOC, silu(pre), 0.0).astype(BF16)

    gx.plane()
    conv_half(xg, wxs, accs, h.z, True)
    gxt.near()
    gx.near_opp()
    ordered(w3t, wxt, 5, 9)
    gxt.far()
    gx.far_opp()
    gx.plane_opp()
    conv_half(xg, wxs, accs, 1 - h.z, False)
    gxt.near_opp()
    gxt.far_opp()
    pre = conv_end(accs)
    hg[me] = hidden_of(pre)
    gh.own()
    gxt.plane()
    conv_half(xgt, wxt, acct, h.z, True)
    gxt.plane_opp()
    conv_half(xgt, wxt, acct, 1 - h.z, False)
    hgt[me] = hidden_of(conv_end(acct))
    ght.own()
    gh.near()

    for which in range(2):
        loads[4 + which].wait()
        for f in range(N_FILT):
            w1p[which, f * LANES : f * LANES + LOC, :] = w1raw[which, f * LOC : (f + 1) * LOC, :]
            w1p[which, f * LANES + LOC : (f + 1) * LANES, :] = jnp.zeros((LANES - LOC, LOC), BF16)

    gh.across()
    ght.near()
    gh.far()
    ght.far()
    ght.across()
    gh.near_opp()
    gh.far_opp()
    ght.near_opp()
    ght.far_opp()
    gh.plane()
    gh.plane_opp()

    def whole(panel):
        return jnp.concatenate([panel[i] for i in range(N_FILT)], axis=1)

    def logits_of(z, head):
        pooled = jnp.sum(silu(z), axis=0, keepdims=True) * (1.0 / POS)
        parts = mm(split3(pooled), head[...], ((1,), (1,)))
        row[...] = jnp.zeros((1, 1024), F32)
        row[:, :K] = parts[0:1] + parts[1:2] + parts[2:3]
        full = row[...]
        return pooled, jnp.concatenate(
            [full[:, i * LANES : (i + 1) * LANES] for i in range(8)], axis=0
        )

    def give_logits(buf, part, idx):
        buf[me] = part
        for i in (8, 7, 9, 6, 10, 5, 11, 4, 12, 3, 13, 2, 14, 1, 15):
            pltpu.make_async_remote_copy(
                src_ref=buf.at[me],
                dst_ref=buf.at[me],
                send_sem=lsend.at[idx],
                recv_sem=lrecv.at[idx],
                device_id={"rep": rep, "filt": (me + i) % N_FILT},
                device_id_type=MESH,
            ).start()

    def wait_bytes(buf, count, sem):
        pltpu.make_async_copy(buf.at[pl.ds(0, count)], buf.at[pl.ds(0, count)], sem).wait()

    def sum_logits(buf, idx):
        wait_bytes(buf, N_FILT - 1, lrecv.at[idx])
        return jnp.sum(buf[...], axis=0)

    loads[6].wait()
    loads[7].wait()
    z_mixed = x[...].astype(F32) + mm(whole(hg), w1p[0])
    pooled, part = logits_of(z_mixed, hds)
    give_logits(ls, part, 0)
    xt = xraw[0].astype(F32)
    ght.plane()
    ght.plane_opp()
    part = logits_of(xt + mm(whole(hgt), w1p[1]), hdt)[1]
    give_logits(lt, part, 1)
    for f in range(N_FILT):
        hc[:, f * LOC : (f + 1) * LOC] = hg[f, :, :LOC]
    logits = sum_logits(ls, 0)

    cls = lax.broadcasted_iota(jnp.int32, (8, LANES), 0) * LANES + lax.broadcasted_iota(
        jnp.int32, (8, LANES), 1
    )
    real = cls < K

    def softmax(v):
        top = jnp.max(jnp.where(real, v, -jnp.inf))
        e = jnp.where(real, jnp.exp(v - top), 0.0)
        return e / jnp.sum(e)

    own_part = 2.0 * softmax(logits) - jnp.where(cls == label[0], 1.0, 0.0)
    slope = dsilu(z_mixed) * (1.0 / POS)
    ua[rep] = sum_logits(lt, 1)
    for i in range(1, N_REP):
        pltpu.make_async_remote_copy(
            src_ref=ua.at[rep],
            dst_ref=ua.at[rep],
            send_sem=asend.at[2],
            recv_sem=arecv.at[2],
            device_id={"rep": (rep + i) % N_REP, "filt": me},
            device_id_type=MESH,
        ).start()
    for f in range(N_FILT):
        for g in range(2):
            xeo[g * POS : (g + 1) * POS, f * HALF : (f + 1) * HALF] = xg[
                f, :, 64 * g : 64 * g + HALF
            ]
    wait_bytes(ua, N_REP - 1, arecv.at[2])
    dl = own_part - softmax(ua[partner[rep]])
    dl_row = jnp.concatenate([dl[i : i + 1, :] for i in range(8)], axis=1)[:, :K]
    parts = mm(split3(dl_row), hds[...])
    dz = ((parts[0:1] + parts[1:2] + parts[2:3]) * slope).astype(BF16)

    def remote(src, dst, kind, target):
        return pltpu.make_async_remote_copy(
            src_ref=src,
            dst_ref=dst,
            send_sem=rsend.at[kind],
            recv_sem=rrecv.at[kind],
            device_id={"rep": rep, "filt": target},
            device_id_type=MESH,
        )

    zz = 1 - h.z
    mine_at = pl.ds(pl.multiple_of(h.k * LANES, LANES), LANES)
    other_at = pl.ds(pl.multiple_of((1 - h.k) * LANES, LANES), LANES)
    places = (h.beyond, h.up, h.down, h.y)
    sib_copies = []
    for i, z in enumerate((zz, h.z)):
        rows = pl.ds(pl.multiple_of(z * 8 * LANES, 8 * LANES), 8 * LANES)
        part = mm(dz, w1p[0, rows, :], ((1,), (1,)))
        for y in range(4):
            block[i * 4 + y] = part[:, y * 2 * LANES : (y + 1) * 2 * LANES]
        for j, y in enumerate(places):
            sendb[i * 4 + j] = block[i * 4 + y, :, other_at].astype(BF16)
            made = remote(sendb.at[i * 4 + j], ra.at[i * 4 + j], i * 4 + j, h.sib)
            made.start()
            sib_copies.append(made)

    mid = POS // 2
    halves = (slice(0, mid), slice(mid, POS))

    def chip_sum(i, j, rows):
        return block[i * 4 + places[j], rows, mine_at] + ra[i * 4 + j, rows].astype(F32)

    side = [h.at(h.z, y, h.k) for y in places[:3]]
    across = []
    for half, rows in enumerate(halves):
        for j in range(3):
            if half == 0:
                sib_copies[j].wait_recv()
            sendb[8 + j, rows] = chip_sum(0, j, rows).astype(BF16)
            made = remote(sendb.at[8 + j, rows], rb.at[j, rows], 8 + half * 3 + j, side[j])
            made.start()
            across.append(made)
    for j in range(3):
        sib_copies[4 + j].wait_recv()
        sendb[11 + j] = chip_sum(1, j, slice(0, POS)).astype(BF16)
        made = remote(sendb.at[11 + j], rb.at[3 + j], 14 + j, side[j])
        made.start()
        across.append(made)
    sib_copies[3].wait_recv()
    last = []
    for half, rows in enumerate(halves):
        total = chip_sum(0, 3, rows)
        for j in (1, 2, 0):
            across[half * 3 + j].wait_recv()
            total = total + rb[j, rows].astype(F32)
        sendb[14, rows] = total.astype(BF16)
        made = remote(sendb.at[14, rows], rc.at[rows], 17 + half, h.opp)
        made.start()
        last.append(made)
    sib_copies[7].wait_recv()
    mine = chip_sum(1, 3, slice(0, POS))
    for j in (1, 2, 0):
        across[6 + j].wait_recv()
        mine = mine + rb[3 + j].astype(F32)
    gw1_out[...] = mm(dz, hc[...], ((0,), (0,)))
    flip = dl.T
    for i in range(8):
        size = min(LANES, K - i * LANES)
        gh_out[i * LANES : i * LANES + size, :] = flip[:size, i : i + 1] * pooled
    slope = dsilu(pre)
    for made in last:
        made.wait_recv()
    dhidden = mine + rc[...].astype(F32)
    dpre_out[...] = (dhidden * slope)[:, :LOC].astype(BF16)

    for gather in (gx, gxt, gh, ght):
        gather.drain()
    for made in sib_copies + across + last:
        made.wait_send()
    wait_bytes(ls, N_FILT - 1, lsend.at[0])
    wait_bytes(lt, N_FILT - 1, lsend.at[1])
    wait_bytes(ua, N_REP - 1, asend.at[2])

    @pl.when(relay)
    def _():
        wait_bytes(sb, CHUNKS - 1, asend.at[0])
        wait_bytes(sb, N_REP, asend.at[1])
        wait_bytes(sb, N_REP - 1, asend.at[3])

    @pl.when(jnp.logical_not(relay))
    def _():
        wait_bytes(sb, CHUNKS, asend.at[0])


def grads_kernel(xeo, dpre, r1, r0, gw3, gw1, gh, turned, r3, sem):
    copies = []

    def out(src, dst, i):
        made = pltpu.make_async_copy(src, dst, sem.at[i])
        made.start()
        copies.append(made)

    out(r1, gw1.at[:, 0, :], 9)
    out(r0, gh, 10)
    dp = dpre[...].astype(F32)
    even = lax.broadcasted_iota(jnp.int32, (POS, LOC), 1) % 2 == 0
    column = lax.broadcasted_iota(jnp.int32, (POS, LOC), 0) % MAP_W
    zero = jnp.zeros((MAP_W, LOC), F32)
    for b in range(3):
        moved = dp
        if b == 0:
            moved = pltpu.roll(jnp.where(column >= 1, dp, 0.0), POS - 1, 0)
        if b == 2:
            moved = pltpu.roll(jnp.where(column <= MAP_W - 2, dp, 0.0), 1, 0)
        for a in range(3):
            d = moved
            if a == 0:
                d = jnp.concatenate([moved[MAP_W:], zero], axis=0)
            if a == 2:
                d = jnp.concatenate([zero, moved[: POS - MAP_W]], axis=0)
            where = slice(a * LANES, a * LANES + LOC)
            turned[b, :POS, where] = jnp.where(even, d, 0.0).astype(BF16)
            turned[b, POS:, where] = jnp.where(even, 0.0, d).astype(BF16)
    for b in range(3):
        rows = mm(turned[b], xeo[...], ((0,), (0,)))
        for a in range(3):
            t = 3 * a + b
            r3[t] = rows[a * LANES : a * LANES + LOC]
            out(r3.at[t], gw3.at[:, t, 0, :], t)
    for made in copies:
        made.wait()


def per_device(
    images, labels, partner, student_w3, student_w1, student_head, stale_w3, stale_w1, stale_head
):
    vmem = pl.BlockSpec(memory_space=pltpu.VMEM)
    hbm = pl.BlockSpec(memory_space=pltpu.HBM)
    sds = jax.ShapeDtypeStruct
    dma = pltpu.SemaphoreType.DMA
    weights = []
    for w3, w1, head in (
        (student_w3, student_w1, student_head),
        (stale_w3, stale_w1, stale_head),
    ):
        weights += [w3[0].transpose(1, 2, 0), w1[0].T, head[0].T]
    saved = pl.pallas_call(
        main_kernel,
        out_shape=(
            pltpu.VMEM((2 * POS, GW), BF16),
            pltpu.VMEM((POS, LOC), BF16),
            pltpu.VMEM((LOC, C), F32),
            pltpu.VMEM((K, LOC), F32),
        ),
        in_specs=[pl.BlockSpec(memory_space=pltpu.SMEM)] + [hbm] * 8,
        out_specs=[vmem] * 4,
        scratch_shapes=[
            pltpu.SMEM((N_REP,), jnp.int32),
            pltpu.VMEM((POS, LOC), BF16),
            pltpu.VMEM((2, POS, LOC), BF16),
            pltpu.VMEM((POS, C), BF16),
            pltpu.VMEM((9, GW, LOC), BF16),
            pltpu.VMEM((9, GW, LOC), BF16),
            pltpu.VMEM((N_FILT * LANES, 9 * LANES), BF16),
            pltpu.VMEM((N_FILT * LANES, 9 * LANES), BF16),
            pltpu.VMEM((2, C, LOC), BF16),
            pltpu.VMEM((2, N_FILT * LANES, LOC), BF16),
            pltpu.VMEM((K, LOC), BF16),
            pltpu.VMEM((K, LOC), BF16),
            pltpu.VMEM((N_FILT, POS, LANES), BF16),
            pltpu.VMEM((N_FILT, POS, LANES), BF16),
            pltpu.VMEM((N_FILT, POS, LANES), BF16),
            pltpu.VMEM((N_FILT, POS, LANES), BF16),
            pltpu.VMEM((POS, 9 * LANES), F32),
            pltpu.VMEM((POS, 9 * LANES), F32),
            pltpu.VMEM((N_REP, RELAY, LOC), BF16),
            pltpu.VMEM((N_REP, RELAY, LOC), BF16),
            pltpu.VMEM((N_FILT, 8, LANES), F32),
            pltpu.VMEM((N_FILT, 8, LANES), F32),
            pltpu.VMEM((N_REP, 8, LANES), F32),
            pltpu.VMEM((1, 1024), F32),
            pltpu.VMEM((15, POS, LANES), BF16),
            pltpu.VMEM((8, POS, 2 * LANES), F32),
            pltpu.VMEM((8, POS, LANES), BF16),
            pltpu.VMEM((6, POS, LANES), BF16),
            pltpu.VMEM((POS, LANES), BF16),
            dma((8,)),
            dma((4, 19)),
            dma((4, 19)),
            dma((4,)),
            dma((4,)),
            dma((2,)),
            dma((2,)),
            dma((19,)),
            dma((19,)),
        ],
        compiler_params=pltpu.CompilerParams(
            collective_id=0, has_side_effects=True, vmem_limit_bytes=48 * 1024 * 1024
        ),
        name="step",
    )(
        labels,
        *(
            pltpu.with_memory_space_constraint(a, pltpu.HBM)
            for a in (partner, images.transpose(1, 2, 0)[0], *weights)
        ),
    )
    gw3, gw1, gh = pl.pallas_call(
        grads_kernel,
        out_shape=(
            sds((LOC, 9, 1, GW), F32),
            sds((LOC, 1, C), F32),
            sds((K, LOC), F32),
        ),
        in_specs=[vmem] * 4,
        out_specs=[hbm] * 3,
        scratch_shapes=[
            pltpu.VMEM((3, 2 * POS, 3 * LANES), BF16),
            pltpu.VMEM((9, LOC, GW), F32),
            dma((11,)),
        ],
        compiler_params=pltpu.CompilerParams(vmem_limit_bytes=40 * 1024 * 1024),
        name="grads",
    )(*saved)
    return (gw3.transpose(2, 0, 1, 3), gw1.transpose(1, 0, 2), gh.T[None])


def solution(mesh):
    in_specs = (
        P("filt", "rep", None),
        P("rep"),
        P(),
        P("rep", "filt", None, None),
        P("rep", "filt", None),
        P("rep", "filt", None),
        P("rep", "filt", None, None),
        P("rep", "filt", None),
        P("rep", "filt", None),
    )
    out_specs = (P("rep", "filt", None, None), P("rep", "filt", None), P("rep", "filt", None))
    return jax.shard_map(
        per_device, mesh=mesh, in_specs=in_specs, out_specs=out_specs, check_vma=False
    )
```

```python
import functools

import jax
import jax.numpy as jnp
from jax import lax
from jax.experimental import pallas as pl
from jax.experimental.pallas import tpu as pltpu
from jax.sharding import PartitionSpec as P

C = 2016
GW = 1008
K = 1000
ROWS = 4
MAP_W = 56
POS = ROWS * MAP_W
N_REP = 16
N_FILT = 16
LOC = C // N_FILT
HALF = LOC // 2
RELAY = 32
CHUNKS = POS // RELAY
LANES = 128
F32 = jnp.float32
BF16 = jnp.bfloat16
MESH = pl.DeviceIdType.MESH


def mm(a, b, dims=((1,), (0,))):
    return lax.dot_general(a, b, (dims, ((), ())), preferred_element_type=F32)


def silu(v):
    return v / (1.0 + jnp.exp(-v))


def dsilu(v):
    sig = 1.0 / (1.0 + jnp.exp(-v))
    return sig * (1.0 + v * (1.0 - sig))


def split3(v):
    hi = v.astype(BF16)
    rest = v - hi.astype(F32)
    mid = rest.astype(BF16)
    low = (rest - mid.astype(F32)).astype(BF16)
    pad = jnp.zeros((13,) + v.shape[1:], BF16)
    return jnp.concatenate([hi, mid, low, pad], axis=0)


class Gather:
    def __init__(self, panel, send, recv, here, parts=1):
        self.panel, self.send, self.recv, self.here = panel, send, recv, here
        self.parts = parts
        self.started = []

    def copy(self, kind, slot, target, part=None):
        where = self.panel.at[slot]
        if part is not None and self.parts > 1:
            size = POS // self.parts
            where = self.panel.at[slot, pl.ds(part * size, size)]
            kind = kind if part == 0 else 15 + (0, 3, 4, 6).index(kind)
        return pltpu.make_async_remote_copy(
            src_ref=where,
            dst_ref=where,
            send_sem=self.send.at[kind],
            recv_sem=self.recv.at[kind],
            device_id={"rep": self.here.rep, "filt": target},
            device_id_type=MESH,
        )

    def go(self, kind, slot, target, part=None):
        made = self.copy(kind, slot, target, part)
        made.start()
        self.started.append(made)

    def got(self, kind, slot, part=None):
        self.copy(kind, slot, self.here.sib, part).wait_recv()

    def own(self):
        for part in range(self.parts):
            self.go(0, self.here.me, self.here.opp, part)
        self.spread()

    def spread(self):
        h = self.here
        self.go(1, h.me, h.right)
        self.go(2, h.me, h.left)
        self.go(5, h.me, h.far)
        self.go(7, h.me, h.sib)

    def across(self):
        for part in range(self.parts):
            self.got(0, self.here.opp, part)
            self.spread_opp(part)
        self.go(8, self.here.opp, self.here.sib)

    def spread_opp(self, part):
        h = self.here
        self.go(3, h.opp, h.right, part)
        self.go(4, h.opp, h.left, part)
        self.go(6, h.opp, h.far, part)

    def near(self):
        h = self.here
        for kind, slot, onward in ((1, h.left, 9), (2, h.right, 10), (5, h.far, 13)):
            self.got(kind, slot)
            self.go(onward, slot, h.sib)

    def near_opp(self):
        h = self.here
        for kind, slot, onward in ((3, h.left_opp, 11), (4, h.right_opp, 12), (6, h.far_opp, 14)):
            for part in range(self.parts):
                self.got(kind, slot, part)
            self.go(onward, slot, h.sib)

    def plane(self):
        h = self.here
        self.got(7, h.sib)
        self.got(9, h.other(h.left))
        self.got(10, h.other(h.right))
        self.got(13, h.other(h.far))

    def plane_opp(self):
        h = self.here
        self.got(8, h.other(h.opp))
        self.got(11, h.other(h.left_opp))
        self.got(12, h.other(h.right_opp))
        self.got(14, h.other(h.far_opp))

    def drain(self):
        for made in self.started:
            made.wait_send()


class Here:
    def __init__(self):
        self.rep = lax.axis_index("rep")
        self.me = lax.axis_index("filt")
        self.z = self.me // 8
        self.y = (self.me % 8) // 2
        self.k = self.me % 2
        self.up = (self.y + 1) % 4
        self.down = (self.y + 3) % 4
        self.beyond = (self.y + 2) % 4
        self.sib = self.at(self.z, self.y, 1 - self.k)
        self.opp = self.at(1 - self.z, self.y, self.k)
        self.right = self.at(self.z, self.up, self.k)
        self.left = self.at(self.z, self.down, self.k)
        self.far = self.at(self.z, self.beyond, self.k)
        self.right_opp = self.at(1 - self.z, self.up, self.k)
        self.left_opp = self.at(1 - self.z, self.down, self.k)
        self.far_opp = self.at(1 - self.z, self.beyond, self.k)

    def at(self, z, y, k):
        return z * 8 + y * 2 + k

    def other(self, slot):
        return slot + 1 - 2 * (slot % 2)


def main_kernel(
    label, partner_h, x_h, w3s_h, w1s_h, hds_h, w3t_h, w1t_h, hdt_h,
    xeo, dpre_out, gw1_out, gh_out,
    partner, x, xraw, hc, w3s, w3t, wxs, wxt, w1raw, w1p, hds, hdt, xg, xgt, hg, hgt, accs, acct,
    a1, sb, ls, lt, ua, row, sendb, block, ra, rb, rc,
    wsem, gsend, grecv, asend, arecv, lsend, lrecv, rsend, rrecv,
):
    h = Here()
    rep, me = h.rep, h.me

    loads = [
        pltpu.make_async_copy(src, dst, wsem.at[i])
        for i, (src, dst) in enumerate(
            (
                (x_h, x),
                (partner_h, partner),
                (w3s_h, w3s),
                (w3t_h, w3t),
                (w1s_h, w1raw.at[0]),
                (w1t_h, w1raw.at[1]),
                (hds_h, hds),
                (hdt_h, hdt),
            )
        )
    ]
    for load in loads[:2]:
        load.start()
    barrier = pltpu.get_barrier_semaphore()
    for i in range(1, N_REP):
        pl.semaphore_signal(
            barrier, inc=1, device_id={"rep": (rep + i) % N_REP, "filt": me}, device_id_type=MESH
        )
    for i in range(1, N_FILT):
        pl.semaphore_signal(
            barrier, inc=1, device_id={"rep": rep, "filt": (me + i) % N_FILT}, device_id_type=MESH
        )

    for load in loads[2:]:
        load.start()

    lane_from = lax.broadcasted_iota(jnp.int32, (LOC, LANES), 0)
    lane_to = lax.broadcasted_iota(jnp.int32, (LOC, LANES), 1)
    inside = lane_to % 64
    perm = jnp.where((inside < HALF) & (lane_from == 2 * inside + lane_to // 64), 1.0, 0.0)
    perm = perm.astype(BF16)
    pl.semaphore_wait(barrier, N_REP - 1 + N_FILT - 1)

    gx = Gather(xg, gsend.at[0], grecv.at[0], h, 2)
    gxt = Gather(xgt, gsend.at[1], grecv.at[1], h)
    gh = Gather(hg, gsend.at[2], grecv.at[2], h, 2)
    ght = Gather(hgt, gsend.at[3], grecv.at[3], h, 2)

    for i in range(1, N_REP):
        q = (rep + i) % N_REP

        @pl.when(q < 2 * CHUNKS)
        def _():
            pltpu.make_async_remote_copy(
                src_ref=x_h.at[pl.ds(pl.multiple_of(q // 2 * RELAY, RELAY), RELAY)],
                dst_ref=a1.at[rep],
                send_sem=asend.at[0],
                recv_sem=arecv.at[0],
                device_id={"rep": q, "filt": me},
                device_id_type=MESH,
            ).start()

    loads[0].wait()
    xg[me] = mm(x[...], perm).astype(BF16)
    gx.own()
    loads[1].wait()

    def ordered(w3, wx, first, last):
        keep = lax.broadcasted_iota(jnp.int32, (64, LOC), 0) < HALF
        even = lax.broadcasted_iota(jnp.int32, (64, LOC), 1) % 2 == 0

        def body(t, carry):
            where = pl.ds(pl.multiple_of(t * LANES, LANES), LOC)
            w = jnp.concatenate([w3[t].astype(F32), jnp.zeros((8, LOC), F32)], axis=0)
            for f in range(N_FILT):
                piece = w[f * HALF : f * HALF + 64]
                wx[f * LANES : f * LANES + 64, where] = jnp.where(
                    keep & even, piece, 0.0
                ).astype(BF16)
                wx[f * LANES + 64 : (f + 1) * LANES, where] = jnp.where(
                    keep & ~even, piece, 0.0
                ).astype(BF16)
            return carry

        lax.fori_loop(first, last, body, 0)

    relay = rep < 2 * CHUNKS
    chunk = pl.ds(pl.multiple_of(rep % (2 * CHUNKS) // 2 * RELAY, RELAY), RELAY)
    loads[2].wait()
    ordered(w3s, wxs, 0, 4)

    @pl.when(relay)
    def _():
        pltpu.make_async_copy(a1.at[pl.ds(0, 15)], a1.at[pl.ds(0, 15)], arecv.at[0]).wait()
        a1[rep] = x[chunk]
        xraw[0, chunk] = a1[partner[rep]]
        for i in (4, 3, 5, 2, 6, 1, 7, 0):
            p = (rep + 2 * i) % N_REP
            sb[i] = a1[partner[p]]
            for plane, target in enumerate((h.opp, me)):
                if i > 0 or plane == 0:
                    pltpu.make_async_remote_copy(
                        src_ref=sb.at[i],
                        dst_ref=xraw.at[1 - plane, chunk],
                        send_sem=asend.at[1 + 2 * plane],
                        recv_sem=arecv.at[1 + 2 * plane],
                        device_id={"rep": p, "filt": target},
                        device_id_type=MESH,
                    ).start()

    gx.near()
    ordered(w3s, wxs, 4, 8)
    gx.across()
    ordered(w3s, wxs, 8, 9)
    loads[3].wait()
    ordered(w3t, wxt, 0, 2)

    @pl.when(relay)
    def _():
        pltpu.make_async_copy(
            xraw.at[0, pl.ds(0, RELAY * (CHUNKS - 1))],
            xraw.at[0, pl.ds(0, RELAY * (CHUNKS - 1))],
            arecv.at[3],
        ).wait()

    @pl.when(jnp.logical_not(relay))
    def _():
        pltpu.make_async_copy(xraw.at[0], xraw.at[0], arecv.at[3]).wait()

    xgt[me] = mm(xraw[0], perm).astype(BF16)
    gxt.spread()
    pltpu.make_async_copy(xraw.at[1], xraw.at[1], arecv.at[1]).wait()
    xgt[h.opp] = mm(xraw[1], perm).astype(BF16)
    gxt.spread_opp(0)
    gxt.go(8, h.opp, h.sib)
    ordered(w3t, wxt, 2, 5)

    def conv_half(panel, wx, acc, z, first):
        rows = pl.ds(pl.multiple_of(z * (8 * LANES), 8 * LANES), 8 * LANES)
        left = jnp.concatenate([panel[z * 8 + i] for i in range(8)], axis=1)
        for low in (0, 4, 8):
            where = slice(low * LANES, min(low + 4, 9) * LANES)
            part = mm(left, wx[rows, where])
            acc[:, where] = part if first else acc[:, where] + part

    lanes = lax.broadcasted_iota(jnp.int32, (POS, LANES), 1)
    column = lax.broadcasted_iota(jnp.int32, (POS, LANES), 0) % MAP_W

    def conv_end(acc):
        total = None
        top = jnp.zeros((MAP_W, LANES), F32)

        def tap(t, low, high):
            return acc[low:high, t * LANES : (t + 1) * LANES]

        for b in range(3):
            part = tap(3 + b, 0, POS)
            part = part + jnp.concatenate([top, tap(b, 0, POS - MAP_W)], axis=0)
            part = part + jnp.concatenate([tap(6 + b, MAP_W, POS), top], axis=0)
            if b == 0:
                part = jnp.where(column >= 1, pltpu.roll(part, 1, 0), 0.0)
            if b == 2:
                part = jnp.where(column <= MAP_W - 2, pltpu.roll(part, POS - 1, 0), 0.0)
            total = part if total is None else total + part
        return total

    def hidden_of(pre):
        return jnp.where(lanes < LOC, silu(pre), 0.0).astype(BF16)

    gx.plane()
    conv_half(xg, wxs, accs, h.z, True)
    gxt.near()
    gx.near_opp()
    ordered(w3t, wxt, 5, 9)
    gx.plane_opp()
    conv_half(xg, wxs, accs, 1 - h.z, False)
    gxt.near_opp()
    pre = conv_end(accs)
    hg[me] = hidden_of(pre)
    gh.own()
    gxt.plane()
    conv_half(xgt, wxt, acct, h.z, True)
    gxt.plane_opp()
    conv_half(xgt, wxt, acct, 1 - h.z, False)
    hgt[me] = hidden_of(conv_end(acct))
    ght.own()
    gh.near()
    gh.across()

    for which in range(2):
        loads[4 + which].wait()
        for f in range(N_FILT):
            w1p[which, f * LANES : f * LANES + LOC, :] = w1raw[which, f * LOC : (f + 1) * LOC, :]
            w1p[which, f * LANES + LOC : (f + 1) * LANES, :] = jnp.zeros((LANES - LOC, LOC), BF16)

    gh.near_opp()
    ght.near()
    ght.across()
    gh.plane()
    gh.plane_opp()
    ght.near_opp()

    def whole(panel):
        return jnp.concatenate([panel[i] for i in range(N_FILT)], axis=1)

    def logits_of(z, head):
        pooled = jnp.sum(silu(z), axis=0, keepdims=True) * (1.0 / POS)
        parts = mm(split3(pooled), head[...], ((1,), (1,)))
        row[...] = jnp.zeros((1, 1024), F32)
        row[:, :K] = parts[0:1] + parts[1:2] + parts[2:3]
        full = row[...]
        return pooled, jnp.concatenate(
            [full[:, i * LANES : (i + 1) * LANES] for i in range(8)], axis=0
        )

    def give_logits(buf, part, idx):
        buf[me] = part
        for i in (8, 7, 9, 6, 10, 5, 11, 4, 12, 3, 13, 2, 14, 1, 15):
            pltpu.make_async_remote_copy(
                src_ref=buf.at[me],
                dst_ref=buf.at[me],
                send_sem=lsend.at[idx],
                recv_sem=lrecv.at[idx],
                device_id={"rep": rep, "filt": (me + i) % N_FILT},
                device_id_type=MESH,
            ).start()

    def wait_bytes(buf, count, sem):
        pltpu.make_async_copy(buf.at[pl.ds(0, count)], buf.at[pl.ds(0, count)], sem).wait()

    def sum_logits(buf, idx):
        wait_bytes(buf, N_FILT - 1, lrecv.at[idx])
        return jnp.sum(buf[...], axis=0)

    loads[6].wait()
    loads[7].wait()
    z_mixed = x[...].astype(F32) + mm(whole(hg), w1p[0])
    pooled, part = logits_of(z_mixed, hds)
    give_logits(ls, part, 0)
    xt = xraw[0].astype(F32)
    ght.plane()
    ght.plane_opp()
    part = logits_of(xt + mm(whole(hgt), w1p[1]), hdt)[1]
    give_logits(lt, part, 1)
    for f in range(N_FILT):
        hc[:, f * LOC : (f + 1) * LOC] = hg[f, :, :LOC]
    logits = sum_logits(ls, 0)

    cls = lax.broadcasted_iota(jnp.int32, (8, LANES), 0) * LANES + lax.broadcasted_iota(
        jnp.int32, (8, LANES), 1
    )
    real = cls < K

    def softmax(v):
        top = jnp.max(jnp.where(real, v, -jnp.inf))
        e = jnp.where(real, jnp.exp(v - top), 0.0)
        return e / jnp.sum(e)

    own_part = 2.0 * softmax(logits) - jnp.where(cls == label[0], 1.0, 0.0)
    slope = dsilu(z_mixed) * (1.0 / POS)
    ua[rep] = sum_logits(lt, 1)
    for i in range(1, N_REP):
        pltpu.make_async_remote_copy(
            src_ref=ua.at[rep],
            dst_ref=ua.at[rep],
            send_sem=asend.at[2],
            recv_sem=arecv.at[2],
            device_id={"rep": (rep + i) % N_REP, "filt": me},
            device_id_type=MESH,
        ).start()
    for f in range(N_FILT):
        for g in range(2):
            xeo[g * POS : (g + 1) * POS, f * HALF : (f + 1) * HALF] = xg[
                f, :, 64 * g : 64 * g + HALF
            ]
    wait_bytes(ua, N_REP - 1, arecv.at[2])
    dl = own_part - softmax(ua[partner[rep]])
    dl_row = jnp.concatenate([dl[i : i + 1, :] for i in range(8)], axis=1)[:, :K]
    parts = mm(split3(dl_row), hds[...])
    dz = ((parts[0:1] + parts[1:2] + parts[2:3]) * slope).astype(BF16)

    def remote(src, dst, kind, target):
        return pltpu.make_async_remote_copy(
            src_ref=src,
            dst_ref=dst,
            send_sem=rsend.at[kind],
            recv_sem=rrecv.at[kind],
            device_id={"rep": rep, "filt": target},
            device_id_type=MESH,
        )

    zz = 1 - h.z
    mine_at = pl.ds(pl.multiple_of(h.k * LANES, LANES), LANES)
    other_at = pl.ds(pl.multiple_of((1 - h.k) * LANES, LANES), LANES)
    places = (h.beyond, h.up, h.down, h.y)
    sib_copies = []
    for i, z in enumerate((zz, h.z)):
        rows = pl.ds(pl.multiple_of(z * 8 * LANES, 8 * LANES), 8 * LANES)
        part = mm(dz, w1p[0, rows, :], ((1,), (1,)))
        for y in range(4):
            block[i * 4 + y] = part[:, y * 2 * LANES : (y + 1) * 2 * LANES]
        for j, y in enumerate(places):
            sendb[i * 4 + j] = block[i * 4 + y, :, other_at].astype(BF16)
            made = remote(sendb.at[i * 4 + j], ra.at[i * 4 + j], i * 4 + j, h.sib)
            made.start()
            sib_copies.append(made)

    mid = POS // 2
    halves = (slice(0, mid), slice(mid, POS))

    def chip_sum(i, j, rows):
        return block[i * 4 + places[j], rows, mine_at] + ra[i * 4 + j, rows].astype(F32)

    side = [h.at(h.z, y, h.k) for y in places[:3]]
    across = []
    for half, rows in enumerate(halves):
        for j in range(3):
            if half == 0:
                sib_copies[j].wait_recv()
            sendb[8 + j, rows] = chip_sum(0, j, rows).astype(BF16)
            made = remote(sendb.at[8 + j, rows], rb.at[j, rows], 8 + half * 3 + j, side[j])
            made.start()
            across.append(made)
    for j in range(3):
        sib_copies[4 + j].wait_recv()
        sendb[11 + j] = chip_sum(1, j, slice(0, POS)).astype(BF16)
        made = remote(sendb.at[11 + j], rb.at[3 + j], 14 + j, side[j])
        made.start()
        across.append(made)
    sib_copies[3].wait_recv()
    last = []
    for half, rows in enumerate(halves):
        total = chip_sum(0, 3, rows)
        for j in (1, 2, 0):
            across[half * 3 + j].wait_recv()
            total = total + rb[j, rows].astype(F32)
        sendb[14, rows] = total.astype(BF16)
        made = remote(sendb.at[14, rows], rc.at[rows], 17 + half, h.opp)
        made.start()
        last.append(made)
    sib_copies[7].wait_recv()
    mine = chip_sum(1, 3, slice(0, POS))
    for j in (1, 2, 0):
        across[6 + j].wait_recv()
        mine = mine + rb[3 + j].astype(F32)
    gw1_out[...] = mm(dz, hc[...], ((0,), (0,)))
    flip = dl.T
    for i in range(8):
        size = min(LANES, K - i * LANES)
        gh_out[i * LANES : i * LANES + size, :] = flip[:size, i : i + 1] * pooled
    slope = dsilu(pre)
    for made in last:
        made.wait_recv()
    dhidden = mine + rc[...].astype(F32)
    dpre_out[...] = (dhidden * slope)[:, :LOC].astype(BF16)

    for gather in (gx, gxt, gh, ght):
        gather.drain()
    for made in sib_copies + across + last:
        made.wait_send()
    wait_bytes(ls, N_FILT - 1, lsend.at[0])
    wait_bytes(lt, N_FILT - 1, lsend.at[1])
    wait_bytes(ua, N_REP - 1, asend.at[2])

    @pl.when(relay)
    def _():
        wait_bytes(sb, 2 * CHUNKS - 1, asend.at[0])
        wait_bytes(sb, 8, asend.at[1])
        wait_bytes(sb, 7, asend.at[3])

    @pl.when(jnp.logical_not(relay))
    def _():
        wait_bytes(sb, 2 * CHUNKS, asend.at[0])


def grads_kernel(xeo, dpre, r1, r0, gw3, gw1, gh, turned, r3, sem):
    copies = []

    def out(src, dst, i):
        made = pltpu.make_async_copy(src, dst, sem.at[i])
        made.start()
        copies.append(made)

    out(r1, gw1.at[:, 0, :], 9)
    out(r0, gh, 10)
    dp = dpre[...].astype(F32)
    even = lax.broadcasted_iota(jnp.int32, (POS, LOC), 1) % 2 == 0
    column = lax.broadcasted_iota(jnp.int32, (POS, LOC), 0) % MAP_W
    zero = jnp.zeros((MAP_W, LOC), F32)
    for b in (1, 0, 2):
        moved = dp
        if b == 0:
            moved = pltpu.roll(jnp.where(column >= 1, dp, 0.0), POS - 1, 0)
        if b == 2:
            moved = pltpu.roll(jnp.where(column <= MAP_W - 2, dp, 0.0), 1, 0)
        for a in range(3):
            d = moved
            if a == 0:
                d = jnp.concatenate([moved[MAP_W:], zero], axis=0)
            if a == 2:
                d = jnp.concatenate([zero, moved[: POS - MAP_W]], axis=0)
            where = slice(a * LANES, a * LANES + LOC)
            turned[b, :POS, where] = jnp.where(even, d, 0.0).astype(BF16)
            turned[b, POS:, where] = jnp.where(even, 0.0, d).astype(BF16)
        rows = mm(turned[b], xeo[...], ((0,), (0,)))
        for a in range(3):
            t = 3 * a + b
            r3[t] = rows[a * LANES : a * LANES + LOC]
            out(r3.at[t], gw3.at[:, t, 0, :], t)
    for made in copies:
        made.wait()


def per_device(
    images, labels, partner, student_w3, student_w1, student_head, stale_w3, stale_w1, stale_head
):
    vmem = pl.BlockSpec(memory_space=pltpu.VMEM)
    hbm = pl.BlockSpec(memory_space=pltpu.HBM)
    sds = jax.ShapeDtypeStruct
    dma = pltpu.SemaphoreType.DMA
    weights = []
    for w3, w1, head in (
        (student_w3, student_w1, student_head),
        (stale_w3, stale_w1, stale_head),
    ):
        weights += [w3[0].transpose(1, 2, 0), w1[0].T, head[0].T]
    saved = pl.pallas_call(
        main_kernel,
        out_shape=(
            pltpu.VMEM((2 * POS, GW), BF16),
            pltpu.VMEM((POS, LOC), BF16),
            pltpu.VMEM((LOC, C), F32),
            pltpu.VMEM((K, LOC), F32),
        ),
        in_specs=[pl.BlockSpec(memory_space=pltpu.SMEM)] + [hbm] * 8,
        out_specs=[vmem] * 4,
        scratch_shapes=[
            pltpu.SMEM((N_REP,), jnp.int32),
            pltpu.VMEM((POS, LOC), BF16),
            pltpu.VMEM((2, POS, LOC), BF16),
            pltpu.VMEM((POS, C), BF16),
            pltpu.VMEM((9, GW, LOC), BF16),
            pltpu.VMEM((9, GW, LOC), BF16),
            pltpu.VMEM((N_FILT * LANES, 9 * LANES), BF16),
            pltpu.VMEM((N_FILT * LANES, 9 * LANES), BF16),
            pltpu.VMEM((2, C, LOC), BF16),
            pltpu.VMEM((2, N_FILT * LANES, LOC), BF16),
            pltpu.VMEM((K, LOC), BF16),
            pltpu.VMEM((K, LOC), BF16),
            pltpu.VMEM((N_FILT, POS, LANES), BF16),
            pltpu.VMEM((N_FILT, POS, LANES), BF16),
            pltpu.VMEM((N_FILT, POS, LANES), BF16),
            pltpu.VMEM((N_FILT, POS, LANES), BF16),
            pltpu.VMEM((POS, 9 * LANES), F32),
            pltpu.VMEM((POS, 9 * LANES), F32),
            pltpu.VMEM((N_REP, RELAY, LOC), BF16),
            pltpu.VMEM((N_REP, RELAY, LOC), BF16),
            pltpu.VMEM((N_FILT, 8, LANES), F32),
            pltpu.VMEM((N_FILT, 8, LANES), F32),
            pltpu.VMEM((N_REP, 8, LANES), F32),
            pltpu.VMEM((1, 1024), F32),
            pltpu.VMEM((15, POS, LANES), BF16),
            pltpu.VMEM((8, POS, 2 * LANES), F32),
            pltpu.VMEM((8, POS, LANES), BF16),
            pltpu.VMEM((6, POS, LANES), BF16),
            pltpu.VMEM((POS, LANES), BF16),
            dma((8,)),
            dma((4, 19)),
            dma((4, 19)),
            dma((4,)),
            dma((4,)),
            dma((2,)),
            dma((2,)),
            dma((19,)),
            dma((19,)),
        ],
        compiler_params=pltpu.CompilerParams(
            collective_id=0, has_side_effects=True, vmem_limit_bytes=48 * 1024 * 1024
        ),
        name="step",
    )(
        labels,
        *(
            pltpu.with_memory_space_constraint(a, pltpu.HBM)
            for a in (partner, images.transpose(1, 2, 0)[0], *weights)
        ),
    )
    gw3, gw1, gh = pl.pallas_call(
        grads_kernel,
        out_shape=(
            sds((LOC, 9, 1, GW), F32),
            sds((LOC, 1, C), F32),
            sds((K, LOC), F32),
        ),
        in_specs=[vmem] * 4,
        out_specs=[hbm] * 3,
        scratch_shapes=[
            pltpu.VMEM((3, 2 * POS, 3 * LANES), BF16),
            pltpu.VMEM((9, LOC, GW), F32),
            dma((11,)),
        ],
        compiler_params=pltpu.CompilerParams(vmem_limit_bytes=40 * 1024 * 1024),
        name="grads",
    )(*saved)
    return (gw3.transpose(2, 0, 1, 3), gw1.transpose(1, 0, 2), gh.T[None])


def solution(mesh):
    in_specs = (
        P("filt", "rep", None),
        P("rep"),
        P(),
        P("rep", "filt", None, None),
        P("rep", "filt", None),
        P("rep", "filt", None),
        P("rep", "filt", None, None),
        P("rep", "filt", None),
        P("rep", "filt", None),
    )
    out_specs = (P("rep", "filt", None, None), P("rep", "filt", None), P("rep", "filt", None))
    return jax.shard_map(
        per_device, mesh=mesh, in_specs=in_specs, out_specs=out_specs, check_vma=False
    )
```

```python
import functools

import jax
import jax.numpy as jnp
from jax import lax
from jax.experimental import pallas as pl
from jax.experimental.pallas import tpu as pltpu
from jax.sharding import PartitionSpec as P

C = 2016
GW = 1008
K = 1000
ROWS = 4
MAP_W = 56
POS = ROWS * MAP_W
N_REP = 16
N_FILT = 16
LOC = C // N_FILT
HALF = LOC // 2
RELAY = 32
CHUNKS = POS // RELAY
LANES = 128
F32 = jnp.float32
BF16 = jnp.bfloat16
MESH = pl.DeviceIdType.MESH


def mm(a, b, dims=((1,), (0,))):
    return lax.dot_general(a, b, (dims, ((), ())), preferred_element_type=F32)


def silu(v):
    return v / (1.0 + jnp.exp(-v))


def dsilu(v):
    sig = 1.0 / (1.0 + jnp.exp(-v))
    return sig * (1.0 + v * (1.0 - sig))


def split3(v):
    hi = v.astype(BF16)
    rest = v - hi.astype(F32)
    mid = rest.astype(BF16)
    low = (rest - mid.astype(F32)).astype(BF16)
    pad = jnp.zeros((13,) + v.shape[1:], BF16)
    return jnp.concatenate([hi, mid, low, pad], axis=0)


class Gather:
    def __init__(self, panel, send, recv, here, parts=1):
        self.panel, self.send, self.recv, self.here = panel, send, recv, here
        self.parts = parts
        self.started = []

    def copy(self, kind, slot, target, part=None):
        where = self.panel.at[slot]
        if part is not None and self.parts > 1:
            size = POS // self.parts
            where = self.panel.at[slot, pl.ds(part * size, size)]
            kind = kind if part == 0 else 15 + (0, 3, 4, 6).index(kind)
        return pltpu.make_async_remote_copy(
            src_ref=where,
            dst_ref=where,
            send_sem=self.send.at[kind],
            recv_sem=self.recv.at[kind],
            device_id={"rep": self.here.rep, "filt": target},
            device_id_type=MESH,
        )

    def go(self, kind, slot, target, part=None):
        made = self.copy(kind, slot, target, part)
        made.start()
        self.started.append(made)

    def got(self, kind, slot, part=None):
        self.copy(kind, slot, self.here.sib, part).wait_recv()

    def own(self):
        for part in range(self.parts):
            self.go(0, self.here.me, self.here.opp, part)
        self.spread()

    def spread(self):
        h = self.here
        self.go(1, h.me, h.right)
        self.go(2, h.me, h.left)
        self.go(5, h.me, h.far)
        self.go(7, h.me, h.sib)

    def across(self):
        for part in range(self.parts):
            self.got(0, self.here.opp, part)
            self.spread_opp(part)
        self.go(8, self.here.opp, self.here.sib)

    def spread_opp(self, part):
        h = self.here
        self.go(3, h.opp, h.right, part)
        self.go(4, h.opp, h.left, part)
        self.go(6, h.opp, h.far, part)

    def near(self):
        h = self.here
        for kind, slot, onward in ((1, h.left, 9), (2, h.right, 10), (5, h.far, 13)):
            self.got(kind, slot)
            self.go(onward, slot, h.sib)

    def near_opp(self):
        h = self.here
        for kind, slot, onward in ((3, h.left_opp, 11), (4, h.right_opp, 12), (6, h.far_opp, 14)):
            for part in range(self.parts):
                self.got(kind, slot, part)
            self.go(onward, slot, h.sib)

    def plane(self):
        h = self.here
        self.got(7, h.sib)
        self.got(9, h.other(h.left))
        self.got(10, h.other(h.right))
        self.got(13, h.other(h.far))

    def plane_opp(self):
        h = self.here
        self.got(8, h.other(h.opp))
        self.got(11, h.other(h.left_opp))
        self.got(12, h.other(h.right_opp))
        self.got(14, h.other(h.far_opp))

    def drain(self):
        for made in self.started:
            made.wait_send()


class Here:
    def __init__(self):
        self.rep = lax.axis_index("rep")
        self.me = lax.axis_index("filt")
        self.z = self.me // 8
        self.y = (self.me % 8) // 2
        self.k = self.me % 2
        self.up = (self.y + 1) % 4
        self.down = (self.y + 3) % 4
        self.beyond = (self.y + 2) % 4
        self.sib = self.at(self.z, self.y, 1 - self.k)
        self.opp = self.at(1 - self.z, self.y, self.k)
        self.right = self.at(self.z, self.up, self.k)
        self.left = self.at(self.z, self.down, self.k)
        self.far = self.at(self.z, self.beyond, self.k)
        self.right_opp = self.at(1 - self.z, self.up, self.k)
        self.left_opp = self.at(1 - self.z, self.down, self.k)
        self.far_opp = self.at(1 - self.z, self.beyond, self.k)

    def at(self, z, y, k):
        return z * 8 + y * 2 + k

    def other(self, slot):
        return slot + 1 - 2 * (slot % 2)


def main_kernel(
    label, partner_h, x_h, w3s_h, w1s_h, hds_h, w3t_h, w1t_h, hdt_h,
    xeo, dpre_out, gw1_out, gh_out,
    partner, x, xraw, xeot, hc, w3s, w3t, wxs, wxt, w1raw, w1p, hds, hdt, xg, xgt, hg, hgt, accs, acct,
    a1, sb, ls, lt, ua, row, sendb, block, ra, rb, rc,
    wsem, gsend, grecv, asend, arecv, lsend, lrecv, rsend, rrecv,
):
    h = Here()
    rep, me = h.rep, h.me

    loads = [
        pltpu.make_async_copy(src, dst, wsem.at[i])
        for i, (src, dst) in enumerate(
            (
                (x_h, x),
                (partner_h, partner),
                (w3s_h, w3s),
                (w3t_h, w3t),
                (w1s_h, w1raw.at[0]),
                (w1t_h, w1raw.at[1]),
                (hds_h, hds),
                (hdt_h, hdt),
            )
        )
    ]
    for load in loads[:2]:
        load.start()
    barrier = pltpu.get_barrier_semaphore()
    for i in range(1, N_REP):
        pl.semaphore_signal(
            barrier, inc=1, device_id={"rep": (rep + i) % N_REP, "filt": me}, device_id_type=MESH
        )
    for i in range(1, N_FILT):
        pl.semaphore_signal(
            barrier, inc=1, device_id={"rep": rep, "filt": (me + i) % N_FILT}, device_id_type=MESH
        )

    for load in loads[2:]:
        load.start()

    lane_from = lax.broadcasted_iota(jnp.int32, (LOC, LANES), 0)
    lane_to = lax.broadcasted_iota(jnp.int32, (LOC, LANES), 1)
    inside = lane_to % 64
    perm = jnp.where((inside < HALF) & (lane_from == 2 * inside + lane_to // 64), 1.0, 0.0)
    perm = perm.astype(BF16)
    pl.semaphore_wait(barrier, N_REP - 1 + N_FILT - 1)

    gx = Gather(xg, gsend.at[0], grecv.at[0], h, 2)
    gxt = Gather(xgt, gsend.at[1], grecv.at[1], h)
    gh = Gather(hg, gsend.at[2], grecv.at[2], h, 2)
    ght = Gather(hgt, gsend.at[3], grecv.at[3], h, 2)

    for i in range(1, N_REP):
        q = (rep + i) % N_REP

        @pl.when(q < 2 * CHUNKS)
        def _():
            pltpu.make_async_remote_copy(
                src_ref=x_h.at[pl.ds(pl.multiple_of(q // 2 * RELAY, RELAY), RELAY)],
                dst_ref=a1.at[rep],
                send_sem=asend.at[0],
                recv_sem=arecv.at[0],
                device_id={"rep": q, "filt": me},
                device_id_type=MESH,
            ).start()

    loads[0].wait()
    xg[me] = mm(x[...], perm).astype(BF16)
    gx.own()
    loads[1].wait()

    def pack(w3, wx):
        for t in range(9):
            wx[:, t * LANES : t * LANES + LOC] = w3[t]

    relay = rep < 2 * CHUNKS
    chunk = pl.ds(pl.multiple_of(rep % (2 * CHUNKS) // 2 * RELAY, RELAY), RELAY)
    loads[2].wait()
    pack(w3s, wxs)

    @pl.when(relay)
    def _():
        pltpu.make_async_copy(a1.at[pl.ds(0, 15)], a1.at[pl.ds(0, 15)], arecv.at[0]).wait()
        a1[rep] = x[chunk]
        xraw[0, chunk] = a1[partner[rep]]
        for i in (4, 3, 5, 2, 6, 1, 7, 0):
            p = (rep + 2 * i) % N_REP
            sb[i] = a1[partner[p]]
            for plane, target in enumerate((h.opp, me)):
                if i > 0 or plane == 0:
                    pltpu.make_async_remote_copy(
                        src_ref=sb.at[i],
                        dst_ref=xraw.at[1 - plane, chunk],
                        send_sem=asend.at[1 + 2 * plane],
                        recv_sem=arecv.at[1 + 2 * plane],
                        device_id={"rep": p, "filt": target},
                        device_id_type=MESH,
                    ).start()

    gx.near()
    gx.across()
    loads[3].wait()
    pack(w3t, wxt)

    @pl.when(relay)
    def _():
        pltpu.make_async_copy(
            xraw.at[0, pl.ds(0, RELAY * (CHUNKS - 1))],
            xraw.at[0, pl.ds(0, RELAY * (CHUNKS - 1))],
            arecv.at[3],
        ).wait()

    @pl.when(jnp.logical_not(relay))
    def _():
        pltpu.make_async_copy(xraw.at[0], xraw.at[0], arecv.at[3]).wait()

    xgt[me] = mm(xraw[0], perm).astype(BF16)
    gxt.spread()
    pltpu.make_async_copy(xraw.at[1], xraw.at[1], arecv.at[1]).wait()
    xgt[h.opp] = mm(xraw[1], perm).astype(BF16)
    gxt.spread_opp(0)
    gxt.go(8, h.opp, h.sib)

    def assemble(panel, out, z):
        for plane in range(2):

            @pl.when(z == plane)
            def _():
                for f in range(plane * 8, plane * 8 + 8):
                    for g in range(2):
                        out[g * POS : (g + 1) * POS, f * HALF : (f + 1) * HALF] = panel[
                            f, :, 64 * g : 64 * g + HALF
                        ]

    def conv(panel, wx, acc):
        for low in (0, 4, 8):
            where = slice(low * LANES, min(low + 4, 9) * LANES)
            both = mm(panel[...], wx[:, where])
            even = lax.broadcasted_iota(jnp.int32, (POS, both.shape[1]), 1) % 2 == 0
            acc[:, where] = jnp.where(even, both[:POS], both[POS:])

    lanes = lax.broadcasted_iota(jnp.int32, (POS, LANES), 1)
    column = lax.broadcasted_iota(jnp.int32, (POS, LANES), 0) % MAP_W

    def conv_end(acc):
        total = None
        top = jnp.zeros((MAP_W, LANES), F32)

        def tap(t, low, high):
            return acc[low:high, t * LANES : (t + 1) * LANES]

        for b in range(3):
            part = tap(3 + b, 0, POS)
            part = part + jnp.concatenate([top, tap(b, 0, POS - MAP_W)], axis=0)
            part = part + jnp.concatenate([tap(6 + b, MAP_W, POS), top], axis=0)
            if b == 0:
                part = jnp.where(column >= 1, pltpu.roll(part, 1, 0), 0.0)
            if b == 2:
                part = jnp.where(column <= MAP_W - 2, pltpu.roll(part, POS - 1, 0), 0.0)
            total = part if total is None else total + part
        return total

    def hidden_of(pre):
        return jnp.where(lanes < LOC, silu(pre), 0.0).astype(BF16)

    gx.plane()
    assemble(xg, xeo, h.z)
    gxt.near()
    gx.near_opp()
    gx.plane_opp()
    assemble(xg, xeo, 1 - h.z)
    conv(xeo, wxs, accs)
    gxt.near_opp()
    pre = conv_end(accs)
    hg[me] = hidden_of(pre)
    gh.own()
    gxt.plane()
    assemble(xgt, xeot, h.z)
    gxt.plane_opp()
    assemble(xgt, xeot, 1 - h.z)
    conv(xeot, wxt, acct)
    hgt[me] = hidden_of(conv_end(acct))
    ght.own()
    gh.near()
    gh.across()

    for which in range(2):
        loads[4 + which].wait()
        for f in range(N_FILT):
            w1p[which, f * LANES : f * LANES + LOC, :] = w1raw[which, f * LOC : (f + 1) * LOC, :]
            w1p[which, f * LANES + LOC : (f + 1) * LANES, :] = jnp.zeros((LANES - LOC, LOC), BF16)

    gh.near_opp()
    ght.near()
    ght.across()
    gh.plane()
    gh.plane_opp()
    ght.near_opp()

    def whole(panel):
        return jnp.concatenate([panel[i] for i in range(N_FILT)], axis=1)

    def logits_of(z, head):
        pooled = jnp.sum(silu(z), axis=0, keepdims=True) * (1.0 / POS)
        parts = mm(split3(pooled), head[...], ((1,), (1,)))
        row[...] = jnp.zeros((1, 1024), F32)
        row[:, :K] = parts[0:1] + parts[1:2] + parts[2:3]
        full = row[...]
        return pooled, jnp.concatenate(
            [full[:, i * LANES : (i + 1) * LANES] for i in range(8)], axis=0
        )

    def give_logits(buf, part, idx):
        buf[me] = part
        for i in (8, 7, 9, 6, 10, 5, 11, 4, 12, 3, 13, 2, 14, 1, 15):
            pltpu.make_async_remote_copy(
                src_ref=buf.at[me],
                dst_ref=buf.at[me],
                send_sem=lsend.at[idx],
                recv_sem=lrecv.at[idx],
                device_id={"rep": rep, "filt": (me + i) % N_FILT},
                device_id_type=MESH,
            ).start()

    def wait_bytes(buf, count, sem):
        pltpu.make_async_copy(buf.at[pl.ds(0, count)], buf.at[pl.ds(0, count)], sem).wait()

    def sum_logits(buf, idx):
        wait_bytes(buf, N_FILT - 1, lrecv.at[idx])
        return jnp.sum(buf[...], axis=0)

    loads[6].wait()
    loads[7].wait()
    z_mixed = x[...].astype(F32) + mm(whole(hg), w1p[0])
    pooled, part = logits_of(z_mixed, hds)
    give_logits(ls, part, 0)
    xt = xraw[0].astype(F32)
    ght.plane()
    ght.plane_opp()
    part = logits_of(xt + mm(whole(hgt), w1p[1]), hdt)[1]
    give_logits(lt, part, 1)
    for f in range(N_FILT):
        hc[:, f * LOC : (f + 1) * LOC] = hg[f, :, :LOC]
    logits = sum_logits(ls, 0)

    cls = lax.broadcasted_iota(jnp.int32, (8, LANES), 0) * LANES + lax.broadcasted_iota(
        jnp.int32, (8, LANES), 1
    )
    real = cls < K

    def softmax(v):
        top = jnp.max(jnp.where(real, v, -jnp.inf))
        e = jnp.where(real, jnp.exp(v - top), 0.0)
        return e / jnp.sum(e)

    own_part = 2.0 * softmax(logits) - jnp.where(cls == label[0], 1.0, 0.0)
    slope = dsilu(z_mixed) * (1.0 / POS)
    ua[rep] = sum_logits(lt, 1)
    for i in range(1, N_REP):
        pltpu.make_async_remote_copy(
            src_ref=ua.at[rep],
            dst_ref=ua.at[rep],
            send_sem=asend.at[2],
            recv_sem=arecv.at[2],
            device_id={"rep": (rep + i) % N_REP, "filt": me},
            device_id_type=MESH,
        ).start()
    wait_bytes(ua, N_REP - 1, arecv.at[2])
    dl = own_part - softmax(ua[partner[rep]])
    dl_row = jnp.concatenate([dl[i : i + 1, :] for i in range(8)], axis=1)[:, :K]
    parts = mm(split3(dl_row), hds[...])
    dz = ((parts[0:1] + parts[1:2] + parts[2:3]) * slope).astype(BF16)

    def remote(src, dst, kind, target):
        return pltpu.make_async_remote_copy(
            src_ref=src,
            dst_ref=dst,
            send_sem=rsend.at[kind],
            recv_sem=rrecv.at[kind],
            device_id={"rep": rep, "filt": target},
            device_id_type=MESH,
        )

    zz = 1 - h.z
    mine_at = pl.ds(pl.multiple_of(h.k * LANES, LANES), LANES)
    other_at = pl.ds(pl.multiple_of((1 - h.k) * LANES, LANES), LANES)
    places = (h.beyond, h.up, h.down, h.y)
    sib_copies = []
    for i, z in enumerate((zz, h.z)):
        rows = pl.ds(pl.multiple_of(z * 8 * LANES, 8 * LANES), 8 * LANES)
        part = mm(dz, w1p[0, rows, :], ((1,), (1,)))
        for y in range(4):
            block[i * 4 + y] = part[:, y * 2 * LANES : (y + 1) * 2 * LANES]
        for j, y in enumerate(places):
            sendb[i * 4 + j] = block[i * 4 + y, :, other_at].astype(BF16)
            made = remote(sendb.at[i * 4 + j], ra.at[i * 4 + j], i * 4 + j, h.sib)
            made.start()
            sib_copies.append(made)

    mid = POS // 2
    halves = (slice(0, mid), slice(mid, POS))

    def chip_sum(i, j, rows):
        return block[i * 4 + places[j], rows, mine_at] + ra[i * 4 + j, rows].astype(F32)

    side = [h.at(h.z, y, h.k) for y in places[:3]]
    across = []
    for half, rows in enumerate(halves):
        for j in range(3):
            if half == 0:
                sib_copies[j].wait_recv()
            sendb[8 + j, rows] = chip_sum(0, j, rows).astype(BF16)
            made = remote(sendb.at[8 + j, rows], rb.at[j, rows], 8 + half * 3 + j, side[j])
            made.start()
            across.append(made)
    for j in range(3):
        sib_copies[4 + j].wait_recv()
        sendb[11 + j] = chip_sum(1, j, slice(0, POS)).astype(BF16)
        made = remote(sendb.at[11 + j], rb.at[3 + j], 14 + j, side[j])
        made.start()
        across.append(made)
    sib_copies[3].wait_recv()
    last = []
    for half, rows in enumerate(halves):
        total = chip_sum(0, 3, rows)
        for j in (1, 2, 0):
            across[half * 3 + j].wait_recv()
            total = total + rb[j, rows].astype(F32)
        sendb[14, rows] = total.astype(BF16)
        made = remote(sendb.at[14, rows], rc.at[rows], 17 + half, h.opp)
        made.start()
        last.append(made)
    sib_copies[7].wait_recv()
    mine = chip_sum(1, 3, slice(0, POS))
    for j in (1, 2, 0):
        across[6 + j].wait_recv()
        mine = mine + rb[3 + j].astype(F32)
    gw1_out[...] = mm(dz, hc[...], ((0,), (0,)))
    flip = dl.T
    for i in range(8):
        size = min(LANES, K - i * LANES)
        gh_out[i * LANES : i * LANES + size, :] = flip[:size, i : i + 1] * pooled
    slope = dsilu(pre)
    for made in last:
        made.wait_recv()
    dhidden = mine + rc[...].astype(F32)
    dpre_out[...] = (dhidden * slope)[:, :LOC].astype(BF16)

    for gather in (gx, gxt, gh, ght):
        gather.drain()
    for made in sib_copies + across + last:
        made.wait_send()
    wait_bytes(ls, N_FILT - 1, lsend.at[0])
    wait_bytes(lt, N_FILT - 1, lsend.at[1])
    wait_bytes(ua, N_REP - 1, asend.at[2])

    @pl.when(relay)
    def _():
        wait_bytes(sb, 2 * CHUNKS - 1, asend.at[0])
        wait_bytes(sb, 8, asend.at[1])
        wait_bytes(sb, 7, asend.at[3])

    @pl.when(jnp.logical_not(relay))
    def _():
        wait_bytes(sb, 2 * CHUNKS, asend.at[0])


def grads_kernel(xeo, dpre, r1, r0, gw3, gw1, gh, turned, r3, sem):
    copies = []

    def out(src, dst, i):
        made = pltpu.make_async_copy(src, dst, sem.at[i])
        made.start()
        copies.append(made)

    out(r1, gw1.at[:, 0, :], 9)
    out(r0, gh, 10)
    dp = dpre[...].astype(F32)
    even = lax.broadcasted_iota(jnp.int32, (POS, LOC), 1) % 2 == 0
    column = lax.broadcasted_iota(jnp.int32, (POS, LOC), 0) % MAP_W
    zero = jnp.zeros((MAP_W, LOC), F32)
    for b in (1, 0, 2):
        moved = dp
        if b == 0:
            moved = pltpu.roll(jnp.where(column >= 1, dp, 0.0), POS - 1, 0)
        if b == 2:
            moved = pltpu.roll(jnp.where(column <= MAP_W - 2, dp, 0.0), 1, 0)
        for a in range(3):
            d = moved
            if a == 0:
                d = jnp.concatenate([moved[MAP_W:], zero], axis=0)
            if a == 2:
                d = jnp.concatenate([zero, moved[: POS - MAP_W]], axis=0)
            where = slice(a * LANES, a * LANES + LOC)
            turned[b, :POS, where] = jnp.where(even, d, 0.0).astype(BF16)
            turned[b, POS:, where] = jnp.where(even, 0.0, d).astype(BF16)
        rows = mm(turned[b], xeo[...], ((0,), (0,)))
        for a in range(3):
            t = 3 * a + b
            r3[t] = rows[a * LANES : a * LANES + LOC]
            out(r3.at[t], gw3.at[:, t, 0, :], t)
    for made in copies:
        made.wait()


def per_device(
    images, labels, partner, student_w3, student_w1, student_head, stale_w3, stale_w1, stale_head
):
    vmem = pl.BlockSpec(memory_space=pltpu.VMEM)
    hbm = pl.BlockSpec(memory_space=pltpu.HBM)
    sds = jax.ShapeDtypeStruct
    dma = pltpu.SemaphoreType.DMA
    weights = []
    for w3, w1, head in (
        (student_w3, student_w1, student_head),
        (stale_w3, stale_w1, stale_head),
    ):
        weights += [w3[0].transpose(1, 2, 0), w1[0].T, head[0].T]
    saved = pl.pallas_call(
        main_kernel,
        out_shape=(
            pltpu.VMEM((2 * POS, GW), BF16),
            pltpu.VMEM((POS, LOC), BF16),
            pltpu.VMEM((LOC, C), F32),
            pltpu.VMEM((K, LOC), F32),
        ),
        in_specs=[pl.BlockSpec(memory_space=pltpu.SMEM)] + [hbm] * 8,
        out_specs=[vmem] * 4,
        scratch_shapes=[
            pltpu.SMEM((N_REP,), jnp.int32),
            pltpu.VMEM((POS, LOC), BF16),
            pltpu.VMEM((2, POS, LOC), BF16),
            pltpu.VMEM((2 * POS, GW), BF16),
            pltpu.VMEM((POS, C), BF16),
            pltpu.VMEM((9, GW, LOC), BF16),
            pltpu.VMEM((9, GW, LOC), BF16),
            pltpu.VMEM((GW, 9 * LANES), BF16),
            pltpu.VMEM((GW, 9 * LANES), BF16),
            pltpu.VMEM((2, C, LOC), BF16),
            pltpu.VMEM((2, N_FILT * LANES, LOC), BF16),
            pltpu.VMEM((K, LOC), BF16),
            pltpu.VMEM((K, LOC), BF16),
            pltpu.VMEM((N_FILT, POS, LANES), BF16),
            pltpu.VMEM((N_FILT, POS, LANES), BF16),
            pltpu.VMEM((N_FILT, POS, LANES), BF16),
            pltpu.VMEM((N_FILT, POS, LANES), BF16),
            pltpu.VMEM((POS, 9 * LANES), F32),
            pltpu.VMEM((POS, 9 * LANES), F32),
            pltpu.VMEM((N_REP, RELAY, LOC), BF16),
            pltpu.VMEM((N_REP, RELAY, LOC), BF16),
            pltpu.VMEM((N_FILT, 8, LANES), F32),
            pltpu.VMEM((N_FILT, 8, LANES), F32),
            pltpu.VMEM((N_REP, 8, LANES), F32),
            pltpu.VMEM((1, 1024), F32),
            pltpu.VMEM((15, POS, LANES), BF16),
            pltpu.VMEM((8, POS, 2 * LANES), F32),
            pltpu.VMEM((8, POS, LANES), BF16),
            pltpu.VMEM((6, POS, LANES), BF16),
            pltpu.VMEM((POS, LANES), BF16),
            dma((8,)),
            dma((4, 19)),
            dma((4, 19)),
            dma((4,)),
            dma((4,)),
            dma((2,)),
            dma((2,)),
            dma((19,)),
            dma((19,)),
        ],
        compiler_params=pltpu.CompilerParams(
            collective_id=0, has_side_effects=True, vmem_limit_bytes=48 * 1024 * 1024
        ),
        name="step",
    )(
        labels,
        *(
            pltpu.with_memory_space_constraint(a, pltpu.HBM)
            for a in (partner, images.transpose(1, 2, 0)[0], *weights)
        ),
    )
    gw3, gw1, gh = pl.pallas_call(
        grads_kernel,
        out_shape=(
            sds((LOC, 9, 1, GW), F32),
            sds((LOC, 1, C), F32),
            sds((K, LOC), F32),
        ),
        in_specs=[vmem] * 4,
        out_specs=[hbm] * 3,
        scratch_shapes=[
            pltpu.VMEM((3, 2 * POS, 3 * LANES), BF16),
            pltpu.VMEM((9, LOC, GW), F32),
            dma((11,)),
        ],
        compiler_params=pltpu.CompilerParams(vmem_limit_bytes=40 * 1024 * 1024),
        name="grads",
    )(*saved)
    return (gw3.transpose(2, 0, 1, 3), gw1.transpose(1, 0, 2), gh.T[None])


def solution(mesh):
    in_specs = (
        P("filt", "rep", None),
        P("rep"),
        P(),
        P("rep", "filt", None, None),
        P("rep", "filt", None),
        P("rep", "filt", None),
        P("rep", "filt", None, None),
        P("rep", "filt", None),
        P("rep", "filt", None),
    )
    out_specs = (P("rep", "filt", None, None), P("rep", "filt", None), P("rep", "filt", None))
    return jax.shard_map(
        per_device, mesh=mesh, in_specs=in_specs, out_specs=out_specs, check_vma=False
    )
```

```python
import functools

import jax
import jax.numpy as jnp
from jax import lax
from jax.experimental import pallas as pl
from jax.experimental.pallas import tpu as pltpu
from jax.sharding import PartitionSpec as P

C = 2016
GW = 1008
K = 1000
ROWS = 4
MAP_W = 56
POS = ROWS * MAP_W
N_REP = 16
N_FILT = 16
LOC = C // N_FILT
HALF = LOC // 2
RELAY = 32
CHUNKS = POS // RELAY
LANES = 128
F32 = jnp.float32
BF16 = jnp.bfloat16
MESH = pl.DeviceIdType.MESH


def mm(a, b, dims=((1,), (0,))):
    return lax.dot_general(a, b, (dims, ((), ())), preferred_element_type=F32)


def silu(v):
    return v / (1.0 + jnp.exp(-v))


def dsilu(v):
    sig = 1.0 / (1.0 + jnp.exp(-v))
    return sig * (1.0 + v * (1.0 - sig))


def split3(v):
    hi = v.astype(BF16)
    rest = v - hi.astype(F32)
    mid = rest.astype(BF16)
    low = (rest - mid.astype(F32)).astype(BF16)
    pad = jnp.zeros((13,) + v.shape[1:], BF16)
    return jnp.concatenate([hi, mid, low, pad], axis=0)


class Gather:
    def __init__(self, panel, send, recv, here, parts=1):
        self.panel, self.send, self.recv, self.here = panel, send, recv, here
        self.parts = parts
        self.started = []

    def copy(self, kind, slot, target, part=None):
        where = self.panel.at[slot]
        if part is not None and self.parts > 1:
            size = POS // self.parts
            where = self.panel.at[slot, pl.ds(part * size, size)]
            kind = kind if part == 0 else 15 + (0, 3, 4, 6).index(kind)
        return pltpu.make_async_remote_copy(
            src_ref=where,
            dst_ref=where,
            send_sem=self.send.at[kind],
            recv_sem=self.recv.at[kind],
            device_id={"rep": self.here.rep, "filt": target},
            device_id_type=MESH,
        )

    def go(self, kind, slot, target, part=None):
        made = self.copy(kind, slot, target, part)
        made.start()
        self.started.append(made)

    def got(self, kind, slot, part=None):
        self.copy(kind, slot, self.here.sib, part).wait_recv()

    def own(self):
        for part in range(self.parts):
            self.go(0, self.here.me, self.here.opp, part)
        self.spread()

    def spread(self):
        h = self.here
        self.go(1, h.me, h.right)
        self.go(2, h.me, h.left)
        self.go(5, h.me, h.far)
        self.go(7, h.me, h.sib)

    def across(self):
        for part in range(self.parts):
            self.got(0, self.here.opp, part)
            self.spread_opp(part)
        self.go(8, self.here.opp, self.here.sib)

    def spread_opp(self, part):
        h = self.here
        self.go(3, h.opp, h.right, part)
        self.go(4, h.opp, h.left, part)
        self.go(6, h.opp, h.far, part)

    def near(self):
        h = self.here
        for kind, slot, onward in ((1, h.left, 9), (2, h.right, 10), (5, h.far, 13)):
            self.got(kind, slot)
            self.go(onward, slot, h.sib)

    def near_opp(self):
        h = self.here
        for kind, slot, onward in ((3, h.left_opp, 11), (4, h.right_opp, 12), (6, h.far_opp, 14)):
            for part in range(self.parts):
                self.got(kind, slot, part)
            self.go(onward, slot, h.sib)

    def plane(self):
        h = self.here
        self.got(7, h.sib)
        self.got(9, h.other(h.left))
        self.got(10, h.other(h.right))
        self.got(13, h.other(h.far))

    def plane_opp(self):
        h = self.here
        self.got(8, h.other(h.opp))
        self.got(11, h.other(h.left_opp))
        self.got(12, h.other(h.right_opp))
        self.got(14, h.other(h.far_opp))

    def drain(self):
        for made in self.started:
            made.wait_send()


class Here:
    def __init__(self):
        self.rep = lax.axis_index("rep")
        self.me = lax.axis_index("filt")
        self.z = self.me // 8
        self.y = (self.me % 8) // 2
        self.k = self.me % 2
        self.up = (self.y + 1) % 4
        self.down = (self.y + 3) % 4
        self.beyond = (self.y + 2) % 4
        self.sib = self.at(self.z, self.y, 1 - self.k)
        self.opp = self.at(1 - self.z, self.y, self.k)
        self.right = self.at(self.z, self.up, self.k)
        self.left = self.at(self.z, self.down, self.k)
        self.far = self.at(self.z, self.beyond, self.k)
        self.right_opp = self.at(1 - self.z, self.up, self.k)
        self.left_opp = self.at(1 - self.z, self.down, self.k)
        self.far_opp = self.at(1 - self.z, self.beyond, self.k)

    def at(self, z, y, k):
        return z * 8 + y * 2 + k

    def other(self, slot):
        return slot + 1 - 2 * (slot % 2)


def main_kernel(
    label, partner_h, x_h, w3s_h, w1s_h, hds_h, w3t_h, w1t_h, hdt_h,
    xeo, dpre_out, gw1_out, gh_out,
    partner, x, xraw, hc, w3s, w3t, wxs, wxt, w1raw, w1p, hds, hdt, xg, xgt, hg, hgt, accs, acct,
    a1, sb, ls, lt, ua, row, sendb, block, ra, rb, rc,
    wsem, gsend, grecv, asend, arecv, lsend, lrecv, rsend, rrecv,
):
    h = Here()
    rep, me = h.rep, h.me

    loads = [
        pltpu.make_async_copy(src, dst, wsem.at[i])
        for i, (src, dst) in enumerate(
            (
                (x_h, x),
                (partner_h, partner),
                (w3s_h, w3s),
                (w3t_h, w3t),
                (w1s_h, w1raw.at[0]),
                (w1t_h, w1raw.at[1]),
                (hds_h, hds),
                (hdt_h, hdt),
            )
        )
    ]
    for load in loads[:2]:
        load.start()
    barrier = pltpu.get_barrier_semaphore()
    for i in range(1, N_REP):
        pl.semaphore_signal(
            barrier, inc=1, device_id={"rep": (rep + i) % N_REP, "filt": me}, device_id_type=MESH
        )
    for i in range(1, N_FILT):
        pl.semaphore_signal(
            barrier, inc=1, device_id={"rep": rep, "filt": (me + i) % N_FILT}, device_id_type=MESH
        )

    for load in loads[2:]:
        load.start()

    lane_from = lax.broadcasted_iota(jnp.int32, (LOC, LANES), 0)
    lane_to = lax.broadcasted_iota(jnp.int32, (LOC, LANES), 1)
    inside = lane_to % 64
    perm = jnp.where((inside < HALF) & (lane_from == 2 * inside + lane_to // 64), 1.0, 0.0)
    perm = perm.astype(BF16)
    pl.semaphore_wait(barrier, N_REP - 1 + N_FILT - 1)

    gx = Gather(xg, gsend.at[0], grecv.at[0], h, 2)
    gxt = Gather(xgt, gsend.at[1], grecv.at[1], h)
    gh = Gather(hg, gsend.at[2], grecv.at[2], h, 2)
    ght = Gather(hgt, gsend.at[3], grecv.at[3], h, 2)

    for i in range(1, N_REP):
        q = (rep + i) % N_REP

        @pl.when(q < 2 * CHUNKS)
        def _():
            pltpu.make_async_remote_copy(
                src_ref=x_h.at[pl.ds(pl.multiple_of(q // 2 * RELAY, RELAY), RELAY)],
                dst_ref=a1.at[rep],
                send_sem=asend.at[0],
                recv_sem=arecv.at[0],
                device_id={"rep": q, "filt": me},
                device_id_type=MESH,
            ).start()

    loads[0].wait()
    xg[me] = mm(x[...], perm).astype(BF16)
    gx.own()
    loads[1].wait()

    def ordered(w3, wx, first, last):
        keep = lax.broadcasted_iota(jnp.int32, (64, LOC), 0) < HALF
        even = lax.broadcasted_iota(jnp.int32, (64, LOC), 1) % 2 == 0

        def body(t, carry):
            where = pl.ds(pl.multiple_of(t * LANES, LANES), LOC)
            w = jnp.concatenate([w3[t].astype(F32), jnp.zeros((8, LOC), F32)], axis=0)
            for f in range(N_FILT):
                piece = w[f * HALF : f * HALF + 64]
                wx[f * LANES : f * LANES + 64, where] = jnp.where(
                    keep & even, piece, 0.0
                ).astype(BF16)
                wx[f * LANES + 64 : (f + 1) * LANES, where] = jnp.where(
                    keep & ~even, piece, 0.0
                ).astype(BF16)
            return carry

        lax.fori_loop(first, last, body, 0)

    relay = rep < 2 * CHUNKS
    chunk = pl.ds(pl.multiple_of(rep % (2 * CHUNKS) // 2 * RELAY, RELAY), RELAY)
    loads[2].wait()
    ordered(w3s, wxs, 0, 4)

    @pl.when(relay)
    def _():
        pltpu.make_async_copy(a1.at[pl.ds(0, 15)], a1.at[pl.ds(0, 15)], arecv.at[0]).wait()
        a1[rep] = x[chunk]
        xraw[0, chunk] = a1[partner[rep]]
        for i in (4, 3, 5, 2, 6, 1, 7, 0):
            p = (rep + 2 * i) % N_REP
            sb[i] = a1[partner[p]]
            for plane, target in enumerate((h.opp, me)):
                if i > 0 or plane == 0:
                    pltpu.make_async_remote_copy(
                        src_ref=sb.at[i],
                        dst_ref=xraw.at[1 - plane, chunk],
                        send_sem=asend.at[1 + 2 * plane],
                        recv_sem=arecv.at[1 + 2 * plane],
                        device_id={"rep": p, "filt": target},
                        device_id_type=MESH,
                    ).start()

    gx.near()
    ordered(w3s, wxs, 4, 8)
    gx.across()
    ordered(w3s, wxs, 8, 9)
    loads[3].wait()
    ordered(w3t, wxt, 0, 2)

    @pl.when(relay)
    def _():
        pltpu.make_async_copy(
            xraw.at[0, pl.ds(0, RELAY * (CHUNKS - 1))],
            xraw.at[0, pl.ds(0, RELAY * (CHUNKS - 1))],
            arecv.at[3],
        ).wait()

    @pl.when(jnp.logical_not(relay))
    def _():
        pltpu.make_async_copy(xraw.at[0], xraw.at[0], arecv.at[3]).wait()

    xgt[me] = mm(xraw[0], perm).astype(BF16)
    gxt.spread()
    pltpu.make_async_copy(xraw.at[1], xraw.at[1], arecv.at[1]).wait()
    xgt[h.opp] = mm(xraw[1], perm).astype(BF16)
    gxt.spread_opp(0)
    gxt.go(8, h.opp, h.sib)
    ordered(w3t, wxt, 2, 5)

    def conv_half(panel, wx, acc, z, first):
        rows = pl.ds(pl.multiple_of(z * (8 * LANES), 8 * LANES), 8 * LANES)
        left = jnp.concatenate([panel[z * 8 + i] for i in range(8)], axis=1)
        for low in (0, 4, 8):
            where = slice(low * LANES, min(low + 4, 9) * LANES)
            part = mm(left, wx[rows, where])
            acc[:, where] = part if first else acc[:, where] + part

    lanes = lax.broadcasted_iota(jnp.int32, (POS, LANES), 1)
    column = lax.broadcasted_iota(jnp.int32, (POS, LANES), 0) % MAP_W

    def conv_end(acc):
        total = None
        top = jnp.zeros((MAP_W, LANES), F32)

        def tap(t, low, high):
            return acc[low:high, t * LANES : (t + 1) * LANES]

        for b in range(3):
            part = tap(3 + b, 0, POS)
            part = part + jnp.concatenate([top, tap(b, 0, POS - MAP_W)], axis=0)
            part = part + jnp.concatenate([tap(6 + b, MAP_W, POS), top], axis=0)
            if b == 0:
                part = jnp.where(column >= 1, pltpu.roll(part, 1, 0), 0.0)
            if b == 2:
                part = jnp.where(column <= MAP_W - 2, pltpu.roll(part, POS - 1, 0), 0.0)
            total = part if total is None else total + part
        return total

    def hidden_of(pre):
        return jnp.where(lanes < LOC, silu(pre), 0.0).astype(BF16)

    gx.plane()
    conv_half(xg, wxs, accs, h.z, True)
    gxt.near()
    gx.near_opp()
    ordered(w3t, wxt, 5, 9)
    gx.plane_opp()
    conv_half(xg, wxs, accs, 1 - h.z, False)
    gxt.near_opp()
    pre = conv_end(accs)
    hg[me] = hidden_of(pre)
    gh.own()
    gxt.plane()
    conv_half(xgt, wxt, acct, h.z, True)
    gxt.plane_opp()
    conv_half(xgt, wxt, acct, 1 - h.z, False)
    hgt[me] = hidden_of(conv_end(acct))
    ght.own()
    gh.near()
    gh.across()

    for which in range(2):
        loads[4 + which].wait()
        for f in range(N_FILT):
            w1p[which, f * LANES : f * LANES + LOC, :] = w1raw[which, f * LOC : (f + 1) * LOC, :]
            w1p[which, f * LANES + LOC : (f + 1) * LANES, :] = jnp.zeros((LANES - LOC, LOC), BF16)

    for f in range(N_FILT):
        for g in range(2):
            xeo[g * POS : (g + 1) * POS, f * HALF : (f + 1) * HALF] = xg[
                f, :, 64 * g : 64 * g + HALF
            ]
    gh.near_opp()
    ght.near()
    ght.across()
    ght.near_opp()

    def mixed(panel, which, z):
        rows = pl.ds(pl.multiple_of(z * 8 * LANES, 8 * LANES), 8 * LANES)
        left = jnp.concatenate([panel[z * 8 + i] for i in range(8)], axis=1)
        return mm(left, w1p[which, rows, :])

    def logits_of(z, head):
        pooled = jnp.sum(silu(z), axis=0, keepdims=True) * (1.0 / POS)
        parts = mm(split3(pooled), head[...], ((1,), (1,)))
        row[...] = jnp.zeros((1, 1024), F32)
        row[:, :K] = parts[0:1] + parts[1:2] + parts[2:3]
        full = row[...]
        return pooled, jnp.concatenate(
            [full[:, i * LANES : (i + 1) * LANES] for i in range(8)], axis=0
        )

    def give_logits(buf, part, idx):
        buf[me] = part
        for i in (8, 7, 9, 6, 10, 5, 11, 4, 12, 3, 13, 2, 14, 1, 15):
            pltpu.make_async_remote_copy(
                src_ref=buf.at[me],
                dst_ref=buf.at[me],
                send_sem=lsend.at[idx],
                recv_sem=lrecv.at[idx],
                device_id={"rep": rep, "filt": (me + i) % N_FILT},
                device_id_type=MESH,
            ).start()

    def wait_bytes(buf, count, sem):
        pltpu.make_async_copy(buf.at[pl.ds(0, count)], buf.at[pl.ds(0, count)], sem).wait()

    def sum_logits(buf, idx):
        wait_bytes(buf, N_FILT - 1, lrecv.at[idx])
        return jnp.sum(buf[...], axis=0)

    loads[6].wait()
    loads[7].wait()
    ght.plane()
    zt = xraw[0].astype(F32) + mixed(hgt, 1, h.z)
    ght.plane_opp()
    part = logits_of(zt + mixed(hgt, 1, 1 - h.z), hdt)[1]
    give_logits(lt, part, 1)
    gh.plane()
    gh.plane_opp()
    z_mixed = x[...].astype(F32) + mixed(hg, 0, h.z) + mixed(hg, 0, 1 - h.z)
    pooled, part = logits_of(z_mixed, hds)
    give_logits(ls, part, 0)
    ua[rep] = sum_logits(lt, 1)
    for i in range(1, N_REP):
        pltpu.make_async_remote_copy(
            src_ref=ua.at[rep],
            dst_ref=ua.at[rep],
            send_sem=asend.at[2],
            recv_sem=arecv.at[2],
            device_id={"rep": (rep + i) % N_REP, "filt": me},
            device_id_type=MESH,
        ).start()
    slope = dsilu(z_mixed) * (1.0 / POS)
    logits = sum_logits(ls, 0)

    cls = lax.broadcasted_iota(jnp.int32, (8, LANES), 0) * LANES + lax.broadcasted_iota(
        jnp.int32, (8, LANES), 1
    )
    real = cls < K

    def softmax(v):
        top = jnp.max(jnp.where(real, v, -jnp.inf))
        e = jnp.where(real, jnp.exp(v - top), 0.0)
        return e / jnp.sum(e)

    own_part = 2.0 * softmax(logits) - jnp.where(cls == label[0], 1.0, 0.0)
    wait_bytes(ua, N_REP - 1, arecv.at[2])
    dl = own_part - softmax(ua[partner[rep]])
    dl_row = jnp.concatenate([dl[i : i + 1, :] for i in range(8)], axis=1)[:, :K]
    parts = mm(split3(dl_row), hds[...])
    dz = ((parts[0:1] + parts[1:2] + parts[2:3]) * slope).astype(BF16)

    def remote(src, dst, kind, target):
        return pltpu.make_async_remote_copy(
            src_ref=src,
            dst_ref=dst,
            send_sem=rsend.at[kind],
            recv_sem=rrecv.at[kind],
            device_id={"rep": rep, "filt": target},
            device_id_type=MESH,
        )

    zz = 1 - h.z
    mine_at = pl.ds(pl.multiple_of(h.k * LANES, LANES), LANES)
    other_at = pl.ds(pl.multiple_of((1 - h.k) * LANES, LANES), LANES)
    places = (h.beyond, h.up, h.down, h.y)
    sib_copies = []
    for i, z in enumerate((zz, h.z)):
        rows = pl.ds(pl.multiple_of(z * 8 * LANES, 8 * LANES), 8 * LANES)
        part = mm(dz, w1p[0, rows, :], ((1,), (1,)))
        for y in range(4):
            block[i * 4 + y] = part[:, y * 2 * LANES : (y + 1) * 2 * LANES]
        for j, y in enumerate(places):
            sendb[i * 4 + j] = block[i * 4 + y, :, other_at].astype(BF16)
            made = remote(sendb.at[i * 4 + j], ra.at[i * 4 + j], i * 4 + j, h.sib)
            made.start()
            sib_copies.append(made)

    mid = POS // 2
    halves = (slice(0, mid), slice(mid, POS))

    def chip_sum(i, j, rows):
        return block[i * 4 + places[j], rows, mine_at] + ra[i * 4 + j, rows].astype(F32)

    side = [h.at(h.z, y, h.k) for y in places[:3]]
    across = []
    for half, rows in enumerate(halves):
        for j in range(3):
            if half == 0:
                sib_copies[j].wait_recv()
            sendb[8 + j, rows] = chip_sum(0, j, rows).astype(BF16)
            made = remote(sendb.at[8 + j, rows], rb.at[j, rows], 8 + half * 3 + j, side[j])
            made.start()
            across.append(made)
    for j in range(3):
        sib_copies[4 + j].wait_recv()
        sendb[11 + j] = chip_sum(1, j, slice(0, POS)).astype(BF16)
        made = remote(sendb.at[11 + j], rb.at[3 + j], 14 + j, side[j])
        made.start()
        across.append(made)
    sib_copies[3].wait_recv()
    last = []
    for half, rows in enumerate(halves):
        total = chip_sum(0, 3, rows)
        for j in (1, 2, 0):
            across[half * 3 + j].wait_recv()
            total = total + rb[j, rows].astype(F32)
        sendb[14, rows] = total.astype(BF16)
        made = remote(sendb.at[14, rows], rc.at[rows], 17 + half, h.opp)
        made.start()
        last.append(made)
    sib_copies[7].wait_recv()
    mine = chip_sum(1, 3, slice(0, POS))
    for j in (1, 2, 0):
        across[6 + j].wait_recv()
        mine = mine + rb[3 + j].astype(F32)
    for f in range(N_FILT):
        hc[:, f * LOC : (f + 1) * LOC] = hg[f, :, :LOC]
    gw1_out[...] = mm(dz, hc[...], ((0,), (0,)))
    flip = dl.T
    for i in range(8):
        size = min(LANES, K - i * LANES)
        gh_out[i * LANES : i * LANES + size, :] = flip[:size, i : i + 1] * pooled
    slope = dsilu(pre)
    for made in last:
        made.wait_recv()
    dhidden = mine + rc[...].astype(F32)
    dpre_out[...] = (dhidden * slope)[:, :LOC].astype(BF16)

    for gather in (gx, gxt, gh, ght):
        gather.drain()
    for made in sib_copies + across + last:
        made.wait_send()
    wait_bytes(ls, N_FILT - 1, lsend.at[0])
    wait_bytes(lt, N_FILT - 1, lsend.at[1])
    wait_bytes(ua, N_REP - 1, asend.at[2])

    @pl.when(relay)
    def _():
        wait_bytes(sb, 2 * CHUNKS - 1, asend.at[0])
        wait_bytes(sb, 8, asend.at[1])
        wait_bytes(sb, 7, asend.at[3])

    @pl.when(jnp.logical_not(relay))
    def _():
        wait_bytes(sb, 2 * CHUNKS, asend.at[0])


def grads_kernel(xeo, dpre, r1, r0, gw3, gw1, gh, turned, r3, sem):
    copies = []

    def out(src, dst, i):
        made = pltpu.make_async_copy(src, dst, sem.at[i])
        made.start()
        copies.append(made)

    out(r1, gw1.at[:, 0, :], 9)
    out(r0, gh, 10)
    dp = dpre[...].astype(F32)
    even = lax.broadcasted_iota(jnp.int32, (POS, LOC), 1) % 2 == 0
    column = lax.broadcasted_iota(jnp.int32, (POS, LOC), 0) % MAP_W
    zero = jnp.zeros((MAP_W, LOC), F32)
    for b in (1, 0, 2):
        moved = dp
        if b == 0:
            moved = pltpu.roll(jnp.where(column >= 1, dp, 0.0), POS - 1, 0)
        if b == 2:
            moved = pltpu.roll(jnp.where(column <= MAP_W - 2, dp, 0.0), 1, 0)
        for a in range(3):
            d = moved
            if a == 0:
                d = jnp.concatenate([moved[MAP_W:], zero], axis=0)
            if a == 2:
                d = jnp.concatenate([zero, moved[: POS - MAP_W]], axis=0)
            where = slice(a * LANES, a * LANES + LOC)
            turned[b, :POS, where] = jnp.where(even, d, 0.0).astype(BF16)
            turned[b, POS:, where] = jnp.where(even, 0.0, d).astype(BF16)
        rows = mm(turned[b], xeo[...], ((0,), (0,)))
        for a in range(3):
            t = 3 * a + b
            r3[t] = rows[a * LANES : a * LANES + LOC]
            out(r3.at[t], gw3.at[:, t, 0, :], t)
    for made in copies:
        made.wait()


def per_device(
    images, labels, partner, student_w3, student_w1, student_head, stale_w3, stale_w1, stale_head
):
    vmem = pl.BlockSpec(memory_space=pltpu.VMEM)
    hbm = pl.BlockSpec(memory_space=pltpu.HBM)
    sds = jax.ShapeDtypeStruct
    dma = pltpu.SemaphoreType.DMA
    weights = []
    for w3, w1, head in (
        (student_w3, student_w1, student_head),
        (stale_w3, stale_w1, stale_head),
    ):
        weights += [w3[0].transpose(1, 2, 0), w1[0].T, head[0].T]
    saved = pl.pallas_call(
        main_kernel,
        out_shape=(
            pltpu.VMEM((2 * POS, GW), BF16),
            pltpu.VMEM((POS, LOC), BF16),
            pltpu.VMEM((LOC, C), F32),
            pltpu.VMEM((K, LOC), F32),
        ),
        in_specs=[pl.BlockSpec(memory_space=pltpu.SMEM)] + [hbm] * 8,
        out_specs=[vmem] * 4,
        scratch_shapes=[
            pltpu.SMEM((N_REP,), jnp.int32),
            pltpu.VMEM((POS, LOC), BF16),
            pltpu.VMEM((2, POS, LOC), BF16),
            pltpu.VMEM((POS, C), BF16),
            pltpu.VMEM((9, GW, LOC), BF16),
            pltpu.VMEM((9, GW, LOC), BF16),
            pltpu.VMEM((N_FILT * LANES, 9 * LANES), BF16),
            pltpu.VMEM((N_FILT * LANES, 9 * LANES), BF16),
            pltpu.VMEM((2, C, LOC), BF16),
            pltpu.VMEM((2, N_FILT * LANES, LOC), BF16),
            pltpu.VMEM((K, LOC), BF16),
            pltpu.VMEM((K, LOC), BF16),
            pltpu.VMEM((N_FILT, POS, LANES), BF16),
            pltpu.VMEM((N_FILT, POS, LANES), BF16),
            pltpu.VMEM((N_FILT, POS, LANES), BF16),
            pltpu.VMEM((N_FILT, POS, LANES), BF16),
            pltpu.VMEM((POS, 9 * LANES), F32),
            pltpu.VMEM((POS, 9 * LANES), F32),
            pltpu.VMEM((N_REP, RELAY, LOC), BF16),
            pltpu.VMEM((N_REP, RELAY, LOC), BF16),
            pltpu.VMEM((N_FILT, 8, LANES), F32),
            pltpu.VMEM((N_FILT, 8, LANES), F32),
            pltpu.VMEM((N_REP, 8, LANES), F32),
            pltpu.VMEM((1, 1024), F32),
            pltpu.VMEM((15, POS, LANES), BF16),
            pltpu.VMEM((8, POS, 2 * LANES), F32),
            pltpu.VMEM((8, POS, LANES), BF16),
            pltpu.VMEM((6, POS, LANES), BF16),
            pltpu.VMEM((POS, LANES), BF16),
            dma((8,)),
            dma((4, 19)),
            dma((4, 19)),
            dma((4,)),
            dma((4,)),
            dma((2,)),
            dma((2,)),
            dma((19,)),
            dma((19,)),
        ],
        compiler_params=pltpu.CompilerParams(
            collective_id=0, has_side_effects=True, vmem_limit_bytes=48 * 1024 * 1024
        ),
        name="step",
    )(
        labels,
        *(
            pltpu.with_memory_space_constraint(a, pltpu.HBM)
            for a in (partner, images.transpose(1, 2, 0)[0], *weights)
        ),
    )
    gw3, gw1, gh = pl.pallas_call(
        grads_kernel,
        out_shape=(
            sds((LOC, 9, 1, GW), F32),
            sds((LOC, 1, C), F32),
            sds((K, LOC), F32),
        ),
        in_specs=[vmem] * 4,
        out_specs=[hbm] * 3,
        scratch_shapes=[
            pltpu.VMEM((3, 2 * POS, 3 * LANES), BF16),
            pltpu.VMEM((9, LOC, GW), F32),
            dma((11,)),
        ],
        compiler_params=pltpu.CompilerParams(vmem_limit_bytes=40 * 1024 * 1024),
        name="grads",
    )(*saved)
    return (gw3.transpose(2, 0, 1, 3), gw1.transpose(1, 0, 2), gh.T[None])


def solution(mesh):
    in_specs = (
        P("filt", "rep", None),
        P("rep"),
        P(),
        P("rep", "filt", None, None),
        P("rep", "filt", None),
        P("rep", "filt", None),
        P("rep", "filt", None, None),
        P("rep", "filt", None),
        P("rep", "filt", None),
    )
    out_specs = (P("rep", "filt", None, None), P("rep", "filt", None), P("rep", "filt", None))
    return jax.shard_map(
        per_device, mesh=mesh, in_specs=in_specs, out_specs=out_specs, check_vma=False
    )
```

```python
import functools

import jax
import jax.numpy as jnp
from jax import lax
from jax.experimental import pallas as pl
from jax.experimental.pallas import tpu as pltpu
from jax.sharding import PartitionSpec as P

C = 2016
GW = 1008
K = 1000
ROWS = 4
MAP_W = 56
POS = ROWS * MAP_W
N_REP = 16
N_FILT = 16
LOC = C // N_FILT
HALF = LOC // 2
RELAY = 32
CHUNKS = POS // RELAY
LANES = 128
F32 = jnp.float32
BF16 = jnp.bfloat16
MESH = pl.DeviceIdType.MESH


def mm(a, b, dims=((1,), (0,))):
    return lax.dot_general(a, b, (dims, ((), ())), preferred_element_type=F32)


def silu(v):
    return v / (1.0 + jnp.exp(-v))


def dsilu(v):
    sig = 1.0 / (1.0 + jnp.exp(-v))
    return sig * (1.0 + v * (1.0 - sig))


def split3(v):
    hi = v.astype(BF16)
    rest = v - hi.astype(F32)
    mid = rest.astype(BF16)
    low = (rest - mid.astype(F32)).astype(BF16)
    pad = jnp.zeros((13,) + v.shape[1:], BF16)
    return jnp.concatenate([hi, mid, low, pad], axis=0)


class Gather:
    def __init__(self, panel, send, recv, here, parts=1, both=False):
        self.panel, self.send, self.recv, self.here = panel, send, recv, here
        self.parts = parts
        self.both = both
        self.started = []

    def copy(self, kind, slot, target, part=None):
        where = self.panel.at[slot]
        if part is not None and self.parts > 1:
            size = POS // self.parts
            where = self.panel.at[slot, pl.ds(part * size, size)]
            kind = kind if part == 0 else 15 + (0, 3, 4, 6, 11, 12, 14).index(kind)
        return pltpu.make_async_remote_copy(
            src_ref=where,
            dst_ref=where,
            send_sem=self.send.at[kind],
            recv_sem=self.recv.at[kind],
            device_id={"rep": self.here.rep, "filt": target},
            device_id_type=MESH,
        )

    def go(self, kind, slot, target, part=None):
        made = self.copy(kind, slot, target, part)
        made.start()
        self.started.append(made)

    def got(self, kind, slot, part=None):
        self.copy(kind, slot, self.here.sib, part).wait_recv()

    def own(self):
        for part in range(self.parts):
            self.go(0, self.here.me, self.here.opp, part)
        self.spread()

    def spread(self):
        h = self.here
        self.go(1, h.me, h.right)
        self.go(2, h.me, h.left)
        self.go(5, h.me, h.far)
        self.go(7, h.me, h.sib)

    def across(self):
        for part in range(self.parts):
            self.got(0, self.here.opp, part)
            self.spread_opp(part)
        self.go(8, self.here.opp, self.here.sib)

    def spread_opp(self, part):
        h = self.here
        self.go(3, h.opp, h.right, part)
        self.go(4, h.opp, h.left, part)
        self.go(6, h.opp, h.far, part)
        if self.both:
            self.go(11, h.opp, h.other(h.right), part)
            self.go(12, h.opp, h.other(h.left), part)
            self.go(14, h.opp, h.other(h.far), part)

    def near(self):
        h = self.here
        for kind, slot, onward in ((1, h.left, 9), (2, h.right, 10), (5, h.far, 13)):
            self.got(kind, slot)
            self.go(onward, slot, h.sib)

    def near_opp(self):
        h = self.here
        for kind, slot, onward in ((3, h.left_opp, 11), (4, h.right_opp, 12), (6, h.far_opp, 14)):
            for part in range(self.parts):
                self.got(kind, slot, part)
            if not self.both:
                self.go(onward, slot, h.sib)

    def plane(self):
        h = self.here
        self.got(7, h.sib)
        self.got(9, h.other(h.left))
        self.got(10, h.other(h.right))
        self.got(13, h.other(h.far))

    def plane_opp(self):
        h = self.here
        self.got(8, h.other(h.opp))
        for kind, slot in ((11, h.left_opp), (12, h.right_opp), (14, h.far_opp)):
            for part in range(self.parts) if self.both else (None,):
                self.got(kind, h.other(slot), part)

    def drain(self):
        for made in self.started:
            made.wait_send()


class Here:
    def __init__(self):
        self.rep = lax.axis_index("rep")
        self.me = lax.axis_index("filt")
        self.z = self.me // 8
        self.y = (self.me % 8) // 2
        self.k = self.me % 2
        self.up = (self.y + 1) % 4
        self.down = (self.y + 3) % 4
        self.beyond = (self.y + 2) % 4
        self.sib = self.at(self.z, self.y, 1 - self.k)
        self.opp = self.at(1 - self.z, self.y, self.k)
        self.right = self.at(self.z, self.up, self.k)
        self.left = self.at(self.z, self.down, self.k)
        self.far = self.at(self.z, self.beyond, self.k)
        self.right_opp = self.at(1 - self.z, self.up, self.k)
        self.left_opp = self.at(1 - self.z, self.down, self.k)
        self.far_opp = self.at(1 - self.z, self.beyond, self.k)

    def at(self, z, y, k):
        return z * 8 + y * 2 + k

    def other(self, slot):
        return slot + 1 - 2 * (slot % 2)


def main_kernel(
    label, partner_h, x_h, w3s_h, w1s_h, hds_h, w3t_h, w1t_h, hdt_h,
    xeo, dpre_out, gw1_out, gh_out,
    partner, x, xraw, hc, w3s, w3t, wxs, wxt, w1raw, w1p, hds, hdt, xg, xgt, hg, hgt, accs, acct,
    a1, sb, ls, lt, ua, row, sendb, block, ra, rb, rc,
    wsem, gsend, grecv, asend, arecv, lsend, lrecv, rsend, rrecv,
):
    h = Here()
    rep, me = h.rep, h.me

    loads = [
        pltpu.make_async_copy(src, dst, wsem.at[i])
        for i, (src, dst) in enumerate(
            (
                (x_h, x),
                (partner_h, partner),
                (w3s_h, w3s),
                (w3t_h, w3t),
                (w1s_h, w1raw.at[0]),
                (w1t_h, w1raw.at[1]),
                (hds_h, hds),
                (hdt_h, hdt),
            )
        )
    ]
    for load in loads[:2]:
        load.start()
    barrier = pltpu.get_barrier_semaphore()
    for i in range(1, N_REP):
        pl.semaphore_signal(
            barrier, inc=1, device_id={"rep": (rep + i) % N_REP, "filt": me}, device_id_type=MESH
        )
    for i in range(1, N_FILT):
        pl.semaphore_signal(
            barrier, inc=1, device_id={"rep": rep, "filt": (me + i) % N_FILT}, device_id_type=MESH
        )

    for load in loads[2:]:
        load.start()

    lane_from = lax.broadcasted_iota(jnp.int32, (LOC, LANES), 0)
    lane_to = lax.broadcasted_iota(jnp.int32, (LOC, LANES), 1)
    inside = lane_to % 64
    perm = jnp.where((inside < HALF) & (lane_from == 2 * inside + lane_to // 64), 1.0, 0.0)
    perm = perm.astype(BF16)
    pl.semaphore_wait(barrier, N_REP - 1 + N_FILT - 1)

    gx = Gather(xg, gsend.at[0], grecv.at[0], h, 2)
    gxt = Gather(xgt, gsend.at[1], grecv.at[1], h, 1, True)
    gh = Gather(hg, gsend.at[2], grecv.at[2], h, 2)
    ght = Gather(hgt, gsend.at[3], grecv.at[3], h, 2, True)

    for i in range(1, N_REP):
        q = (rep + i) % N_REP

        @pl.when(q < 2 * CHUNKS)
        def _():
            pltpu.make_async_remote_copy(
                src_ref=x_h.at[pl.ds(pl.multiple_of(q // 2 * RELAY, RELAY), RELAY)],
                dst_ref=a1.at[rep],
                send_sem=asend.at[0],
                recv_sem=arecv.at[0],
                device_id={"rep": q, "filt": me},
                device_id_type=MESH,
            ).start()

    loads[0].wait()
    xg[me] = mm(x[...], perm).astype(BF16)
    gx.own()
    loads[1].wait()

    def ordered(w3, wx, first, last):
        keep = lax.broadcasted_iota(jnp.int32, (64, LOC), 0) < HALF
        even = lax.broadcasted_iota(jnp.int32, (64, LOC), 1) % 2 == 0

        def body(t, carry):
            where = pl.ds(pl.multiple_of(t * LANES, LANES), LOC)
            w = jnp.concatenate([w3[t].astype(F32), jnp.zeros((8, LOC), F32)], axis=0)
            for f in range(N_FILT):
                piece = w[f * HALF : f * HALF + 64]
                wx[f * LANES : f * LANES + 64, where] = jnp.where(
                    keep & even, piece, 0.0
                ).astype(BF16)
                wx[f * LANES + 64 : (f + 1) * LANES, where] = jnp.where(
                    keep & ~even, piece, 0.0
                ).astype(BF16)
            return carry

        lax.fori_loop(first, last, body, 0)

    relay = rep < 2 * CHUNKS
    chunk = pl.ds(pl.multiple_of(rep % (2 * CHUNKS) // 2 * RELAY, RELAY), RELAY)
    loads[2].wait()
    ordered(w3s, wxs, 0, 4)

    @pl.when(relay)
    def _():
        pltpu.make_async_copy(a1.at[pl.ds(0, 15)], a1.at[pl.ds(0, 15)], arecv.at[0]).wait()
        a1[rep] = x[chunk]
        xraw[0, chunk] = a1[partner[rep]]
        for i in (4, 3, 5, 2, 6, 1, 7, 0):
            p = (rep + 2 * i) % N_REP
            sb[i] = a1[partner[p]]
            for plane, target in enumerate((h.opp, me)):
                if i > 0 or plane == 0:
                    pltpu.make_async_remote_copy(
                        src_ref=sb.at[i],
                        dst_ref=xraw.at[1 - plane, chunk],
                        send_sem=asend.at[1 + 2 * plane],
                        recv_sem=arecv.at[1 + 2 * plane],
                        device_id={"rep": p, "filt": target},
                        device_id_type=MESH,
                    ).start()

    gx.near()
    ordered(w3s, wxs, 4, 8)
    gx.across()
    ordered(w3s, wxs, 8, 9)
    loads[3].wait()
    ordered(w3t, wxt, 0, 2)

    @pl.when(relay)
    def _():
        pltpu.make_async_copy(
            xraw.at[0, pl.ds(0, RELAY * (CHUNKS - 1))],
            xraw.at[0, pl.ds(0, RELAY * (CHUNKS - 1))],
            arecv.at[3],
        ).wait()

    @pl.when(jnp.logical_not(relay))
    def _():
        pltpu.make_async_copy(xraw.at[0], xraw.at[0], arecv.at[3]).wait()

    xgt[me] = mm(xraw[0], perm).astype(BF16)
    gxt.spread()
    pltpu.make_async_copy(xraw.at[1], xraw.at[1], arecv.at[1]).wait()
    xgt[h.opp] = mm(xraw[1], perm).astype(BF16)
    gxt.spread_opp(0)
    gxt.go(8, h.opp, h.sib)
    ordered(w3t, wxt, 2, 5)

    def conv_half(panel, wx, acc, z, first):
        rows = pl.ds(pl.multiple_of(z * (8 * LANES), 8 * LANES), 8 * LANES)
        left = jnp.concatenate([panel[z * 8 + i] for i in range(8)], axis=1)
        for low in (0, 4, 8):
            where = slice(low * LANES, min(low + 4, 9) * LANES)
            part = mm(left, wx[rows, where])
            acc[:, where] = part if first else acc[:, where] + part

    lanes = lax.broadcasted_iota(jnp.int32, (POS, LANES), 1)
    column = lax.broadcasted_iota(jnp.int32, (POS, LANES), 0) % MAP_W

    def conv_end(acc):
        total = None
        top = jnp.zeros((MAP_W, LANES), F32)

        def tap(t, low, high):
            return acc[low:high, t * LANES : (t + 1) * LANES]

        for b in range(3):
            part = tap(3 + b, 0, POS)
            part = part + jnp.concatenate([top, tap(b, 0, POS - MAP_W)], axis=0)
            part = part + jnp.concatenate([tap(6 + b, MAP_W, POS), top], axis=0)
            if b == 0:
                part = jnp.where(column >= 1, pltpu.roll(part, 1, 0), 0.0)
            if b == 2:
                part = jnp.where(column <= MAP_W - 2, pltpu.roll(part, POS - 1, 0), 0.0)
            total = part if total is None else total + part
        return total

    def hidden_of(pre):
        return jnp.where(lanes < LOC, silu(pre), 0.0).astype(BF16)

    gx.plane()
    conv_half(xg, wxs, accs, h.z, True)
    gxt.near()
    gx.near_opp()
    ordered(w3t, wxt, 5, 9)
    gx.plane_opp()
    conv_half(xg, wxs, accs, 1 - h.z, False)
    gxt.near_opp()
    pre = conv_end(accs)
    hg[me] = hidden_of(pre)
    gh.own()
    gxt.plane()
    conv_half(xgt, wxt, acct, h.z, True)
    gxt.plane_opp()
    conv_half(xgt, wxt, acct, 1 - h.z, False)
    hgt[me] = hidden_of(conv_end(acct))
    ght.own()
    gh.near()
    gh.across()

    for which in range(2):
        loads[4 + which].wait()
        for f in range(N_FILT):
            w1p[which, f * LANES : f * LANES + LOC, :] = w1raw[which, f * LOC : (f + 1) * LOC, :]
            w1p[which, f * LANES + LOC : (f + 1) * LANES, :] = jnp.zeros((LANES - LOC, LOC), BF16)

    gh.near_opp()
    ght.near()
    ght.across()
    gh.plane()
    gh.plane_opp()
    ght.near_opp()

    def whole(panel):
        return jnp.concatenate([panel[i] for i in range(N_FILT)], axis=1)

    def logits_of(z, head):
        pooled = jnp.sum(silu(z), axis=0, keepdims=True) * (1.0 / POS)
        parts = mm(split3(pooled), head[...], ((1,), (1,)))
        row[...] = jnp.zeros((1, 1024), F32)
        row[:, :K] = parts[0:1] + parts[1:2] + parts[2:3]
        full = row[...]
        return pooled, jnp.concatenate(
            [full[:, i * LANES : (i + 1) * LANES] for i in range(8)], axis=0
        )

    def give_logits(buf, part, idx):
        buf[me] = part
        for i in (8, 7, 9, 6, 10, 5, 11, 4, 12, 3, 13, 2, 14, 1, 15):
            pltpu.make_async_remote_copy(
                src_ref=buf.at[me],
                dst_ref=buf.at[me],
                send_sem=lsend.at[idx],
                recv_sem=lrecv.at[idx],
                device_id={"rep": rep, "filt": (me + i) % N_FILT},
                device_id_type=MESH,
            ).start()

    def wait_bytes(buf, count, sem):
        pltpu.make_async_copy(buf.at[pl.ds(0, count)], buf.at[pl.ds(0, count)], sem).wait()

    def sum_logits(buf, idx):
        wait_bytes(buf, N_FILT - 1, lrecv.at[idx])
        return jnp.sum(buf[...], axis=0)

    loads[6].wait()
    loads[7].wait()
    z_mixed = x[...].astype(F32) + mm(whole(hg), w1p[0])
    pooled, part = logits_of(z_mixed, hds)
    give_logits(ls, part, 0)
    xt = xraw[0].astype(F32)
    ght.plane()
    ght.plane_opp()
    part = logits_of(xt + mm(whole(hgt), w1p[1]), hdt)[1]
    give_logits(lt, part, 1)
    for f in range(N_FILT):
        hc[:, f * LOC : (f + 1) * LOC] = hg[f, :, :LOC]
    logits = sum_logits(ls, 0)

    cls = lax.broadcasted_iota(jnp.int32, (8, LANES), 0) * LANES + lax.broadcasted_iota(
        jnp.int32, (8, LANES), 1
    )
    real = cls < K

    def softmax(v):
        top = jnp.max(jnp.where(real, v, -jnp.inf))
        e = jnp.where(real, jnp.exp(v - top), 0.0)
        return e / jnp.sum(e)

    own_part = 2.0 * softmax(logits) - jnp.where(cls == label[0], 1.0, 0.0)
    slope = dsilu(z_mixed) * (1.0 / POS)
    ua[rep] = sum_logits(lt, 1)
    for i in range(1, N_REP):
        pltpu.make_async_remote_copy(
            src_ref=ua.at[rep],
            dst_ref=ua.at[rep],
            send_sem=asend.at[2],
            recv_sem=arecv.at[2],
            device_id={"rep": (rep + i) % N_REP, "filt": me},
            device_id_type=MESH,
        ).start()
    for f in range(N_FILT):
        for g in range(2):
            xeo[g * POS : (g + 1) * POS, f * HALF : (f + 1) * HALF] = xg[
                f, :, 64 * g : 64 * g + HALF
            ]
    wait_bytes(ua, N_REP - 1, arecv.at[2])
    dl = own_part - softmax(ua[partner[rep]])
    dl_row = jnp.concatenate([dl[i : i + 1, :] for i in range(8)], axis=1)[:, :K]
    parts = mm(split3(dl_row), hds[...])
    dz = ((parts[0:1] + parts[1:2] + parts[2:3]) * slope).astype(BF16)

    def remote(src, dst, kind, target):
        return pltpu.make_async_remote_copy(
            src_ref=src,
            dst_ref=dst,
            send_sem=rsend.at[kind],
            recv_sem=rrecv.at[kind],
            device_id={"rep": rep, "filt": target},
            device_id_type=MESH,
        )

    zz = 1 - h.z
    mine_at = pl.ds(pl.multiple_of(h.k * LANES, LANES), LANES)
    other_at = pl.ds(pl.multiple_of((1 - h.k) * LANES, LANES), LANES)
    places = (h.beyond, h.up, h.down, h.y)
    sib_copies = []
    for i, z in enumerate((zz, h.z)):
        rows = pl.ds(pl.multiple_of(z * 8 * LANES, 8 * LANES), 8 * LANES)
        part = mm(dz, w1p[0, rows, :], ((1,), (1,)))
        for y in range(4):
            block[i * 4 + y] = part[:, y * 2 * LANES : (y + 1) * 2 * LANES]
        for j, y in enumerate(places):
            sendb[i * 4 + j] = block[i * 4 + y, :, other_at].astype(BF16)
            made = remote(sendb.at[i * 4 + j], ra.at[i * 4 + j], i * 4 + j, h.sib)
            made.start()
            sib_copies.append(made)

    mid = POS // 2
    halves = (slice(0, mid), slice(mid, POS))

    def chip_sum(i, j, rows):
        return block[i * 4 + places[j], rows, mine_at] + ra[i * 4 + j, rows].astype(F32)

    side = [h.at(h.z, y, h.k) for y in places[:3]]
    across = []
    for half, rows in enumerate(halves):
        for j in range(3):
            if half == 0:
                sib_copies[j].wait_recv()
            sendb[8 + j, rows] = chip_sum(0, j, rows).astype(BF16)
            made = remote(sendb.at[8 + j, rows], rb.at[j, rows], 8 + half * 3 + j, side[j])
            made.start()
            across.append(made)
    for j in range(3):
        sib_copies[4 + j].wait_recv()
        sendb[11 + j] = chip_sum(1, j, slice(0, POS)).astype(BF16)
        made = remote(sendb.at[11 + j], rb.at[3 + j], 14 + j, side[j])
        made.start()
        across.append(made)
    sib_copies[3].wait_recv()
    last = []
    for half, rows in enumerate(halves):
        total = chip_sum(0, 3, rows)
        for j in (1, 2, 0):
            across[half * 3 + j].wait_recv()
            total = total + rb[j, rows].astype(F32)
        sendb[14, rows] = total.astype(BF16)
        made = remote(sendb.at[14, rows], rc.at[rows], 17 + half, h.opp)
        made.start()
        last.append(made)
    sib_copies[7].wait_recv()
    mine = chip_sum(1, 3, slice(0, POS))
    for j in (1, 2, 0):
        across[6 + j].wait_recv()
        mine = mine + rb[3 + j].astype(F32)
    gw1_out[...] = mm(dz, hc[...], ((0,), (0,)))
    flip = dl.T
    for i in range(8):
        size = min(LANES, K - i * LANES)
        gh_out[i * LANES : i * LANES + size, :] = flip[:size, i : i + 1] * pooled
    slope = dsilu(pre)
    for made in last:
        made.wait_recv()
    dhidden = mine + rc[...].astype(F32)
    dpre_out[...] = (dhidden * slope)[:, :LOC].astype(BF16)

    for gather in (gx, gxt, gh, ght):
        gather.drain()
    for made in sib_copies + across + last:
        made.wait_send()
    wait_bytes(ls, N_FILT - 1, lsend.at[0])
    wait_bytes(lt, N_FILT - 1, lsend.at[1])
    wait_bytes(ua, N_REP - 1, asend.at[2])

    @pl.when(relay)
    def _():
        wait_bytes(sb, 2 * CHUNKS - 1, asend.at[0])
        wait_bytes(sb, 8, asend.at[1])
        wait_bytes(sb, 7, asend.at[3])

    @pl.when(jnp.logical_not(relay))
    def _():
        wait_bytes(sb, 2 * CHUNKS, asend.at[0])


def grads_kernel(xeo, dpre, r1, r0, gw3, gw1, gh, turned, r3, sem):
    copies = []

    def out(src, dst, i):
        made = pltpu.make_async_copy(src, dst, sem.at[i])
        made.start()
        copies.append(made)

    out(r1, gw1.at[:, 0, :], 9)
    out(r0, gh, 10)
    dp = dpre[...].astype(F32)
    even = lax.broadcasted_iota(jnp.int32, (POS, LOC), 1) % 2 == 0
    column = lax.broadcasted_iota(jnp.int32, (POS, LOC), 0) % MAP_W
    zero = jnp.zeros((MAP_W, LOC), F32)
    for b in (1, 0, 2):
        moved = dp
        if b == 0:
            moved = pltpu.roll(jnp.where(column >= 1, dp, 0.0), POS - 1, 0)
        if b == 2:
            moved = pltpu.roll(jnp.where(column <= MAP_W - 2, dp, 0.0), 1, 0)
        for a in range(3):
            d = moved
            if a == 0:
                d = jnp.concatenate([moved[MAP_W:], zero], axis=0)
            if a == 2:
                d = jnp.concatenate([zero, moved[: POS - MAP_W]], axis=0)
            where = slice(a * LANES, a * LANES + LOC)
            turned[b, :POS, where] = jnp.where(even, d, 0.0).astype(BF16)
            turned[b, POS:, where] = jnp.where(even, 0.0, d).astype(BF16)
        rows = mm(turned[b], xeo[...], ((0,), (0,)))
        for a in range(3):
            t = 3 * a + b
            r3[t] = rows[a * LANES : a * LANES + LOC]
            out(r3.at[t], gw3.at[:, t, 0, :], t)
    for made in copies:
        made.wait()


def per_device(
    images, labels, partner, student_w3, student_w1, student_head, stale_w3, stale_w1, stale_head
):
    vmem = pl.BlockSpec(memory_space=pltpu.VMEM)
    hbm = pl.BlockSpec(memory_space=pltpu.HBM)
    sds = jax.ShapeDtypeStruct
    dma = pltpu.SemaphoreType.DMA
    weights = []
    for w3, w1, head in (
        (student_w3, student_w1, student_head),
        (stale_w3, stale_w1, stale_head),
    ):
        weights += [w3[0].transpose(1, 2, 0), w1[0].T, head[0].T]
    saved = pl.pallas_call(
        main_kernel,
        out_shape=(
            pltpu.VMEM((2 * POS, GW), BF16),
            pltpu.VMEM((POS, LOC), BF16),
            pltpu.VMEM((LOC, C), F32),
            pltpu.VMEM((K, LOC), F32),
        ),
        in_specs=[pl.BlockSpec(memory_space=pltpu.SMEM)] + [hbm] * 8,
        out_specs=[vmem] * 4,
        scratch_shapes=[
            pltpu.SMEM((N_REP,), jnp.int32),
            pltpu.VMEM((POS, LOC), BF16),
            pltpu.VMEM((2, POS, LOC), BF16),
            pltpu.VMEM((POS, C), BF16),
            pltpu.VMEM((9, GW, LOC), BF16),
            pltpu.VMEM((9, GW, LOC), BF16),
            pltpu.VMEM((N_FILT * LANES, 9 * LANES), BF16),
            pltpu.VMEM((N_FILT * LANES, 9 * LANES), BF16),
            pltpu.VMEM((2, C, LOC), BF16),
            pltpu.VMEM((2, N_FILT * LANES, LOC), BF16),
            pltpu.VMEM((K, LOC), BF16),
            pltpu.VMEM((K, LOC), BF16),
            pltpu.VMEM((N_FILT, POS, LANES), BF16),
            pltpu.VMEM((N_FILT, POS, LANES), BF16),
            pltpu.VMEM((N_FILT, POS, LANES), BF16),
            pltpu.VMEM((N_FILT, POS, LANES), BF16),
            pltpu.VMEM((POS, 9 * LANES), F32),
            pltpu.VMEM((POS, 9 * LANES), F32),
            pltpu.VMEM((N_REP, RELAY, LOC), BF16),
            pltpu.VMEM((N_REP, RELAY, LOC), BF16),
            pltpu.VMEM((N_FILT, 8, LANES), F32),
            pltpu.VMEM((N_FILT, 8, LANES), F32),
            pltpu.VMEM((N_REP, 8, LANES), F32),
            pltpu.VMEM((1, 1024), F32),
            pltpu.VMEM((15, POS, LANES), BF16),
            pltpu.VMEM((8, POS, 2 * LANES), F32),
            pltpu.VMEM((8, POS, LANES), BF16),
            pltpu.VMEM((6, POS, LANES), BF16),
            pltpu.VMEM((POS, LANES), BF16),
            dma((8,)),
            dma((4, 22)),
            dma((4, 22)),
            dma((4,)),
            dma((4,)),
            dma((2,)),
            dma((2,)),
            dma((19,)),
            dma((19,)),
        ],
        compiler_params=pltpu.CompilerParams(
            collective_id=0, has_side_effects=True, vmem_limit_bytes=48 * 1024 * 1024
        ),
        name="step",
    )(
        labels,
        *(
            pltpu.with_memory_space_constraint(a, pltpu.HBM)
            for a in (partner, images.transpose(1, 2, 0)[0], *weights)
        ),
    )
    gw3, gw1, gh = pl.pallas_call(
        grads_kernel,
        out_shape=(
            sds((LOC, 9, 1, GW), F32),
            sds((LOC, 1, C), F32),
            sds((K, LOC), F32),
        ),
        in_specs=[vmem] * 4,
        out_specs=[hbm] * 3,
        scratch_shapes=[
            pltpu.VMEM((3, 2 * POS, 3 * LANES), BF16),
            pltpu.VMEM((9, LOC, GW), F32),
            dma((11,)),
        ],
        compiler_params=pltpu.CompilerParams(vmem_limit_bytes=40 * 1024 * 1024),
        name="grads",
    )(*saved)
    return (gw3.transpose(2, 0, 1, 3), gw1.transpose(1, 0, 2), gh.T[None])


def solution(mesh):
    in_specs = (
        P("filt", "rep", None),
        P("rep"),
        P(),
        P("rep", "filt", None, None),
        P("rep", "filt", None),
        P("rep", "filt", None),
        P("rep", "filt", None, None),
        P("rep", "filt", None),
        P("rep", "filt", None),
    )
    out_specs = (P("rep", "filt", None, None), P("rep", "filt", None), P("rep", "filt", None))
    return jax.shard_map(
        per_device, mesh=mesh, in_specs=in_specs, out_specs=out_specs, check_vma=False
    )
```
